32 devices in a mesh: img: 8 (over z, y), ha: 4 (over x, core).
Axes of the slice: x: 2, y: 2, z: 4, core: 2. Of those that a mesh axis runs over, the one named last changes fastest.
Arguments:
- features: bfloat16 [32, 56, 56, 256], P('img', 'ha'), may hold values from -24 to 24
- reducer: bfloat16 [256, 64], replicated, may hold values from -0.375 to 0.375
- spatial: bfloat16 [3, 3, 64, 64], replicated, may hold values from -0.25 to 0.25
- expander: bfloat16 [64, 256], replicated, may hold values from -0.75 to 0.75
- gain_reduce: float32 [64], replicated, may hold values from 0.1 to 1.9
- bias_reduce: float32 [64], replicated, may hold values from -3 to 3
- gain_spatial: float32 [64], replicated, may hold values from 0.1 to 1.9
- bias_spatial: float32 [64], replicated, may hold values from -3 to 3
- gain_expand: float32 [256], replicated, may hold values from 0.1 to 1.9
- bias_expand: float32 [256], replicated, may hold values from -3 to 3
- upstream: bfloat16 [32, 56, 56, 256], P('img', 'ha'), may hold values from -24 to 24
- image_counts: int32 [8], P('img'), may hold values from 2 to 4, as said below
Outputs:
- activated: bfloat16 [32, 56, 56, 256], P('img', 'ha')
- feature_grad: bfloat16 [32, 56, 56, 256], P('img', 'ha')
- reducer_grad: float32 [256, 64], replicated
- spatial_grad: float32 [3, 3, 64, 64], replicated
- expander_grad: float32 [64, 256], replicated
- gradgain_reduce: float32 [64], replicated
- gradbias_reduce: float32 [64], replicated
- gradgain_spatial: float32 [64], replicated
- gradbias_spatial: float32 [64], replicated
- gradgain_expand: float32 [256], replicated
- gradbias_expand: float32 [256], replicated
The draws below stay inside these ranges and needn't reach their ends.
Inputs may be any that keep to these rules, and one draw needn't show every extreme that they name: `image_counts`: the largest count equals 4; slots past an index's count hold padding images.
All inputs are finite; a program needn't handle non-finite values.
Results may differ from the reference program's by a relative error of at most 0.0056.
Values may be sent and summed in bfloat16 or wider, within the bound.
No kernel may reach another device: no remote copies, remote signals or barrier semaphores. Data moves between devices by JAX's collectives and lax.ppermute only.
A program may use at most 64 MiB of HBM per device.

```python
import math
import jax
import jax.numpy as jnp
from jax import lax

C_IN = 256
C_MID = 64
HEIGHT = 56
WIDTH = 56
IMG_CAP = 4
IMAGES = 32


def shaped(key, noise, spread):
    key_image, key_chan, key_offset, key_ramp = jax.random.split(key, 4)
    images = noise.shape[0]
    height = noise.shape[1]
    channels = noise.shape[3]
    rising = 0.5 + jnp.arange(images, dtype=jnp.float32) / max(images - 1, 1)
    image_scale = jnp.exp(jax.random.uniform(key_image, (images, 1, 1, 1), jnp.float32, -1.0, 1.0) * math.log(spread))
    chan_scale = jnp.exp(jax.random.uniform(key_chan, (channels,), jnp.float32, -1.0, 1.0) * math.log(spread))
    offset = jnp.clip(jax.random.normal(key_offset, (channels,), jnp.float32), -3.0, 3.0)
    profile = (2.0 * jnp.arange(height, dtype=jnp.float32) + 1.0) / height - 1.0
    slope = jax.random.uniform(key_ramp, (channels,), jnp.float32, -2.0, 2.0)
    ramp = profile[None, :, None, None] * slope
    return noise * image_scale * chan_scale + offset * rising[:, None, None, None] + ramp


def draw_features(key, part):
    key = jax.random.fold_in(key, 11)
    key_noise, key_rest = jax.random.split(key)
    shape = (IMAGES, HEIGHT, WIDTH, C_IN)
    noise = jnp.clip(jax.random.normal(key_noise, shape, jnp.float32), -4.0, 4.0)
    spread = 2.0
    return shaped(key_rest, noise, spread).astype(jnp.bfloat16)


def draw_upstream(key, part):
    key = jax.random.fold_in(key, 13)
    key_noise, key_rest = jax.random.split(key)
    shape = (IMAGES, HEIGHT, WIDTH, C_IN)
    noise = jnp.clip(jax.random.normal(key_noise, shape, jnp.float32), -4.0, 4.0)
    spread = 2.0
    return shaped(key_rest, noise, spread).astype(jnp.bfloat16)


def draw_image_counts(key, part):
    key = jax.random.fold_in(key, 7)
    key_counts, key_pick = jax.random.split(key)
    owners = IMAGES // IMG_CAP
    counts = jax.random.randint(key_counts, (owners,), (IMG_CAP + 1) // 2, IMG_CAP + 1)
    picked = jax.random.randint(key_pick, (), 0, owners)
    return jnp.where(jnp.arange(owners) == picked, IMG_CAP, counts).astype(jnp.int32)


def gaussian(key, dims, width, reach, kind=jnp.bfloat16):
    return jnp.clip(width * jax.random.normal(key, dims, jnp.float32), -reach, reach).astype(kind)


def setup_inputs(seed: int = 0) -> dict:
    key_list = jax.random.split(jax.random.key(seed), 13)
    return {
        "features": draw_features(jax.random.fold_in(key_list[12], 71), 0),
        "reducer": gaussian(key_list[1], (C_IN, C_MID), C_IN ** -0.5, 0.375),
        "spatial": gaussian(key_list[2], (3, 3, C_MID, C_MID), (9 * C_MID) ** -0.5, 0.25),
        "expander": gaussian(key_list[3], (C_MID, C_IN), C_MID ** -0.5, 0.75),
        "gain_reduce": jnp.clip(1.0 + 0.18 * jax.random.normal(key_list[4], (C_MID,), jnp.float32), 0.1, 1.9),
        "bias_reduce": gaussian(key_list[5], (C_MID,), 0.5, 3.0, jnp.float32),
        "gain_spatial": jnp.clip(1.0 + 0.18 * jax.random.normal(key_list[6], (C_MID,), jnp.float32), 0.1, 1.9),
        "bias_spatial": gaussian(key_list[7], (C_MID,), 0.5, 3.0, jnp.float32),
        "gain_expand": jnp.clip(1.0 + 0.18 * jax.random.normal(key_list[8], (C_IN,), jnp.float32), 0.1, 1.9),
        "bias_expand": gaussian(key_list[9], (C_IN,), 0.5, 3.0, jnp.float32),
        "upstream": draw_upstream(jax.random.fold_in(key_list[12], 71), 0),
        "image_counts": draw_image_counts(jax.random.fold_in(key_list[12], 71), 0),
    }


EPSILON = 1e-05

@jax.custom_vjp
def low(v):
    return lax.optimization_barrier(v.astype(jnp.bfloat16)).astype(jnp.float32)

@jax.custom_vjp
def low_back(v):
    return v

def low_keep(v):
    return (low(v), None)

def low_pass(kept, grad):
    return (grad,)

def back_keep(v):
    return (v, None)

def back_low(kept, grad):
    return (low(grad),)
low.defvjp(low_keep, low_pass)
low_back.defvjp(back_keep, back_low)

def normalize(values, gain, bias, pixmask, total):
    average = lax.optimization_barrier(jnp.sum(values * pixmask, axis=(0, 1, 2))) / total
    centred = values - average
    variance = lax.optimization_barrier(jnp.sum(pixmask * centred * centred, axis=(0, 1, 2))) / total
    return centred * lax.rsqrt(variance + EPSILON) * gain + bias

def spatial_conv(activation, kernel):
    height, across = (activation.shape[1], activation.shape[2])
    padded = jnp.pad(activation, ((0, 0), (1, 1), (1, 1), (0, 0)))
    result = jnp.zeros(activation.shape[:3] + (kernel.shape[3],), jnp.float32)
    for vertical in range(3):
        for lateral in range(3):
            window = padded[:, vertical:vertical + height, lateral:lateral + across]
            result = result + jnp.einsum('irwc,cd->irwd', window, kernel[vertical, lateral], precision=lax.Precision.HIGHEST)
    return result

def forward(features, reducer, spatial, expander, gain_reduce, bias_reduce, gain_spatial, bias_spatial, gain_expand, bias_expand, pixmask, total):
    first = low_back(jnp.einsum('irwc,cd->irwd', features, reducer, precision=lax.Precision.HIGHEST))
    hidden_one = low(jax.nn.silu(normalize(first, gain_reduce, bias_reduce, pixmask, total)))
    second = low_back(jax.checkpoint(spatial_conv)(hidden_one, spatial))
    hidden_two = low(jax.nn.silu(normalize(second, gain_spatial, bias_spatial, pixmask, total)))
    third = low_back(jnp.einsum('irwc,cd->irwd', hidden_two, expander, precision=lax.Precision.HIGHEST))
    return jax.nn.silu(normalize(third, gain_expand, bias_expand, pixmask, total) + features)

def reference(features, reducer, spatial, expander, gain_reduce, bias_reduce, gain_spatial, bias_spatial, gain_expand, bias_expand, upstream, image_counts):
    slots = jnp.arange(IMAGES, dtype=jnp.int32)
    owners = jnp.repeat(image_counts, IMG_CAP)
    pixmask = (slots % IMG_CAP < owners).astype(jnp.float32)[:, None, None, None]
    total = jnp.sum(image_counts).astype(jnp.float32) * (HEIGHT * WIDTH)

    def wrapped(feat, red, spa, exp_w, g_one, b_one, g_two, b_two, g_three, b_three):
        return forward(feat, red, spa, exp_w, g_one, b_one, g_two, b_two, g_three, b_three, pixmask, total)
    inputs = (features.astype(jnp.float32), reducer.astype(jnp.float32), spatial.astype(jnp.float32), expander.astype(jnp.float32), gain_reduce, bias_reduce, gain_spatial, bias_spatial, gain_expand, bias_expand)
    output, pullback = jax.vjp(wrapped, *inputs)
    grads = pullback(upstream.astype(jnp.float32) * pixmask)
    return (output.astype(jnp.bfloat16), grads[0].astype(jnp.bfloat16), grads[1], grads[2], grads[3], grads[4], grads[5], grads[6], grads[7], grads[8], grads[9])
```

```python
import functools

import jax
import jax.numpy as jnp
from jax import lax
from jax.experimental import pallas as pl
from jax.experimental.pallas import tpu as pltpu
from jax.sharding import PartitionSpec as P

EPSILON = 1e-05
AXES = ("img", "ha")
F32 = jnp.float32
BF16 = jnp.bfloat16
VMEM_MIB = 16


def nn(left, right):
    return lax.dot_general(left, right, (((1,), (0,)), ((), ())), preferred_element_type=F32)


def nt(left, right):
    return lax.dot_general(left, right, (((1,), (1,)), ((), ())), preferred_element_type=F32)


def tn(left, right):
    return lax.dot_general(left, right, (((0,), (0,)), ((), ())), preferred_element_type=F32)


def pair_rows(sizes, ref):
    return jnp.concatenate([ref[half].reshape(sizes.pairs * sizes.own, 256) for half in range(2)], axis=1)


def tn_pair(left, right):
    product = tn(left, right)
    return product[0:64, 0:256] + product[64:128, 256:512]


def pieces(values):
    high = values.astype(BF16)
    rest = values - high.astype(F32)
    middle = rest.astype(BF16)
    low = (rest - middle.astype(F32)).astype(BF16)
    return high, middle, low


def exact(product, values, weights):
    high, middle, _ = pieces(values)
    return product(high, weights) + product(middle, weights)


def exact_rows(product, rows, weights):
    parts = [part for row in rows for part in pieces(row)]
    parts = parts + [jnp.zeros_like(parts[0])] * (-len(parts) % 8)
    result = product(jnp.concatenate([part.astype(F32) for part in parts], axis=0).astype(BF16), weights)
    return [total_of(result[3 * index : 3 * index + 3, :]) for index in range(len(rows))]


def folded(values):
    return jnp.sum(values.reshape(values.shape[0] // 8, 8, values.shape[1]), axis=0)


def total_of(values):
    return jnp.sum(values, axis=0, keepdims=True)


def swap(values):
    return pltpu.roll(values, 64, axis=1)


def low_lanes(shape):
    return lax.broadcasted_iota(jnp.int32, shape, 1) < 64


def low_both(row):
    return jnp.where(low_lanes(row.shape), row, swap(row))


def high_both(row):
    return jnp.where(low_lanes(row.shape), swap(row), row)


def twice(row):
    place = lax.broadcasted_iota(jnp.int32, (64, 128), 0)
    lane = lax.rem(lax.broadcasted_iota(jnp.int32, (64, 128), 1), 64)
    return exact_rows(nn, [row], (place == lane).astype(BF16))[0]


def swish(values):
    half = 0.5 * values
    turn = jnp.tanh(half)
    plus = 1.0 + turn
    value = half * plus
    return value, 0.5 * (plus + value * (1.0 - turn))


def fill_real(sizes, out_ref, count):
    count = jnp.zeros((1, 256), F32) + count.astype(F32)
    low = lax.rem(lax.broadcasted_iota(jnp.int32, (1, 256), 1), 128) < 64
    images = [(float(image) < count).astype(F32) for image in range(sizes.images)]
    rows = [jnp.where(low, images[g], images[g + sizes.pairs]) for g in range(sizes.pairs)] + images
    rows = rows + [jnp.zeros((1, 256), F32)] * (15 - len(rows)) + [count * sizes.pixels]
    out_ref[...] = jnp.concatenate(rows, axis=0)


def pair_mask(real_ref, g):
    return real_ref[g : g + 1, 0:128]


def count_mask(count_ref, g, pairs):
    count = count_ref[0]
    low = (g < count).astype(F32)
    high = (g + pairs < count).astype(F32)
    return jnp.where(low_lanes((1, 128)), low, high)


def image_mask(sizes, real_ref, image):
    return real_ref[sizes.pairs + image : sizes.pairs + image + 1, :]


def real_pixels(real_ref):
    return real_ref[15:16, 0:128]


def columns(row):
    return jnp.transpose(jnp.broadcast_to(row, (128, 128)))


def put_row(out_ref, slot, slots, count, row):
    out_ref[pl.ds(slot, count, stride=slots), :] = jnp.broadcast_to(row, (count, 128))


def put_rows(out_ref, slot, slots, count, matrix):
    rows = min(count, matrix.shape[0])
    for part in range(matrix.shape[0] // rows):
        out_ref[pl.ds(slot + part, rows, stride=slots), :] = matrix[part * rows : (part + 1) * rows, :]


def get_sum(got_ref, slot, slots, count):
    return total_of(got_ref[pl.ds(slot, count, stride=slots), :])


def get_rows(got_ref, slot, slots, count, height):
    rows = min(count, height)
    parts = [got_ref[pl.ds(slot + part, rows, stride=slots), :] for part in range(height // rows)]
    return parts[0] if len(parts) == 1 else jnp.concatenate(parts, axis=0)


def clear(sizes, out_ref, slots, used):
    if sizes.count > 64:
        out_ref[...] = jnp.zeros(out_ref.shape, F32)
    else:
        for slot in range(used, slots):
            put_row(out_ref, slot, slots, sizes.count, jnp.zeros((1, 128), F32))


class Sizes:
    def __init__(self, images, height, across, count):
        self.images, self.height, self.across, self.count = images, height, across, count
        self.pairs = images // 2
        self.own = height * across
        self.pixels = float(height * across)
        self.step = 2 * across
        self.chunks = height // 2
        self.ext = self.own + self.step
        self.sample = 32
        self.wide1 = (height + 4) * across
        self.wide2 = (height + 2) * across
        self.share = max(1, 64 // count)
        self.rows1 = 4
        self.cross_early = min(3, 2 * self.share)
        self.cross_late = 2 * self.share - self.cross_early
        self.rows2 = 4
        self.rows3 = 4 + self.share + self.cross_late
        self.rows4 = 5 + self.share
        self.rows5 = -(-(4 + 8 * self.share) // 4) * 4
        self.rows6 = -(-(1 + 8 * self.share) // 2) * 2


def block(start, size):
    return pl.ds(pl.multiple_of(start, size), size)


def diagonal(out_ref, weight):
    out_ref[...] = jnp.zeros(out_ref.shape, out_ref.dtype)
    out_ref[0:64, 0:256] = weight
    out_ref[64:128, 256:512] = weight


def edge_masks(sizes, low_ref, high_ref):
    column = lax.rem(lax.broadcasted_iota(jnp.int32, (sizes.step, 128), 0), sizes.across)
    low_ref[...] = (column > 0).astype(F32)
    high_ref[...] = (column < sizes.across - 1).astype(F32)


def place_taps(out_ref, vertical, lateral, tap):
    for half in range(2):
        row = vertical * 64 if vertical < 2 else 128 + 64 * half
        column = 128 + 64 * half if lateral == 1 else 64 * ((lateral // 2 + half) % 2)
        out_ref[half, row : row + 64, column : column + 64] = tap


def taps_apart(windows, swapped, weight_ref):
    low = low_lanes(windows[0].shape)
    pair_low = jnp.where(low, windows[0], swapped[1]).astype(BF16)
    pair_high = jnp.where(low, swapped[0], windows[1]).astype(BF16)
    last = windows[2].astype(BF16)
    one = nn(jnp.concatenate([pair_low, last], axis=1), weight_ref[0])
    two = nn(jnp.concatenate([pair_high, last], axis=1), weight_ref[1])
    products = (
        jnp.where(low, one[:, 0:128], two[:, 0:128]),
        one[:, 128:256] + two[:, 128:256],
        swap(jnp.where(low, two[:, 0:128], one[:, 0:128])),
    )
    return products, jnp.concatenate([pair_low, pair_high, last], axis=1)


def from_left(values, low):
    return pltpu.roll(values, 1, axis=0) * low


def from_right(values, high):
    return pltpu.roll(values, values.shape[0] - 1, axis=0) * high


class Stats:
    def __init__(self, real_ref):
        self.real_ref = real_ref
        self.number = real_pixels(real_ref)
        self.near = None
        self.part = [jnp.zeros((8, 128), F32)] * 2
        self.whole = [jnp.zeros((8, 128), F32)] * 2

    def add(self, value):
        if self.near is None:
            self.near = low_both(total_of(value) / float(value.shape[0]))
        apart = value - self.near
        self.part = [self.part[0] + folded(apart), self.part[1] + folded(apart * apart)]

    def close(self, g):
        mask = pair_mask(self.real_ref, g)
        self.whole = [whole + part * mask for whole, part in zip(self.whole, self.part)]
        self.part = [jnp.zeros((8, 128), F32)] * 2

    def row(self):
        total, square = [total_of(value) for value in self.whole]
        total, square = total + swap(total), square + swap(square)
        square = square - total * total / self.number
        return jnp.where(low_lanes((1, 128)), total + self.number * self.near, square)


def prepare_kernel(
    sizes, feat_hbm, up_hbm, redt_hbm, taps_hbm, expander_hbm, count_ref,
    weight_ref, conv_ref, back_ref, expand_ref, real_ref, near_ref, far_ref,
    redt_ref, taps_ref, expander_ref, edge_sem, small_sem,
):
    step, own = sizes.step, sizes.own
    small = [
        pltpu.make_async_copy(source, target, small_sem.at[index])
        for index, (source, target) in enumerate(
            ((redt_hbm, redt_ref), (expander_hbm, expander_ref), (taps_hbm, taps_ref))
        )
    ]
    edges = []
    odd = lax.rem(lax.axis_index("ha"), 2)
    to_last = pl.multiple_of((1 - odd) * (own - step), step)
    to_head = pl.multiple_of(odd * (own - step), step)
    for out, start in ((near_ref, to_last), (far_ref, to_head)):
        for place, source in enumerate((feat_hbm, up_hbm)):
            copy = pltpu.make_async_copy(
                source.at[:, :, pl.ds(start, step), :], out.at[place], edge_sem.at[len(edges)]
            )
            copy.start()
            edges.append(copy)
    for copy in small:
        copy.start()
    conv_ref[...] = jnp.zeros(conv_ref.shape, BF16)
    back_ref[...] = jnp.zeros(back_ref.shape, BF16)
    for copy in small:
        copy.wait()
    fill_real(sizes, real_ref, count_ref[0])
    diagonal(weight_ref, redt_ref[...])
    diagonal(expand_ref, expander_ref[...])
    for vertical in range(3):
        for lateral in range(3):
            tap = taps_ref[(vertical * 3 + lateral) * 64 : (vertical * 3 + lateral + 1) * 64, :]
            turned = jnp.transpose(tap)
            place_taps(conv_ref, vertical, lateral, tap)
            place_taps(back_ref, 2 - vertical, lateral, turned)
    for copy in edges:
        copy.wait()


def reduce_kernel(sizes, feat_ref, weight_ref, real_ref, first_ref, sums_ref, out_ref):
    pairs, step = sizes.pairs, sizes.step
    stats = Stats(real_ref)
    feats = jnp.zeros((8, 256), F32)
    for g in range(pairs):
        low_sum = high_sum = jnp.zeros((8, 256), F32)
        for c in range(sizes.chunks):
            low = feat_ref[0, g, c * step : (c + 1) * step, :]
            high = feat_ref[1, g, c * step : (c + 1) * step, :]
            value = nt(jnp.concatenate([low, high], axis=1), weight_ref[...])
            first_ref[g, c * step : (c + 1) * step, :] = value
            stats.add(value)
            low_sum = low_sum + folded(low.astype(F32))
            high_sum = high_sum + folded(high.astype(F32))
        stats.close(g)
        feats = feats + low_sum * image_mask(sizes, real_ref, g)
        feats = feats + high_sum * image_mask(sizes, real_ref, g + pairs)
    feats = total_of(feats)
    sums_ref[...] = feats
    slots, count = sizes.rows1, sizes.count
    put_row(out_ref, 0, slots, count, stats.row())
    put_row(out_ref, 1, slots, count, stats.number)
    put_row(out_ref, 2, slots, count, feats[:, 0:128])
    put_row(out_ref, 3, slots, count, feats[:, 128:256])


def merged(sizes, got_ref, slots, numbers):
    rows = got_ref[pl.ds(0, sizes.count, stride=slots), :]
    whole = total_of(numbers)
    low = low_lanes(rows.shape)
    both = jnp.where(low, rows, swap(rows))
    average = total_of(both) / whole
    apart = both / numbers - average
    squares = jnp.where(low, swap(rows), rows)
    variance = total_of(squares + numbers * apart * apart) / whole
    return average, lax.rsqrt(variance + EPSILON), whole


def conv_kernel(
    sizes, got_ref, feat_ref, first_ref, near_ref, far_ref, weight_ref, conv_ref, gain_ref, bias_ref, real_ref,
    window_ref, slope_ref, second_ref, norm_ref, cross_ref, out_ref, hidden_ref, turned_ref, low_ref, high_ref, normed_ref,
):
    pairs, step, own, across = sizes.pairs, sizes.step, sizes.own, sizes.across
    numbers = got_ref[pl.ds(1, sizes.count, stride=sizes.rows1), :]
    average, inverse, whole = merged(sizes, got_ref, sizes.rows1, numbers)
    norm_ref[...] = jnp.concatenate([average, inverse, whole, jnp.zeros((5, 128), F32)], axis=0)
    gain, bias = twice(gain_ref[...]), twice(bias_ref[...])
    place = lax.axis_index("ha")
    odd = lax.rem(place, 2)
    has_far = jnp.logical_and(place > 0, place < lax.axis_size("ha") - 1).astype(F32)
    near_start = pl.multiple_of((1 - odd) * (own + step), step)
    far_start = pl.multiple_of(odd * (own + step), step)
    edge_masks(sizes, low_ref, high_ref)
    for g in range(pairs):
        mask = pair_mask(real_ref, g)

        def activate(c, carry):
            normed = (first_ref[g, block(c * step, step), :] - average) * inverse
            value, slope = swish(normed * gain + bias)
            hidden_ref[g, block((c + 1) * step, step), :] = value
            turned_ref[g, block((c + 1) * step, step), :] = swap(value)
            slope_ref[g, block(c * step, step), :] = slope
            normed_ref[block(g * own + c * step, step), :] = (normed * mask).astype(BF16)
            return carry

        lax.fori_loop(0, sizes.chunks, activate, 0, unroll=True)
        for start, valid, rows_ref in ((near_start, 1.0, near_ref), (far_start, has_far, far_ref)):
            low, high = rows_ref[0, 0, g], rows_ref[0, 1, g]
            first = nt(jnp.concatenate([low, high], axis=1), weight_ref[...])
            value, _ = swish((first - average) * inverse * gain + bias)
            value = value * valid
            hidden_ref[g, pl.ds(start, step), :] = value
            turned_ref[g, pl.ds(start, step), :] = swap(value)
    cross = tn_pair(normed_ref[...], pair_rows(sizes, feat_ref))
    cross_ref[...] = cross

    def together(products):
        return from_left(products[0], low_ref[...]) + products[1] + from_right(products[2], high_ref[...])

    total = jnp.zeros((8, 128), F32)
    for g in range(pairs):
        part = jnp.zeros((8, 128), F32)
        starts = [slice((a + 1) * across, (a + 1) * across + own) for a in range(3)]
        products, window_ref[g] = taps_apart(
            *[[ref[g, start, :] for start in starts] for ref in (hidden_ref, turned_ref)], conv_ref
        )
        for c in range(sizes.chunks):
            rows = slice(c * step, (c + 1) * step)
            value = together([product[rows, :] for product in products])
            second_ref[g, rows, :] = value
            part = part + folded(value)
        total = total + part * pair_mask(real_ref, g)
        last = sizes.height + 1
        windows, swapped = [
            [
                jnp.concatenate(
                    [
                        ref[g, a * across : (a + 1) * across, :],
                        ref[g, (last + a) * across : (last + a + 1) * across, :],
                    ],
                    axis=0,
                )
                for a in range(3)
            ]
            for ref in (hidden_ref, turned_ref)
        ]
        products, _ = taps_apart(windows, swapped, conv_ref)
        second_ref[g, own : own + step, :] = together(products)
    total = total_of(total)
    total = total + swap(total)
    local = total / (real_pixels(real_ref))
    square = jnp.zeros((8, 128), F32)
    for g in range(pairs):
        part = jnp.zeros((8, 128), F32)
        for c in range(sizes.chunks):
            apart = second_ref[g, c * step : (c + 1) * step, :] - local
            part = part + folded(apart * apart)
        square = square + part * pair_mask(real_ref, g)
    square = total_of(square)
    square = square + swap(square)
    slots = sizes.rows2
    put_row(out_ref, 0, slots, sizes.count, jnp.where(low_lanes((1, 128)), total, square))
    put_cross(sizes, out_ref, 1, slots, cross, 0, sizes.cross_early)


def cross_rows(sizes):
    return [(half, part) for half in range(2) for part in range(sizes.share)]


def put_cross(sizes, out_ref, slot, slots, cross, start, stop):
    rows = min(sizes.count, 64)
    for index, (half, part) in enumerate(cross_rows(sizes)[start:stop]):
        matrix = cross[part * rows : (part + 1) * rows, half * 128 : (half + 1) * 128]
        out_ref[pl.ds(slot + index, rows, stride=slots), :] = matrix


def middle_kernel(
    sizes, got_ref, first_got_ref, second_ref, gain_ref, bias_ref, expand_ref, cross_ref, real_ref,
    hidden_ref, slope_ref, norm_ref, gram_ref, out_ref, left_ref, right_ref,
):
    pairs, step, own = sizes.pairs, sizes.step, sizes.own
    slots = sizes.rows3
    numbers = first_got_ref[pl.ds(1, sizes.count, stride=sizes.rows1), :]
    average, inverse, _ = merged(sizes, got_ref, sizes.rows2, numbers)
    gain, bias = twice(gain_ref[...]), twice(bias_ref[...])
    centre, tangent = swish(bias)
    sums = (jnp.zeros((8, 128), F32),) * 3
    for g in range(pairs):
        mask = pair_mask(real_ref, g)

        def activate(c, acc):
            rows = block(c * step, step)
            normed = (second_ref[g, rows, :] - average) * inverse
            value, slope = swish(normed * gain + bias)
            rounded = value.astype(BF16)
            hidden_ref[g, rows, :] = rounded
            slope_ref[g, rows, :] = slope
            apart = (rounded.astype(F32) - centre) * mask
            slope = slope * mask
            tilted = slope * normed
            rows = block(g * own + c * step, step)
            left_ref[rows, :] = apart.astype(BF16)
            right_ref[rows, 0:128] = apart.astype(BF16)
            right_ref[rows, 128:256] = (slope - tangent).astype(BF16)
            right_ref[rows, 256:384] = tilted.astype(BF16)
            return acc[0] + folded(apart), acc[1] + folded(slope), acc[2] + folded(tilted)

        sums = lax.fori_loop(0, sizes.chunks, activate, sums, unroll=True)
        value, slope = swish((second_ref[g, own : own + step, :] - average) * inverse * gain + bias)
        hidden_ref[g, own : own + step, :] = value.astype(BF16)
        slope_ref[g, own : own + step, :] = slope
    product = tn(left_ref[...], right_ref[...])
    apart, slope, tilted = [total_of(value) for value in sums]
    apart, slope, tilted = apart + swap(apart), slope + swap(slope), tilted + swap(tilted)
    low, high = product[0:64, :], product[64:128, :]
    gram = low[:, 0:128] + swap(high[:, 0:128])
    slopes = low[:, 128:256] + swap(high[:, 128:256])
    tilts = swap(low[:, 256:384]) + high[:, 256:384]
    wide = low_lanes((64, 128))
    slopes = slopes + columns(apart)[0:64, :] * tangent
    gram = jnp.where(wide, gram, 0.0)
    gram_ref[...] = gram
    weights = expand_ref[0:64, 0:256]
    quad = total_of(exact(nn, gram[:, 0:64], weights) * weights.astype(F32))
    norm_ref[...] = jnp.concatenate(
        [average, inverse, centre, apart, jnp.where(low_lanes((1, 128)), slope, tilted), jnp.zeros((3, 128), F32)],
        axis=0,
    )
    put_row(out_ref, 0, slots, sizes.count, quad[:, 0:128])
    put_row(out_ref, 1, slots, sizes.count, quad[:, 128:256])
    put_row(out_ref, 2, slots, sizes.count, apart)
    put_row(out_ref, 3, slots, sizes.count, jnp.where(low_lanes((1, 128)), slope, tilted))
    put_rows(out_ref, 4, slots, sizes.count, jnp.where(wide, slopes, tilts))
    put_cross(sizes, out_ref, 4 + sizes.share, slots, cross_ref[...], sizes.cross_early, 2 * sizes.share)


def output_kernel(
    sizes, got_ref, norm_one_ref, norm_ref, hidden_ref, slope_ref, second_ref, feat_ref, up_ref,
    near_ref, far_ref, gain_ref, bias_ref, expand_ref, real_ref,
    active_ref, gsum_ref, back_ref, last_ref, raw_ref, out_ref, scaled_ref,
):
    pairs, step, own, across = sizes.pairs, sizes.step, sizes.own, sizes.across
    odd = lax.rem(lax.axis_index("ha"), 2) == 1
    slots, count = sizes.rows3, sizes.count
    whole = norm_one_ref[2:3, :]
    centre = norm_ref[2:3, :]
    apart = get_sum(got_ref, 2, slots, count) / whole
    mean_hidden = centre + apart
    column = expand_ref[:, 0:256]
    shift, average = exact_rows(nn, [apart, mean_hidden], column)
    quad = jnp.concatenate([get_sum(got_ref, 0, slots, count), get_sum(got_ref, 1, slots, count)], axis=1)
    wide = jnp.concatenate([whole, whole], axis=1)
    inverse = lax.rsqrt(quad / wide - shift * shift + EPSILON)
    gain, bias = gain_ref[...], bias_ref[...]
    scale = gain * inverse
    offset = bias - average * scale
    average_two, inverse_two = norm_ref[0:1, :], norm_ref[1:2, :]

    def outward(third, feat):
        half_sum = 0.5 * (third * scale + offset + feat)
        turn = jnp.tanh(half_sum)
        plus = 1.0 + turn
        value = half_sum * plus
        return value, plus + value * (1.0 - turn)

    sample = slice(0, sizes.sample)
    _, slope = outward(nn(hidden_ref[0, sample, :], column), feat_ref[0, 0, sample, :].astype(F32))
    middle = 0.5 * total_of(up_ref[0, 0, sample, :].astype(F32) * slope) / float(sizes.sample)
    flat = scale * middle
    (flat_back,) = exact_rows(nt, [flat], expand_ref[:, 0:256] + expand_ref[:, 256:512])
    last_ref[...] = jnp.concatenate(
        [average, inverse, scale, jnp.concatenate([mean_hidden, apart], axis=1), middle, flat, jnp.zeros((2, 256), F32)],
        axis=0,
    )
    biases = jnp.zeros((8, 256), F32)
    for g in range(pairs):
        valids = [image_mask(sizes, real_ref, g + half * pairs) for half in range(2)]
        middles = [middle * valid for valid in valids]

        def body(c, biases):
            hidden = hidden_ref[g, block(c * step, step), :]
            for half in range(2):
                image = g + half * pairs
                third = nn(hidden, expand_ref[:, half * 256 : (half + 1) * 256])
                for start in range(0, step, 16):
                    here = pl.ds(pl.multiple_of(c * step + start, 16), 16)
                    place = pl.ds(pl.multiple_of(image * own + c * step + start, 16), 16)
                    value, slope = outward(third[start : start + 16, :], feat_ref[half, g, here, :].astype(F32))
                    active_ref[place, :] = value.astype(BF16)
                    grad = up_ref[half, g, here, :].astype(F32) * (0.5 * valids[half]) * slope
                    gsum_ref[place, :] = grad
                    grad = grad - middles[half]
                    biases = biases + folded(grad)
                    there = pl.ds(pl.multiple_of(g * own + c * step + start, 16), 16)
                    scaled_ref[there, half * 256 : (half + 1) * 256] = (grad * scale).astype(BF16)
            return biases

        biases = lax.fori_loop(0, sizes.chunks, body, biases, unroll=True)
        hidden = hidden_ref[g, own : own + step, :]
        edge = pairs * own + g * step
        for half in range(2):
            image = g + half * pairs
            both = []
            for which in range(2):
                near = near_ref[which, half, g].astype(F32)
                far = far_ref[which, half, g].astype(F32)
                upper = jnp.where(odd, near[across:, :], far[across:, :])
                lower = jnp.where(odd, far[0:across, :], near[0:across, :])
                both.append(jnp.concatenate([upper, lower], axis=0))
            _, slope = outward(nn(hidden, expand_ref[:, half * 256 : (half + 1) * 256]), both[0])
            grad = both[1] * (0.5 * valids[half]) * slope
            scaled = ((grad - middles[half]) * scale).astype(BF16)
            scaled_ref[edge : edge + step, half * 256 : (half + 1) * 256] = scaled
    tops = tilts = jnp.zeros((8, 128), F32)
    backs = nt(scaled_ref[...], expand_ref[...])
    for g in range(pairs):
        back = backs[g * own : (g + 1) * own, :]
        back_ref[g, 0:own, :] = back
        top = slope_ref[g, 0:own, :] * back
        normed_two = (second_ref[g, 0:own, :] - average_two) * inverse_two
        tops, tilts = tops + folded(top), tilts + folded(top * normed_two)
        edge = pairs * own + g * step
        back_ref[g, own : own + step, :] = backs[edge : edge + step, :]
    raw = tn_pair(hidden_ref[:, 0:own, :].reshape(pairs * own, 128), scaled_ref[0 : pairs * own, :])
    raw_ref[...] = raw
    biases, tops, tilts = [total_of(value) for value in (biases, tops, tilts)]
    gains = total_of(raw * expand_ref[0:64, 0:256].astype(F32)) / scale - average * biases
    number = real_pixels(real_ref)
    (third_sum,) = exact_rows(nn, [norm_ref[3:4, :] - number * apart], column)
    gains = inverse * (gains + middle * third_sum)
    biases = biases + number[:, 0:1] * middle
    tops, tilts = tops + swap(tops), tilts + swap(tilts)
    tops = jnp.where(low_lanes((1, 128)), tops, tilts) + norm_ref[4:5, :] * flat_back
    sent = sizes.rows4
    put_row(out_ref, 0, sent, count, biases[:, 0:128])
    put_row(out_ref, 1, sent, count, biases[:, 128:256])
    put_row(out_ref, 2, sent, count, gains[:, 0:128])
    put_row(out_ref, 3, sent, count, gains[:, 128:256])
    put_row(out_ref, 4, sent, count, tops)
    for part in range(sizes.share):
        put_row(out_ref, 5 + part, sent, count, get_sum(got_ref, 4 + part, slots, count))


def backward_kernel(
    sizes, got_ref, third_got_ref, norm_one_ref, norm_ref, last_ref, gram_ref, window_ref, slope_one_ref,
    first_ref, hidden_ref, slope_ref, second_ref, back_ref, raw_ref, feat_ref, sums_ref, gain_two_ref, expand_ref,
    conv_back_ref, active_ref, count_ref,
    gain3_out_ref, bias3_out_ref, gain2_out_ref, bias2_out_ref, grad_one_ref, active_hbm, out_ref,
    grad_ref, turned_ref, low_ref, high_ref, right_ref, send_ref, sem_ref,
):
    pairs, step, own, across = sizes.pairs, sizes.step, sizes.own, sizes.across
    leave = pltpu.make_async_copy(active_ref, active_hbm, sem_ref)
    leave.start()
    share, count = sizes.share, sizes.count
    third_slots, slots = sizes.rows3, sizes.rows4
    whole = norm_one_ref[2:3, :]
    whole_wide = jnp.concatenate([whole, whole], axis=1)
    bias3 = jnp.concatenate([get_sum(got_ref, 0, slots, count), get_sum(got_ref, 1, slots, count)], axis=1)
    gain3 = jnp.concatenate([get_sum(got_ref, 2, slots, count), get_sum(got_ref, 3, slots, count)], axis=1)
    bias3_out_ref[...] = bias3
    gain3_out_ref[...] = gain3
    inverse3, scale3 = last_ref[1:2, :], last_ref[2:3, :]
    mean_hidden, apart = last_ref[3:4, 0:128], last_ref[3:4, 128:256]
    flat = scale3 * bias3 / whole_wide
    tilt = scale3 * inverse3 * gain3 / whole_wide
    diag = expand_ref[...]
    stacked = diag[:, 0:256] + diag[:, 256:512]
    flat_here = flat - last_ref[5:6, :]
    flat_back, flat_here_back = exact_rows(nt, [flat, flat_here], stacked)
    tilt_wide = jnp.concatenate([tilt, tilt], axis=1)
    mixing = exact(nt, diag.astype(F32) * tilt_wide, diag)
    mix_high, mix_low, _ = pieces(mixing)
    mix_both = jnp.concatenate([mix_high, mix_low], axis=1)
    mean_mix, apart_mix = [
        row[:, 0:128] + row[:, 128:256] for row in exact_rows(nn, [mean_hidden, apart], mix_both)
    ]
    row_low = low_lanes((1, 128))
    slopes = get_sum(third_got_ref, 3, third_slots, count)
    cross = get_rows(got_ref, 5, slots, count, 64)
    mixed = total_of((mixing[0:64, :] + mixing[64:128, :]) * cross)
    sums = get_sum(got_ref, 4, slots, count) - (slopes * (flat_back - apart_mix) + mixed)
    bias2, gain2 = low_both(sums), high_both(sums)
    bias2_out_ref[...] = bias2[:, 0:64]
    gain2_out_ref[...] = gain2[:, 0:64]
    average_two, inverse_two, centre = norm_ref[0:1, :], norm_ref[1:2, :], norm_ref[2:3, :]
    scale2 = twice(gain_two_ref[...]) * inverse_two
    base = flat_here_back - mean_mix
    place = lax.axis_index("ha")
    has_above = (place > 0).astype(F32)
    has_below = (place < lax.axis_size("ha") - 1).astype(F32)
    edge_masks(sizes, low_ref, high_ref)
    average_one, inverse_one = norm_one_ref[0:1, :], norm_one_ref[1:2, :]

    local = norm_ref[3:4, :]
    number = count_ref[0].astype(F32) * sizes.pixels
    col_hidden = columns(local + number * centre)[0:64, :]
    col_local = columns(local)[0:64, :]
    col_centre = columns(centre)[0:64, :]
    around = gram_ref[...] - col_local * apart + col_centre * (local - number * apart)
    around = exact(nn, around[:, 0:64], diag[0:64, 0:256])
    col_wide = jnp.concatenate([col_hidden, col_hidden], axis=1)
    expander = raw_ref[...] - col_wide * flat_here - around * tilt

    sums = (jnp.zeros((8, 128), F32), jnp.zeros((8, 128), F32))
    for g in range(pairs):
        mask = count_mask(count_ref, g, pairs)

        def inward(rows):
            hidden = hidden_ref[g, rows, :]
            mixed = nn(hidden, mix_both)
            mixed = mixed[:, 0:128] + mixed[:, 128:256]
            grad = slope_ref[g, rows, :] * (back_ref[g, rows, :] - mask * (base + mixed))
            normed = (second_ref[g, rows, :] - average_two) * inverse_two
            return scale2 * (grad - mask * ((bias2 + normed * gain2) / whole))

        def store(c, carry):
            rows = block(c * step, step)
            grad = inward(rows)
            here = pl.ds(pl.multiple_of(c * step + across, 8), step)
            grad_ref[here, :] = grad
            turned_ref[here, :] = swap(grad)
            rows = block(g * own + c * step, step)
            right_ref[rows, 0:128] = from_right(grad, high_ref[...]).astype(BF16)
            right_ref[rows, 128:256] = grad.astype(BF16)
            right_ref[rows, 256:384] = from_left(grad, low_ref[...]).astype(BF16)
            return carry

        lax.fori_loop(0, sizes.chunks, store, 0, unroll=True)
        edge = inward(pl.ds(own, step))
        for start, value in ((0, edge[0:across, :] * has_above), (own + across, edge[across:, :] * has_below)):
            grad_ref[start : start + across, :] = value
            turned_ref[start : start + across, :] = swap(value)

        starts = [slice(a * across, a * across + own) for a in range(3)]
        products, _ = taps_apart(
            [grad_ref[start, :] for start in starts], [turned_ref[start, :] for start in starts[0:2]], conv_back_ref
        )
        for c in range(sizes.chunks):
            rows = slice(c * step, (c + 1) * step)
            value = from_right(products[0][rows, :], high_ref[...]) + products[1][rows, :]
            value = value + from_left(products[2][rows, :], low_ref[...])
            grad = value * slope_one_ref[g, rows, :]
            grad_one_ref[g, rows, :] = grad
            normed = (first_ref[g, rows, :] - average_one) * inverse_one
            sums = sums[0] + folded(grad), sums[1] + folded(grad * normed)
    product = tn(window_ref[...].reshape(pairs * own, 384), right_ref[...])
    grad = grad_one_ref[...].reshape(pairs * own, 128).astype(BF16)
    reducer = tn_pair(grad, pair_rows(sizes, feat_ref))
    tops, tilts = total_of(sums[0]), total_of(sums[1])
    tops, tilts = tops + swap(tops), tilts + swap(tilts)
    sent = sizes.rows5
    clear(sizes, send_ref, sent, 4 + 8 * share)
    for slot, row in enumerate(pieces(jnp.where(row_low, tops, tilts))):
        put_row(send_ref, slot, sent, count, row.astype(F32))
    reducer = reducer - jnp.concatenate([columns(tops / number)[0:64, :]] * 2, axis=1) * sums_ref[...]
    slot = 3
    for matrix in (reducer, expander):
        for half in range(2):
            put_rows(send_ref, slot, sent, count, matrix[:, half * 128 : (half + 1) * 128])
            slot += share
    wide = low_lanes((64, 128))

    def tap(index):
        row, column = index // 3, (index % 3) * 128
        rows = (64 * row, 128 + 64 * row) if row < 2 else (256, 320)
        return [product[start : start + 64, column : column + 128] for start in rows]

    for pair in range(4):
        low, high = tap(2 * pair)
        even = low + swap(high)
        low, high = tap(2 * pair + 1)
        odd = swap(low) + high
        put_rows(send_ref, slot, sent, count, jnp.where(wide, even, odd))
        slot += share
    low, high = tap(8)
    even = low + swap(high)
    put_rows(send_ref, slot, sent, count, jnp.where(low_lanes((32, 128)), even[0:32, :], swap(even[32:64, :])))
    out_ref[...] = send_ref[...].astype(BF16)
    leave.wait()


def shares_kernel(
    sizes, got_ref, first_got_ref, second_got_ref, third_got_ref, norm_one_ref, gain_ref, grad_ref, first_ref,
    gsum_ref, weight_ref, real_ref,
    gain_out_ref, bias_out_ref, feature_ref, out_ref,
    send_ref, wide_ref,
):
    share, count, pairs, step, own = sizes.share, sizes.count, sizes.pairs, sizes.step, sizes.own
    slots = sizes.rows5
    wide_ref[...] = got_ref[...].astype(F32)
    total = jnp.sum(wide_ref[...].reshape(count // 2, 2 * slots, 128), axis=0)
    total = total[0:slots, :] + total[slots:, :]
    whole = norm_one_ref[2:3, :]
    average, inverse = norm_one_ref[0:1, :], norm_one_ref[1:2, :]
    sums = total[0:1, :] + (total[1:2, :] + total[2:3, :])
    bias, gain = low_both(sums), high_both(sums)
    bias_out_ref[...] = bias[:, 0:64]
    gain_out_ref[...] = gain[:, 0:64]
    scale = twice(gain_ref[...]) * inverse
    bias, gain = bias / whole, gain / whole
    for g in range(pairs):
        mask = pair_mask(real_ref, g)

        def body(c, carry):
            rows = block(c * step, step)
            normed = (first_ref[g, rows, :] - average) * inverse
            grad = (scale * (grad_ref[g, rows, :] - mask * (bias + normed * gain))).astype(BF16)
            for half in range(2):
                place = block((g + half * pairs) * own + c * step, step)
                value = nn(grad, weight_ref[:, half * 256 : (half + 1) * 256])
                feature_ref[half, g, rows, :] = (value + gsum_ref[place, :]).astype(BF16)
            return carry

        lax.fori_loop(0, sizes.chunks, body, 0, unroll=True)
    me = lax.axis_index("img") * lax.axis_size("ha") + lax.axis_index("ha")
    lane = lax.broadcasted_iota(jnp.int32, (1, 128), 1)
    sent = sizes.rows6
    local = wide_ref[pl.ds(0, count, stride=slots), :] + (
        wide_ref[pl.ds(1, count, stride=slots), :] + wide_ref[pl.ds(2, count, stride=slots), :]
    )
    local = jnp.where(low_lanes(local.shape), local, swap(local))
    local = local / first_got_ref[pl.ds(1, count, stride=sizes.rows1), :] - bias
    clear(sizes, send_ref, sent, 1 + 8 * share)
    rows = jnp.concatenate([local, scale, gain, jnp.zeros((6, 128), F32)], axis=0)
    picked = [
        jnp.sum(jnp.where(lane == me + part * count, rows, 0.0), axis=1, keepdims=True) for part in range(share)
    ]
    for index, (half, part) in enumerate(cross_rows(sizes)):
        place = 3 + half * share + part
        raw = total[place : place + 1, :]
        if index < sizes.cross_early:
            cross = get_sum(second_got_ref, 1 + index, sizes.rows2, count)
        else:
            cross = get_sum(third_got_ref, 4 + share + index - sizes.cross_early, sizes.rows3, count)
        features = first_got_ref[pl.ds(2 + half, count, stride=sizes.rows1), :]
        local, factor, tilt = [picked[part][a:b, :] for a, b in ((0, count), (count, count + 1), (count + 1, count + 2))]
        value = factor * (raw + total_of(local * features) - tilt * cross)
        put_row(send_ref, half * share + part, sent, count, value)
    for slot in range(2 * share, 8 * share + 1):
        place = 3 + slot
        put_row(send_ref, slot, sent, count, total[place : place + 1, :])
    out_ref[...] = send_ref[...].astype(BF16)


def weights_kernel(sizes, got_ref, redt_out_ref, expander_out_ref, spatial_out_ref, wide_ref):
    share, count = sizes.share, sizes.count
    slots = sizes.rows6
    wide_ref[...] = got_ref[...].astype(F32)
    for out_ref, slot in ((redt_out_ref, 0), (expander_out_ref, 2 * share)):
        for half in range(2):
            out_ref[:, half * 128 : (half + 1) * 128] = get_rows(wide_ref, slot + half * share, slots, count, 64)
    for index in range(8):
        value = get_rows(wide_ref, (4 + index // 2) * share, slots, count, 64)
        if index % 2:
            value = swap(value)
        spatial_out_ref[index * 64 : (index + 1) * 64, :] = value[:, 0:64]
    value = get_rows(wide_ref, 8 * share, slots, count, 32)
    spatial_out_ref[512:544, :] = value[:, 0:64]
    spatial_out_ref[544:576, :] = swap(value)[:, 0:64]


def exchange(rows, count):
    pack = 2 if rows.dtype == BF16 else 1
    parted = rows.reshape(count, rows.shape[0] // (count * pack), pack, 128)
    return lax.all_to_all(parted, AXES, 0, 0).reshape(rows.shape)


def on_device(
    features,
    reducer,
    spatial,
    expander,
    gain_reduce,
    bias_reduce,
    gain_spatial,
    bias_spatial,
    gain_expand,
    bias_expand,
    upstream,
    image_counts,
):
    images, height, across, wide = features.shape
    count = lax.axis_size("img") * lax.axis_size("ha")
    sizes = Sizes(images, height, across, count)
    pairs, own, step = sizes.pairs, sizes.own, sizes.step
    flat = (images * own, wide)
    deep = (2, pairs, own, wide)
    feat_hbm, up_hbm = features.reshape(deep), upstream.reshape(deep)
    gain1, bias1, gain2, bias2, gain3, bias3 = [
        value.reshape(1, value.shape[0])
        for value in (gain_reduce, bias_reduce, gain_spatial, bias_spatial, gain_expand, bias_expand)
    ]
    outside = pl.BlockSpec(memory_space=pltpu.HBM)
    inside = pl.BlockSpec(memory_space=pltpu.VMEM)

    def shape(*dims, dtype=F32):
        return jax.ShapeDtypeStruct(dims, dtype)

    def call(kernel, outs, args, scratch=(), away=(), far=()):
        specs = []
        for arg in args:
            if arg is image_counts:
                specs.append(pl.BlockSpec(memory_space=pltpu.SMEM))
            else:
                specs.append(outside if any(arg is other for other in far) else inside)
        return pl.pallas_call(
            functools.partial(kernel, sizes),
            out_shape=outs,
            in_specs=specs,
            out_specs=tuple(outside if index in away else inside for index in range(len(outs))),
            scratch_shapes=list(scratch),
            compiler_params=pltpu.CompilerParams(vmem_limit_bytes=VMEM_MIB << 20),
        )(*args)

    ha = lax.axis_size("ha")
    near = [(i, i ^ 1) for i in range(ha)]
    far = [(i, i + 1) for i in range(1, ha - 1, 2)]
    far = far + [(target, source) for source, target in far]
    masks = [pltpu.VMEM((step, 128), F32), pltpu.VMEM((step, 128), F32)]

    given = tuple(
        pltpu.with_memory_space_constraint(value, pltpu.HBM)
        for value in (feat_hbm, up_hbm, reducer.T, spatial.reshape(9 * 64, 64), expander)
    )
    weight, conv, conv_back, expand, real, near_rows, far_rows = call(
        prepare_kernel,
        (
            shape(128, 512, dtype=BF16),
            shape(2, 256, 256, dtype=BF16),
            shape(2, 256, 256, dtype=BF16),
            shape(128, 512, dtype=BF16),
            shape(16, 256),
            shape(2, 2, pairs, step, wide, dtype=BF16),
            shape(2, 2, pairs, step, wide, dtype=BF16),
        ),
        (*given, image_counts),
        [
            pltpu.VMEM((64, 256), BF16),
            pltpu.VMEM((9 * 64, 64), BF16),
            pltpu.VMEM((64, 256), BF16),
            pltpu.SemaphoreType.DMA((4,)),
            pltpu.SemaphoreType.DMA((3,)),
        ],
        far=given,
    )
    near_rows = lax.ppermute(near_rows, "ha", near)
    far_rows = lax.ppermute(far_rows, "ha", far)
    feat = feat_hbm
    first, sums, rows = call(
        reduce_kernel,
        (shape(pairs, own, 128), shape(1, 256), shape(count * sizes.rows1, 128)),
        (feat, weight, real),
    )
    got1 = exchange(rows, count)
    windows, slope_one, second, norm_one, cross, rows = call(
        conv_kernel,
        (
            shape(pairs, own, 384, dtype=BF16),
            shape(pairs, own, 128),
            shape(pairs, sizes.ext, 128),
            shape(8, 128),
            shape(64, 256),
            shape(count * sizes.rows2, 128),
        ),
        (got1, feat, first, near_rows, far_rows, weight, conv, gain1, bias1, real),
        [pltpu.VMEM((pairs, sizes.wide1, 128), F32)] * 2 + [*masks, pltpu.VMEM((pairs * own, 128), BF16)],
    )
    got2 = exchange(rows, count)
    hidden_two, slope_two, norm_two, gram, rows = call(
        middle_kernel,
        (
            shape(pairs, sizes.ext, 128, dtype=BF16),
            shape(pairs, sizes.ext, 128),
            shape(8, 128),
            shape(64, 128),
            shape(count * sizes.rows3, 128),
        ),
        (got2, got1, second, gain2, bias2, expand, cross, real),
        [pltpu.VMEM((pairs * own, 128), BF16), pltpu.VMEM((pairs * own, 384), BF16)],
    )
    got3 = exchange(rows, count)
    active, grad_sum, back, norm_three, raw, rows = call(
        output_kernel,
        (
            shape(*flat, dtype=BF16),
            shape(*flat),
            shape(pairs, sizes.ext, 128),
            shape(8, 256),
            shape(64, 256),
            shape(count * sizes.rows4, 128),
        ),
        (
            got3, norm_one, norm_two, hidden_two, slope_two, second, feat, up_hbm, near_rows, far_rows,
            gain3, bias3, expand, real,
        ),
        [pltpu.VMEM((pairs * sizes.ext, 2 * wide), BF16)],
    )
    got4 = exchange(rows, count)
    gradgain3, gradbias3, gradgain2, gradbias2, grad_one, activated, rows = call(
        backward_kernel,
        (
            shape(1, 256),
            shape(1, 256),
            shape(1, 64),
            shape(1, 64),
            shape(pairs, own, 128),
            shape(*flat, dtype=BF16),
            shape(count * sizes.rows5, 128, dtype=BF16),
        ),
        (
            got4, got3, norm_one, norm_two, norm_three, gram, windows, slope_one, first, hidden_two,
            slope_two, second, back, raw, feat, sums, gain2, expand, conv_back, active, image_counts,
        ),
        [pltpu.VMEM((sizes.wide2, 128), F32)] * 2
        + masks
        + [
            pltpu.VMEM((pairs * own, 384), BF16),
            pltpu.VMEM((count * sizes.rows5, 128), F32),
            pltpu.SemaphoreType.DMA,
        ],
        away=(5,),
    )
    got5 = exchange(rows, count)
    gradgain1, gradbias1, feature_grad, rows = call(
        shares_kernel,
        (
            shape(1, 64),
            shape(1, 64),
            pltpu.VMEM(deep, BF16),
            shape(count * sizes.rows6, 128, dtype=BF16),
        ),
        (got5, got1, got2, got3, norm_one, gain1, grad_one, first, grad_sum, weight, real),
        [pltpu.VMEM((count * sizes.rows6, 128), F32), pltpu.VMEM((count * sizes.rows5, 128), F32)],
    )
    got6 = exchange(rows, count)
    redt_grad, expander_grad, spatial_grad = call(
        weights_kernel,
        (shape(64, 256), shape(64, 256), shape(9 * 64, 64)),
        (got6,),
        [pltpu.VMEM((count * sizes.rows6, 128), F32)],
    )
    return (
        activated.reshape(features.shape),
        feature_grad.reshape(features.shape),
        redt_grad.T,
        spatial_grad.reshape(spatial.shape),
        expander_grad,
        gradgain1.reshape(64),
        gradbias1.reshape(64),
        gradgain2.reshape(64),
        gradbias2.reshape(64),
        gradgain3.reshape(256),
        gradbias3.reshape(256),
    )


def solution(mesh):
    whole = P("img", "ha", None, None)
    in_specs = (whole,) + (P(),) * 9 + (whole, P("img"))
    out_specs = (whole, whole) + (P(),) * 9
    return jax.shard_map(
        on_device, mesh=mesh, in_specs=in_specs, out_specs=out_specs, check_vma=False
    )
```

```python
import functools

import jax
import jax.numpy as jnp
from jax import lax
from jax.experimental import pallas as pl
from jax.experimental.pallas import tpu as pltpu
from jax.sharding import PartitionSpec as P

EPSILON = 1e-05
AXES = ("img", "ha")
F32 = jnp.float32
BF16 = jnp.bfloat16
VMEM_MIB = 16


def nn(left, right):
    return lax.dot_general(left, right, (((1,), (0,)), ((), ())), preferred_element_type=F32)


def nt(left, right):
    return lax.dot_general(left, right, (((1,), (1,)), ((), ())), preferred_element_type=F32)


def tn(left, right):
    return lax.dot_general(left, right, (((0,), (0,)), ((), ())), preferred_element_type=F32)


def pair_rows(sizes, ref):
    return jnp.concatenate([ref[half].reshape(sizes.pairs * sizes.own, 256) for half in range(2)], axis=1)


def tn_pair(left, right):
    product = tn(left, right)
    return product[0:64, 0:256] + product[64:128, 256:512]


def pieces(values):
    high = values.astype(BF16)
    rest = values - high.astype(F32)
    middle = rest.astype(BF16)
    low = (rest - middle.astype(F32)).astype(BF16)
    return high, middle, low


def exact(product, values, weights):
    high, middle, _ = pieces(values)
    return product(high, weights) + product(middle, weights)


def exact_rows(product, rows, weights):
    parts = [part for row in rows for part in pieces(row)]
    parts = parts + [jnp.zeros_like(parts[0])] * (-len(parts) % 8)
    result = product(jnp.concatenate([part.astype(F32) for part in parts], axis=0).astype(BF16), weights)
    return [total_of(result[3 * index : 3 * index + 3, :]) for index in range(len(rows))]


def folded(values):
    return jnp.sum(values.reshape(values.shape[0] // 8, 8, values.shape[1]), axis=0)


def total_of(values):
    return jnp.sum(values, axis=0, keepdims=True)


def swap(values):
    return pltpu.roll(values, 64, axis=1)


def low_lanes(shape):
    return lax.broadcasted_iota(jnp.int32, shape, 1) < 64


def low_both(row):
    return jnp.where(low_lanes(row.shape), row, swap(row))


def high_both(row):
    return jnp.where(low_lanes(row.shape), swap(row), row)


def twice(row):
    place = lax.broadcasted_iota(jnp.int32, (64, 128), 0)
    lane = lax.rem(lax.broadcasted_iota(jnp.int32, (64, 128), 1), 64)
    return exact_rows(nn, [row], (place == lane).astype(BF16))[0]


def swish(values):
    half = 0.5 * values
    turn = jnp.tanh(half)
    plus = 1.0 + turn
    value = half * plus
    return value, 0.5 * (plus + value * (1.0 - turn))


def fill_real(sizes, out_ref, count):
    count = jnp.zeros((1, 256), F32) + count.astype(F32)
    low = lax.rem(lax.broadcasted_iota(jnp.int32, (1, 256), 1), 128) < 64
    images = [(float(image) < count).astype(F32) for image in range(sizes.images)]
    rows = [jnp.where(low, images[g], images[g + sizes.pairs]) for g in range(sizes.pairs)] + images
    rows = rows + [jnp.zeros((1, 256), F32)] * (15 - len(rows)) + [count * sizes.pixels]
    out_ref[...] = jnp.concatenate(rows, axis=0)


def pair_mask(real_ref, g):
    return real_ref[g : g + 1, 0:128]


def count_mask(count_ref, g, pairs):
    count = count_ref[0]
    low = (g < count).astype(F32)
    high = (g + pairs < count).astype(F32)
    return jnp.where(low_lanes((1, 128)), low, high)


def image_mask(sizes, real_ref, image):
    return real_ref[sizes.pairs + image : sizes.pairs + image + 1, :]


def real_pixels(real_ref):
    return real_ref[15:16, 0:128]


def columns(row):
    return jnp.transpose(jnp.broadcast_to(row, (128, 128)))


def put_row(out_ref, slot, slots, count, row):
    out_ref[pl.ds(slot, count, stride=slots), :] = jnp.broadcast_to(row, (count, 128))


def put_rows(out_ref, slot, slots, count, matrix):
    rows = min(count, matrix.shape[0])
    for part in range(matrix.shape[0] // rows):
        out_ref[pl.ds(slot + part, rows, stride=slots), :] = matrix[part * rows : (part + 1) * rows, :]


def get_sum(got_ref, slot, slots, count):
    return total_of(got_ref[pl.ds(slot, count, stride=slots), :])


def get_rows(got_ref, slot, slots, count, height):
    rows = min(count, height)
    parts = [got_ref[pl.ds(slot + part, rows, stride=slots), :] for part in range(height // rows)]
    return parts[0] if len(parts) == 1 else jnp.concatenate(parts, axis=0)


def clear(sizes, out_ref, slots, used):
    if sizes.count > 64:
        out_ref[...] = jnp.zeros(out_ref.shape, F32)
    else:
        for slot in range(used, slots):
            put_row(out_ref, slot, slots, sizes.count, jnp.zeros((1, 128), F32))


class Sizes:
    def __init__(self, images, height, across, count):
        self.images, self.height, self.across, self.count = images, height, across, count
        self.pairs = images // 2
        self.own = height * across
        self.pixels = float(height * across)
        self.step = 2 * across
        self.chunks = height // 2
        self.ext = self.own + self.step
        self.sample = 32
        self.wide1 = (height + 4) * across
        self.wide2 = (height + 2) * across
        self.share = max(1, 64 // count)
        self.rows1 = 4
        self.cross_early = min(3, 2 * self.share)
        self.cross_late = 2 * self.share - self.cross_early
        self.rows2 = 4
        self.rows3 = 4 + self.share + self.cross_late
        self.rows4 = 5 + self.share
        self.rows5 = -(-(4 + 8 * self.share) // 4) * 4
        self.rows6 = -(-(1 + 8 * self.share) // 2) * 2


def block(start, size):
    return pl.ds(pl.multiple_of(start, size), size)


def diagonal(out_ref, weight):
    out_ref[...] = jnp.zeros(out_ref.shape, out_ref.dtype)
    out_ref[0:64, 0:256] = weight
    out_ref[64:128, 256:512] = weight


def edge_masks(sizes, low_ref, high_ref):
    column = lax.rem(lax.broadcasted_iota(jnp.int32, (sizes.step, 128), 0), sizes.across)
    low_ref[...] = (column > 0).astype(F32)
    high_ref[...] = (column < sizes.across - 1).astype(F32)


def all_taps(out_ref, taps_ref, back):
    out_ref[...] = jnp.zeros(out_ref.shape, BF16)
    for vertical in range(3):
        for lateral in range(3):
            tap = taps_ref[(vertical * 3 + lateral) * 64 : (vertical * 3 + lateral + 1) * 64, :]
            if back:
                place_taps(out_ref, 2 - vertical, lateral, jnp.transpose(tap))
            else:
                place_taps(out_ref, vertical, lateral, tap)


def place_taps(out_ref, vertical, lateral, tap):
    for half in range(2):
        row = vertical * 64 if vertical < 2 else 128 + 64 * half
        column = 128 + 64 * half if lateral == 1 else 64 * ((lateral // 2 + half) % 2)
        out_ref[half, row : row + 64, column : column + 64] = tap


def taps_apart(windows, swapped, weight_ref):
    low = low_lanes(windows[0].shape)
    pair_low = jnp.where(low, windows[0], swapped[1]).astype(BF16)
    pair_high = jnp.where(low, swapped[0], windows[1]).astype(BF16)
    last = windows[2].astype(BF16)
    one = nn(jnp.concatenate([pair_low, last], axis=1), weight_ref[0])
    two = nn(jnp.concatenate([pair_high, last], axis=1), weight_ref[1])
    products = (
        jnp.where(low, one[:, 0:128], two[:, 0:128]),
        one[:, 128:256] + two[:, 128:256],
        swap(jnp.where(low, two[:, 0:128], one[:, 0:128])),
    )
    return products, jnp.concatenate([pair_low, pair_high, last], axis=1)


def from_left(values, low):
    return pltpu.roll(values, 1, axis=0) * low


def from_right(values, high):
    return pltpu.roll(values, values.shape[0] - 1, axis=0) * high


class Stats:
    def __init__(self, real_ref):
        self.real_ref = real_ref
        self.number = real_pixels(real_ref)
        self.near = None
        self.part = [jnp.zeros((8, 128), F32)] * 2
        self.whole = [jnp.zeros((8, 128), F32)] * 2

    def add(self, value):
        if self.near is None:
            self.near = low_both(total_of(value) / float(value.shape[0]))
        apart = value - self.near
        self.part = [self.part[0] + folded(apart), self.part[1] + folded(apart * apart)]

    def close(self, g):
        mask = pair_mask(self.real_ref, g)
        self.whole = [whole + part * mask for whole, part in zip(self.whole, self.part)]
        self.part = [jnp.zeros((8, 128), F32)] * 2

    def row(self):
        total, square = [total_of(value) for value in self.whole]
        total, square = total + swap(total), square + swap(square)
        square = square - total * total / self.number
        return jnp.where(low_lanes((1, 128)), total + self.number * self.near, square)


def prepare_kernel(
    sizes, feat_hbm, up_hbm, redt_hbm, count_ref, weight_ref, real_ref, near_ref, far_ref, redt_ref, sem_ref,
):
    step, own = sizes.step, sizes.own
    edges = []
    odd = lax.rem(lax.axis_index("ha"), 2)
    to_last = pl.multiple_of((1 - odd) * (own - step), step)
    to_head = pl.multiple_of(odd * (own - step), step)
    for out, start in ((near_ref, to_last), (far_ref, to_head)):
        for place, source in enumerate((feat_hbm, up_hbm)):
            copy = pltpu.make_async_copy(
                source.at[:, :, pl.ds(start, step), :], out.at[place], sem_ref.at[len(edges)]
            )
            copy.start()
            edges.append(copy)
    small = pltpu.make_async_copy(redt_hbm, redt_ref, sem_ref.at[4])
    small.start()
    fill_real(sizes, real_ref, count_ref[0])
    small.wait()
    diagonal(weight_ref, redt_ref[...])
    for copy in edges:
        copy.wait()


def reduce_kernel(sizes, feat_ref, weight_ref, real_ref, first_ref, sums_ref, out_ref):
    pairs, step = sizes.pairs, sizes.step
    stats = Stats(real_ref)
    feats = jnp.zeros((8, 256), F32)
    for g in range(pairs):
        low_sum = high_sum = jnp.zeros((8, 256), F32)
        for c in range(sizes.chunks):
            low = feat_ref[0, g, c * step : (c + 1) * step, :]
            high = feat_ref[1, g, c * step : (c + 1) * step, :]
            value = nt(jnp.concatenate([low, high], axis=1), weight_ref[...])
            first_ref[g, c * step : (c + 1) * step, :] = value
            stats.add(value)
            low_sum = low_sum + folded(low.astype(F32))
            high_sum = high_sum + folded(high.astype(F32))
        stats.close(g)
        feats = feats + low_sum * image_mask(sizes, real_ref, g)
        feats = feats + high_sum * image_mask(sizes, real_ref, g + pairs)
    feats = total_of(feats)
    sums_ref[...] = feats
    slots, count = sizes.rows1, sizes.count
    put_row(out_ref, 0, slots, count, stats.row())
    put_row(out_ref, 1, slots, count, stats.number)
    put_row(out_ref, 2, slots, count, feats[:, 0:128])
    put_row(out_ref, 3, slots, count, feats[:, 128:256])


def merged(sizes, got_ref, slots, numbers):
    rows = got_ref[pl.ds(0, sizes.count, stride=slots), :]
    whole = total_of(numbers)
    low = low_lanes(rows.shape)
    both = jnp.where(low, rows, swap(rows))
    average = total_of(both) / whole
    apart = both / numbers - average
    squares = jnp.where(low, swap(rows), rows)
    variance = total_of(squares + numbers * apart * apart) / whole
    return average, lax.rsqrt(variance + EPSILON), whole


def conv_kernel(
    sizes, got_ref, feat_ref, first_ref, near_ref, far_ref, weight_ref, taps_ref, gain_ref, bias_ref, real_ref,
    window_ref, slope_ref, second_ref, norm_ref, cross_ref, out_ref, conv_ref, hidden_ref, turned_ref, low_ref, high_ref, normed_ref,
):
    pairs, step, own, across = sizes.pairs, sizes.step, sizes.own, sizes.across
    numbers = got_ref[pl.ds(1, sizes.count, stride=sizes.rows1), :]
    average, inverse, whole = merged(sizes, got_ref, sizes.rows1, numbers)
    norm_ref[...] = jnp.concatenate([average, inverse, whole, jnp.zeros((5, 128), F32)], axis=0)
    gain, bias = twice(gain_ref[...]), twice(bias_ref[...])
    place = lax.axis_index("ha")
    odd = lax.rem(place, 2)
    has_far = jnp.logical_and(place > 0, place < lax.axis_size("ha") - 1).astype(F32)
    near_start = pl.multiple_of((1 - odd) * (own + step), step)
    far_start = pl.multiple_of(odd * (own + step), step)
    edge_masks(sizes, low_ref, high_ref)
    all_taps(conv_ref, taps_ref, False)
    for g in range(pairs):
        mask = pair_mask(real_ref, g)

        def activate(c, carry):
            normed = (first_ref[g, block(c * step, step), :] - average) * inverse
            value, slope = swish(normed * gain + bias)
            hidden_ref[g, block((c + 1) * step, step), :] = value
            turned_ref[g, block((c + 1) * step, step), :] = swap(value)
            slope_ref[g, block(c * step, step), :] = slope
            normed_ref[block(g * own + c * step, step), :] = (normed * mask).astype(BF16)
            return carry

        lax.fori_loop(0, sizes.chunks, activate, 0, unroll=True)
        for start, valid, rows_ref in ((near_start, 1.0, near_ref), (far_start, has_far, far_ref)):
            low, high = rows_ref[0, 0, g], rows_ref[0, 1, g]
            first = nt(jnp.concatenate([low, high], axis=1), weight_ref[...])
            value, _ = swish((first - average) * inverse * gain + bias)
            value = value * valid
            hidden_ref[g, pl.ds(start, step), :] = value
            turned_ref[g, pl.ds(start, step), :] = swap(value)
    cross = tn_pair(normed_ref[...], pair_rows(sizes, feat_ref))
    cross_ref[...] = cross

    def together(products):
        return from_left(products[0], low_ref[...]) + products[1] + from_right(products[2], high_ref[...])

    total = jnp.zeros((8, 128), F32)
    for g in range(pairs):
        part = jnp.zeros((8, 128), F32)
        starts = [slice((a + 1) * across, (a + 1) * across + own) for a in range(3)]
        products, window_ref[g] = taps_apart(
            *[[ref[g, start, :] for start in starts] for ref in (hidden_ref, turned_ref)], conv_ref
        )
        for c in range(sizes.chunks):
            rows = slice(c * step, (c + 1) * step)
            value = together([product[rows, :] for product in products])
            second_ref[g, rows, :] = value
            part = part + folded(value)
        total = total + part * pair_mask(real_ref, g)
        last = sizes.height + 1
        windows, swapped = [
            [
                jnp.concatenate(
                    [
                        ref[g, a * across : (a + 1) * across, :],
                        ref[g, (last + a) * across : (last + a + 1) * across, :],
                    ],
                    axis=0,
                )
                for a in range(3)
            ]
            for ref in (hidden_ref, turned_ref)
        ]
        products, _ = taps_apart(windows, swapped, conv_ref)
        second_ref[g, own : own + step, :] = together(products)
    total = total_of(total)
    total = total + swap(total)
    local = total / (real_pixels(real_ref))
    square = jnp.zeros((8, 128), F32)
    for g in range(pairs):
        part = jnp.zeros((8, 128), F32)
        for c in range(sizes.chunks):
            apart = second_ref[g, c * step : (c + 1) * step, :] - local
            part = part + folded(apart * apart)
        square = square + part * pair_mask(real_ref, g)
    square = total_of(square)
    square = square + swap(square)
    slots = sizes.rows2
    put_row(out_ref, 0, slots, sizes.count, jnp.where(low_lanes((1, 128)), total, square))
    put_cross(sizes, out_ref, 1, slots, cross, 0, sizes.cross_early)


def cross_rows(sizes):
    return [(half, part) for half in range(2) for part in range(sizes.share)]


def put_cross(sizes, out_ref, slot, slots, cross, start, stop):
    rows = min(sizes.count, 64)
    for index, (half, part) in enumerate(cross_rows(sizes)[start:stop]):
        matrix = cross[part * rows : (part + 1) * rows, half * 128 : (half + 1) * 128]
        out_ref[pl.ds(slot + index, rows, stride=slots), :] = matrix


def middle_kernel(
    sizes, got_ref, first_got_ref, second_ref, gain_ref, bias_ref, expander_ref, cross_ref, real_ref,
    hidden_ref, slope_ref, norm_ref, gram_ref, expand_ref, out_ref, left_ref, right_ref,
):
    pairs, step, own = sizes.pairs, sizes.step, sizes.own
    slots = sizes.rows3
    numbers = first_got_ref[pl.ds(1, sizes.count, stride=sizes.rows1), :]
    average, inverse, _ = merged(sizes, got_ref, sizes.rows2, numbers)
    gain, bias = twice(gain_ref[...]), twice(bias_ref[...])
    centre, tangent = swish(bias)
    diagonal(expand_ref, expander_ref[...])
    sums = (jnp.zeros((8, 128), F32),) * 3
    for g in range(pairs):
        mask = pair_mask(real_ref, g)

        def activate(c, acc):
            rows = block(c * step, step)
            normed = (second_ref[g, rows, :] - average) * inverse
            value, slope = swish(normed * gain + bias)
            rounded = value.astype(BF16)
            hidden_ref[g, rows, :] = rounded
            slope_ref[g, rows, :] = slope
            apart = (rounded.astype(F32) - centre) * mask
            slope = slope * mask
            tilted = slope * normed
            rows = block(g * own + c * step, step)
            left_ref[rows, :] = apart.astype(BF16)
            right_ref[rows, 0:128] = apart.astype(BF16)
            right_ref[rows, 128:256] = (slope - tangent).astype(BF16)
            right_ref[rows, 256:384] = tilted.astype(BF16)
            return acc[0] + folded(apart), acc[1] + folded(slope), acc[2] + folded(tilted)

        sums = lax.fori_loop(0, sizes.chunks, activate, sums, unroll=True)
        value, slope = swish((second_ref[g, own : own + step, :] - average) * inverse * gain + bias)
        hidden_ref[g, own : own + step, :] = value.astype(BF16)
        slope_ref[g, own : own + step, :] = slope
    product = tn(left_ref[...], right_ref[...])
    apart, slope, tilted = [total_of(value) for value in sums]
    apart, slope, tilted = apart + swap(apart), slope + swap(slope), tilted + swap(tilted)
    low, high = product[0:64, :], product[64:128, :]
    gram = low[:, 0:128] + swap(high[:, 0:128])
    slopes = low[:, 128:256] + swap(high[:, 128:256])
    tilts = swap(low[:, 256:384]) + high[:, 256:384]
    wide = low_lanes((64, 128))
    slopes = slopes + columns(apart)[0:64, :] * tangent
    gram = jnp.where(wide, gram, 0.0)
    gram_ref[...] = gram
    weights = expander_ref[...]
    quad = total_of(exact(nn, gram[:, 0:64], weights) * weights.astype(F32))
    norm_ref[...] = jnp.concatenate(
        [average, inverse, centre, apart, jnp.where(low_lanes((1, 128)), slope, tilted), jnp.zeros((3, 128), F32)],
        axis=0,
    )
    put_row(out_ref, 0, slots, sizes.count, quad[:, 0:128])
    put_row(out_ref, 1, slots, sizes.count, quad[:, 128:256])
    put_row(out_ref, 2, slots, sizes.count, apart)
    put_row(out_ref, 3, slots, sizes.count, jnp.where(low_lanes((1, 128)), slope, tilted))
    put_rows(out_ref, 4, slots, sizes.count, jnp.where(wide, slopes, tilts))
    put_cross(sizes, out_ref, 4 + sizes.share, slots, cross_ref[...], sizes.cross_early, 2 * sizes.share)


def output_kernel(
    sizes, got_ref, norm_one_ref, norm_ref, hidden_ref, slope_ref, second_ref, feat_ref, up_ref,
    near_ref, far_ref, gain_ref, bias_ref, expand_ref, real_ref,
    active_ref, gsum_ref, back_ref, last_ref, raw_ref, out_ref, scaled_ref,
):
    pairs, step, own, across = sizes.pairs, sizes.step, sizes.own, sizes.across
    odd = lax.rem(lax.axis_index("ha"), 2) == 1
    slots, count = sizes.rows3, sizes.count
    whole = norm_one_ref[2:3, :]
    centre = norm_ref[2:3, :]
    apart = get_sum(got_ref, 2, slots, count) / whole
    mean_hidden = centre + apart
    column = expand_ref[:, 0:256]
    shift, average = exact_rows(nn, [apart, mean_hidden], column)
    quad = jnp.concatenate([get_sum(got_ref, 0, slots, count), get_sum(got_ref, 1, slots, count)], axis=1)
    wide = jnp.concatenate([whole, whole], axis=1)
    inverse = lax.rsqrt(quad / wide - shift * shift + EPSILON)
    gain, bias = gain_ref[...], bias_ref[...]
    scale = gain * inverse
    offset = bias - average * scale
    average_two, inverse_two = norm_ref[0:1, :], norm_ref[1:2, :]

    def outward(third, feat):
        half_sum = 0.5 * (third * scale + offset + feat)
        turn = jnp.tanh(half_sum)
        plus = 1.0 + turn
        value = half_sum * plus
        return value, plus + value * (1.0 - turn)

    sample = slice(0, sizes.sample)
    _, slope = outward(nn(hidden_ref[0, sample, :], column), feat_ref[0, 0, sample, :].astype(F32))
    middle = 0.5 * total_of(up_ref[0, 0, sample, :].astype(F32) * slope) / float(sizes.sample)
    flat = scale * middle
    (flat_back,) = exact_rows(nt, [flat], expand_ref[:, 0:256] + expand_ref[:, 256:512])
    last_ref[...] = jnp.concatenate(
        [average, inverse, scale, jnp.concatenate([mean_hidden, apart], axis=1), middle, flat, shift, jnp.zeros((1, 256), F32)],
        axis=0,
    )
    biases = jnp.zeros((8, 256), F32)
    for g in range(pairs):
        valids = [image_mask(sizes, real_ref, g + half * pairs) for half in range(2)]
        middles = [middle * valid for valid in valids]

        def body(c, biases):
            hidden = hidden_ref[g, block(c * step, step), :]
            for half in range(2):
                image = g + half * pairs
                third = nn(hidden, expand_ref[:, half * 256 : (half + 1) * 256])
                for start in range(0, step, 16):
                    here = pl.ds(pl.multiple_of(c * step + start, 16), 16)
                    place = pl.ds(pl.multiple_of(image * own + c * step + start, 16), 16)
                    value, slope = outward(third[start : start + 16, :], feat_ref[half, g, here, :].astype(F32))
                    active_ref[place, :] = value.astype(BF16)
                    grad = up_ref[half, g, here, :].astype(F32) * (0.5 * valids[half]) * slope
                    gsum_ref[place, :] = grad
                    grad = grad - middles[half]
                    biases = biases + folded(grad)
                    there = pl.ds(pl.multiple_of(g * own + c * step + start, 16), 16)
                    scaled_ref[there, half * 256 : (half + 1) * 256] = (grad * scale).astype(BF16)
            return biases

        biases = lax.fori_loop(0, sizes.chunks, body, biases, unroll=True)
        hidden = hidden_ref[g, own : own + step, :]
        edge = pairs * own + g * step
        for half in range(2):
            image = g + half * pairs
            both = []
            for which in range(2):
                near = near_ref[which, half, g].astype(F32)
                far = far_ref[which, half, g].astype(F32)
                upper = jnp.where(odd, near[across:, :], far[across:, :])
                lower = jnp.where(odd, far[0:across, :], near[0:across, :])
                both.append(jnp.concatenate([upper, lower], axis=0))
            _, slope = outward(nn(hidden, expand_ref[:, half * 256 : (half + 1) * 256]), both[0])
            grad = both[1] * (0.5 * valids[half]) * slope
            scaled = ((grad - middles[half]) * scale).astype(BF16)
            scaled_ref[edge : edge + step, half * 256 : (half + 1) * 256] = scaled
    tops = tilts = jnp.zeros((8, 128), F32)
    backs = nt(scaled_ref[...], expand_ref[...])
    for g in range(pairs):
        back = backs[g * own : (g + 1) * own, :]
        back_ref[g, 0:own, :] = back
        top = slope_ref[g, 0:own, :] * back
        normed_two = (second_ref[g, 0:own, :] - average_two) * inverse_two
        tops, tilts = tops + folded(top), tilts + folded(top * normed_two)
        edge = pairs * own + g * step
        back_ref[g, own : own + step, :] = backs[edge : edge + step, :]
    raw = tn_pair(hidden_ref[:, 0:own, :].reshape(pairs * own, 128), scaled_ref[0 : pairs * own, :])
    raw_ref[...] = raw
    biases, tops, tilts = [total_of(value) for value in (biases, tops, tilts)]
    gains = total_of(raw * expand_ref[0:64, 0:256].astype(F32)) / scale - average * biases
    number = real_pixels(real_ref)
    (third_sum,) = exact_rows(nn, [norm_ref[3:4, :] - number * apart], column)
    gains = inverse * (gains + middle * third_sum)
    biases = biases + number[:, 0:1] * middle
    tops, tilts = tops + swap(tops), tilts + swap(tilts)
    tops = jnp.where(low_lanes((1, 128)), tops, tilts) + norm_ref[4:5, :] * flat_back
    sent = sizes.rows4
    put_row(out_ref, 0, sent, count, biases[:, 0:128])
    put_row(out_ref, 1, sent, count, biases[:, 128:256])
    put_row(out_ref, 2, sent, count, gains[:, 0:128])
    put_row(out_ref, 3, sent, count, gains[:, 128:256])
    put_row(out_ref, 4, sent, count, tops)
    for part in range(sizes.share):
        put_row(out_ref, 5 + part, sent, count, get_sum(got_ref, 4 + part, slots, count))


def backward_kernel(
    sizes, got_ref, third_got_ref, norm_one_ref, norm_ref, last_ref, gram_ref, window_ref, slope_one_ref,
    first_ref, hidden_ref, slope_ref, second_ref, back_ref, raw_ref, feat_ref, sums_ref, gain_two_ref, expand_ref,
    taps_ref, active_ref, count_ref,
    gain3_out_ref, bias3_out_ref, gain2_out_ref, bias2_out_ref, grad_one_ref, active_hbm, out_ref,
    conv_back_ref, grad_ref, turned_ref, low_ref, high_ref, right_ref, send_ref, sem_ref,
):
    pairs, step, own, across = sizes.pairs, sizes.step, sizes.own, sizes.across
    leave = pltpu.make_async_copy(active_ref, active_hbm, sem_ref)
    leave.start()
    share, count = sizes.share, sizes.count
    third_slots, slots = sizes.rows3, sizes.rows4
    whole = norm_one_ref[2:3, :]
    whole_wide = jnp.concatenate([whole, whole], axis=1)
    bias3 = jnp.concatenate([get_sum(got_ref, 0, slots, count), get_sum(got_ref, 1, slots, count)], axis=1)
    gain3 = jnp.concatenate([get_sum(got_ref, 2, slots, count), get_sum(got_ref, 3, slots, count)], axis=1)
    bias3_out_ref[...] = bias3
    gain3_out_ref[...] = gain3
    inverse3, scale3 = last_ref[1:2, :], last_ref[2:3, :]
    mean_hidden, apart = last_ref[3:4, 0:128], last_ref[3:4, 128:256]
    flat = scale3 * bias3 / whole_wide
    tilt = scale3 * inverse3 * gain3 / whole_wide
    diag = expand_ref[...]
    stacked = diag[:, 0:256] + diag[:, 256:512]
    flat_here = flat - last_ref[5:6, :]
    flat_back, flat_here_back, mean_mix, apart_mix = exact_rows(
        nt, [flat, flat_here, last_ref[0:1, :] * tilt, last_ref[6:7, :] * tilt], stacked
    )
    tilt_wide = jnp.concatenate([tilt, tilt], axis=1)
    mixing = exact(nt, diag.astype(F32) * tilt_wide, diag)
    mix_high, mix_low, _ = pieces(mixing)
    mix_both = jnp.concatenate([mix_high, mix_low], axis=1)
    row_low = low_lanes((1, 128))
    slopes = get_sum(third_got_ref, 3, third_slots, count)
    cross = get_rows(got_ref, 5, slots, count, 64)
    mixed = total_of((mixing[0:64, :] + mixing[64:128, :]) * cross)
    sums = get_sum(got_ref, 4, slots, count) - (slopes * (flat_back - apart_mix) + mixed)
    bias2, gain2 = low_both(sums), high_both(sums)
    bias2_out_ref[...] = bias2[:, 0:64]
    gain2_out_ref[...] = gain2[:, 0:64]
    average_two, inverse_two, centre = norm_ref[0:1, :], norm_ref[1:2, :], norm_ref[2:3, :]
    scale2 = twice(gain_two_ref[...]) * inverse_two
    base = flat_here_back - mean_mix
    place = lax.axis_index("ha")
    has_above = (place > 0).astype(F32)
    has_below = (place < lax.axis_size("ha") - 1).astype(F32)
    edge_masks(sizes, low_ref, high_ref)
    all_taps(conv_back_ref, taps_ref, True)
    average_one, inverse_one = norm_one_ref[0:1, :], norm_one_ref[1:2, :]

    local = norm_ref[3:4, :]
    number = count_ref[0].astype(F32) * sizes.pixels
    col_hidden = columns(local + number * centre)[0:64, :]
    col_local = columns(local)[0:64, :]
    col_centre = columns(centre)[0:64, :]
    around = gram_ref[...] - col_local * apart + col_centre * (local - number * apart)
    around = exact(nn, around[:, 0:64], diag[0:64, 0:256])
    col_wide = jnp.concatenate([col_hidden, col_hidden], axis=1)
    expander = raw_ref[...] - col_wide * flat_here - around * tilt

    sums = (jnp.zeros((8, 128), F32), jnp.zeros((8, 128), F32))
    for g in range(pairs):
        mask = count_mask(count_ref, g, pairs)

        def inward(rows):
            hidden = hidden_ref[g, rows, :]
            mixed = nn(hidden, mix_both)
            mixed = mixed[:, 0:128] + mixed[:, 128:256]
            grad = slope_ref[g, rows, :] * (back_ref[g, rows, :] - mask * (base + mixed))
            normed = (second_ref[g, rows, :] - average_two) * inverse_two
            return scale2 * (grad - mask * ((bias2 + normed * gain2) / whole))

        def store(c, carry):
            rows = block(c * step, step)
            grad = inward(rows)
            here = pl.ds(pl.multiple_of(c * step + across, 8), step)
            grad_ref[here, :] = grad
            turned_ref[here, :] = swap(grad)
            rows = block(g * own + c * step, step)
            right_ref[rows, 0:128] = from_right(grad, high_ref[...]).astype(BF16)
            right_ref[rows, 128:256] = grad.astype(BF16)
            right_ref[rows, 256:384] = from_left(grad, low_ref[...]).astype(BF16)
            return carry

        lax.fori_loop(0, sizes.chunks, store, 0, unroll=True)
        edge = inward(pl.ds(own, step))
        for start, value in ((0, edge[0:across, :] * has_above), (own + across, edge[across:, :] * has_below)):
            grad_ref[start : start + across, :] = value
            turned_ref[start : start + across, :] = swap(value)

        starts = [slice(a * across, a * across + own) for a in range(3)]
        products, _ = taps_apart(
            [grad_ref[start, :] for start in starts], [turned_ref[start, :] for start in starts[0:2]], conv_back_ref
        )
        for c in range(sizes.chunks):
            rows = slice(c * step, (c + 1) * step)
            value = from_right(products[0][rows, :], high_ref[...]) + products[1][rows, :]
            value = value + from_left(products[2][rows, :], low_ref[...])
            grad = value * slope_one_ref[g, rows, :]
            grad_one_ref[g, rows, :] = grad
            normed = (first_ref[g, rows, :] - average_one) * inverse_one
            sums = sums[0] + folded(grad), sums[1] + folded(grad * normed)
    product = tn(window_ref[...].reshape(pairs * own, 384), right_ref[...])
    grad = grad_one_ref[...].reshape(pairs * own, 128).astype(BF16)
    reducer = tn_pair(grad, pair_rows(sizes, feat_ref))
    tops, tilts = total_of(sums[0]), total_of(sums[1])
    tops, tilts = tops + swap(tops), tilts + swap(tilts)
    sent = sizes.rows5
    clear(sizes, send_ref, sent, 4 + 8 * share)
    for slot, row in enumerate(pieces(jnp.where(row_low, tops, tilts))):
        put_row(send_ref, slot, sent, count, row.astype(F32))
    reducer = reducer - jnp.concatenate([columns(tops / number)[0:64, :]] * 2, axis=1) * sums_ref[...]
    slot = 3
    for matrix in (reducer, expander):
        for half in range(2):
            put_rows(send_ref, slot, sent, count, matrix[:, half * 128 : (half + 1) * 128])
            slot += share
    wide = low_lanes((64, 128))

    def tap(index):
        row, column = index // 3, (index % 3) * 128
        rows = (64 * row, 128 + 64 * row) if row < 2 else (256, 320)
        return [product[start : start + 64, column : column + 128] for start in rows]

    for pair in range(4):
        low, high = tap(2 * pair)
        even = low + swap(high)
        low, high = tap(2 * pair + 1)
        odd = swap(low) + high
        put_rows(send_ref, slot, sent, count, jnp.where(wide, even, odd))
        slot += share
    low, high = tap(8)
    even = low + swap(high)
    put_rows(send_ref, slot, sent, count, jnp.where(low_lanes((32, 128)), even[0:32, :], swap(even[32:64, :])))
    out_ref[...] = send_ref[...].astype(BF16)
    leave.wait()


def shares_kernel(
    sizes, got_ref, first_got_ref, second_got_ref, third_got_ref, norm_one_ref, gain_ref, grad_ref, first_ref,
    gsum_ref, weight_ref, real_ref,
    gain_out_ref, bias_out_ref, feature_ref, out_ref,
    send_ref, wide_ref,
):
    share, count, pairs, step, own = sizes.share, sizes.count, sizes.pairs, sizes.step, sizes.own
    slots = sizes.rows5
    wide_ref[...] = got_ref[...].astype(F32)
    total = jnp.sum(wide_ref[...].reshape(count // 2, 2 * slots, 128), axis=0)
    total = total[0:slots, :] + total[slots:, :]
    whole = norm_one_ref[2:3, :]
    average, inverse = norm_one_ref[0:1, :], norm_one_ref[1:2, :]
    sums = total[0:1, :] + (total[1:2, :] + total[2:3, :])
    bias, gain = low_both(sums), high_both(sums)
    bias_out_ref[...] = bias[:, 0:64]
    gain_out_ref[...] = gain[:, 0:64]
    scale = twice(gain_ref[...]) * inverse
    bias, gain = bias / whole, gain / whole
    for g in range(pairs):
        mask = pair_mask(real_ref, g)

        def body(c, carry):
            rows = block(c * step, step)
            normed = (first_ref[g, rows, :] - average) * inverse
            grad = (scale * (grad_ref[g, rows, :] - mask * (bias + normed * gain))).astype(BF16)
            for half in range(2):
                place = block((g + half * pairs) * own + c * step, step)
                value = nn(grad, weight_ref[:, half * 256 : (half + 1) * 256])
                feature_ref[half, g, rows, :] = (value + gsum_ref[place, :]).astype(BF16)
            return carry

        lax.fori_loop(0, sizes.chunks, body, 0, unroll=True)
    me = lax.axis_index("img") * lax.axis_size("ha") + lax.axis_index("ha")
    lane = lax.broadcasted_iota(jnp.int32, (1, 128), 1)
    sent = sizes.rows6
    local = wide_ref[pl.ds(0, count, stride=slots), :] + (
        wide_ref[pl.ds(1, count, stride=slots), :] + wide_ref[pl.ds(2, count, stride=slots), :]
    )
    local = jnp.where(low_lanes(local.shape), local, swap(local))
    local = local / first_got_ref[pl.ds(1, count, stride=sizes.rows1), :] - bias
    clear(sizes, send_ref, sent, 1 + 8 * share)
    rows = jnp.concatenate([local, scale, gain, jnp.zeros((6, 128), F32)], axis=0)
    picked = [
        jnp.sum(jnp.where(lane == me + part * count, rows, 0.0), axis=1, keepdims=True) for part in range(share)
    ]
    for index, (half, part) in enumerate(cross_rows(sizes)):
        place = 3 + half * share + part
        raw = total[place : place + 1, :]
        if index < sizes.cross_early:
            cross = get_sum(second_got_ref, 1 + index, sizes.rows2, count)
        else:
            cross = get_sum(third_got_ref, 4 + share + index - sizes.cross_early, sizes.rows3, count)
        features = first_got_ref[pl.ds(2 + half, count, stride=sizes.rows1), :]
        local, factor, tilt = [picked[part][a:b, :] for a, b in ((0, count), (count, count + 1), (count + 1, count + 2))]
        value = factor * (raw + total_of(local * features) - tilt * cross)
        put_row(send_ref, half * share + part, sent, count, value)
    for slot in range(2 * share, 8 * share + 1):
        place = 3 + slot
        put_row(send_ref, slot, sent, count, total[place : place + 1, :])
    out_ref[...] = send_ref[...].astype(BF16)


def weights_kernel(sizes, got_ref, redt_out_ref, expander_out_ref, spatial_out_ref, wide_ref):
    share, count = sizes.share, sizes.count
    slots = sizes.rows6
    wide_ref[...] = got_ref[...].astype(F32)
    for out_ref, slot in ((redt_out_ref, 0), (expander_out_ref, 2 * share)):
        for half in range(2):
            out_ref[:, half * 128 : (half + 1) * 128] = get_rows(wide_ref, slot + half * share, slots, count, 64)
    for index in range(8):
        value = get_rows(wide_ref, (4 + index // 2) * share, slots, count, 64)
        if index % 2:
            value = swap(value)
        spatial_out_ref[index * 64 : (index + 1) * 64, :] = value[:, 0:64]
    value = get_rows(wide_ref, 8 * share, slots, count, 32)
    spatial_out_ref[512:544, :] = value[:, 0:64]
    spatial_out_ref[544:576, :] = swap(value)[:, 0:64]


def exchange(rows, count):
    pack = 2 if rows.dtype == BF16 else 1
    parted = rows.reshape(count, rows.shape[0] // (count * pack), pack, 128)
    return lax.all_to_all(parted, AXES, 0, 0).reshape(rows.shape)


def on_device(
    features,
    reducer,
    spatial,
    expander,
    gain_reduce,
    bias_reduce,
    gain_spatial,
    bias_spatial,
    gain_expand,
    bias_expand,
    upstream,
    image_counts,
):
    images, height, across, wide = features.shape
    count = lax.axis_size("img") * lax.axis_size("ha")
    sizes = Sizes(images, height, across, count)
    pairs, own, step = sizes.pairs, sizes.own, sizes.step
    flat = (images * own, wide)
    deep = (2, pairs, own, wide)
    feat_hbm, up_hbm = features.reshape(deep), upstream.reshape(deep)
    taps = spatial.reshape(9 * 64, 64)
    gain1, bias1, gain2, bias2, gain3, bias3 = [
        value.reshape(1, value.shape[0])
        for value in (gain_reduce, bias_reduce, gain_spatial, bias_spatial, gain_expand, bias_expand)
    ]
    outside = pl.BlockSpec(memory_space=pltpu.HBM)
    inside = pl.BlockSpec(memory_space=pltpu.VMEM)

    def shape(*dims, dtype=F32):
        return jax.ShapeDtypeStruct(dims, dtype)

    def call(kernel, outs, args, scratch=(), away=(), far=()):
        specs = []
        for arg in args:
            if arg is image_counts:
                specs.append(pl.BlockSpec(memory_space=pltpu.SMEM))
            else:
                specs.append(outside if any(arg is other for other in far) else inside)
        return pl.pallas_call(
            functools.partial(kernel, sizes),
            out_shape=outs,
            in_specs=specs,
            out_specs=tuple(outside if index in away else inside for index in range(len(outs))),
            scratch_shapes=list(scratch),
            compiler_params=pltpu.CompilerParams(vmem_limit_bytes=VMEM_MIB << 20),
        )(*args)

    ha = lax.axis_size("ha")
    near = [(i, i ^ 1) for i in range(ha)]
    far = [(i, i + 1) for i in range(1, ha - 1, 2)]
    far = far + [(target, source) for source, target in far]
    masks = [pltpu.VMEM((step, 128), F32), pltpu.VMEM((step, 128), F32)]

    given = tuple(
        pltpu.with_memory_space_constraint(value, pltpu.HBM)
        for value in (feat_hbm, up_hbm, reducer.T)
    )
    weight, real, near_rows, far_rows = call(
        prepare_kernel,
        (
            shape(128, 512, dtype=BF16),
            shape(16, 256),
            shape(2, 2, pairs, step, wide, dtype=BF16),
            shape(2, 2, pairs, step, wide, dtype=BF16),
        ),
        (*given, image_counts),
        [pltpu.VMEM((64, 256), BF16), pltpu.SemaphoreType.DMA((5,))],
        far=given,
    )
    near_rows = lax.ppermute(near_rows, "ha", near)
    far_rows = lax.ppermute(far_rows, "ha", far)
    feat = feat_hbm
    first, sums, rows = call(
        reduce_kernel,
        (shape(pairs, own, 128), shape(1, 256), shape(count * sizes.rows1, 128)),
        (feat, weight, real),
    )
    got1 = exchange(rows, count)
    windows, slope_one, second, norm_one, cross, rows = call(
        conv_kernel,
        (
            shape(pairs, own, 384, dtype=BF16),
            shape(pairs, own, 128),
            shape(pairs, sizes.ext, 128),
            shape(8, 128),
            shape(64, 256),
            shape(count * sizes.rows2, 128),
        ),
        (got1, feat, first, near_rows, far_rows, weight, taps, gain1, bias1, real),
        [pltpu.VMEM((2, 256, 256), BF16)] + [pltpu.VMEM((pairs, sizes.wide1, 128), F32)] * 2 + [*masks, pltpu.VMEM((pairs * own, 128), BF16)],
    )
    got2 = exchange(rows, count)
    hidden_two, slope_two, norm_two, gram, expand, rows = call(
        middle_kernel,
        (
            shape(pairs, sizes.ext, 128, dtype=BF16),
            shape(pairs, sizes.ext, 128),
            shape(8, 128),
            shape(64, 128),
            shape(128, 512, dtype=BF16),
            shape(count * sizes.rows3, 128),
        ),
        (got2, got1, second, gain2, bias2, expander, cross, real),
        [pltpu.VMEM((pairs * own, 128), BF16), pltpu.VMEM((pairs * own, 384), BF16)],
    )
    got3 = exchange(rows, count)
    active, grad_sum, back, norm_three, raw, rows = call(
        output_kernel,
        (
            shape(*flat, dtype=BF16),
            shape(*flat),
            shape(pairs, sizes.ext, 128),
            shape(8, 256),
            shape(64, 256),
            shape(count * sizes.rows4, 128),
        ),
        (
            got3, norm_one, norm_two, hidden_two, slope_two, second, feat, up_hbm, near_rows, far_rows,
            gain3, bias3, expand, real,
        ),
        [pltpu.VMEM((pairs * sizes.ext, 2 * wide), BF16)],
    )
    got4 = exchange(rows, count)
    gradgain3, gradbias3, gradgain2, gradbias2, grad_one, activated, rows = call(
        backward_kernel,
        (
            shape(1, 256),
            shape(1, 256),
            shape(1, 64),
            shape(1, 64),
            shape(pairs, own, 128),
            shape(*flat, dtype=BF16),
            shape(count * sizes.rows5, 128, dtype=BF16),
        ),
        (
            got4, got3, norm_one, norm_two, norm_three, gram, windows, slope_one, first, hidden_two,
            slope_two, second, back, raw, feat, sums, gain2, expand, taps, active, image_counts,
        ),
        [pltpu.VMEM((2, 256, 256), BF16)]
        + [pltpu.VMEM((sizes.wide2, 128), F32)] * 2
        + masks
        + [
            pltpu.VMEM((pairs * own, 384), BF16),
            pltpu.VMEM((count * sizes.rows5, 128), F32),
            pltpu.SemaphoreType.DMA,
        ],
        away=(5,),
    )
    got5 = exchange(rows, count)
    gradgain1, gradbias1, feature_grad, rows = call(
        shares_kernel,
        (
            shape(1, 64),
            shape(1, 64),
            pltpu.VMEM(deep, BF16),
            shape(count * sizes.rows6, 128, dtype=BF16),
        ),
        (got5, got1, got2, got3, norm_one, gain1, grad_one, first, grad_sum, weight, real),
        [pltpu.VMEM((count * sizes.rows6, 128), F32), pltpu.VMEM((count * sizes.rows5, 128), F32)],
    )
    got6 = exchange(rows, count)
    redt_grad, expander_grad, spatial_grad = call(
        weights_kernel,
        (shape(64, 256), shape(64, 256), shape(9 * 64, 64)),
        (got6,),
        [pltpu.VMEM((count * sizes.rows6, 128), F32)],
    )
    return (
        activated.reshape(features.shape),
        feature_grad.reshape(features.shape),
        redt_grad.T,
        spatial_grad.reshape(spatial.shape),
        expander_grad,
        gradgain1.reshape(64),
        gradbias1.reshape(64),
        gradgain2.reshape(64),
        gradbias2.reshape(64),
        gradgain3.reshape(256),
        gradbias3.reshape(256),
    )


def solution(mesh):
    whole = P("img", "ha", None, None)
    in_specs = (whole,) + (P(),) * 9 + (whole, P("img"))
    out_specs = (whole, whole) + (P(),) * 9
    return jax.shard_map(
        on_device, mesh=mesh, in_specs=in_specs, out_specs=out_specs, check_vma=False
    )
```

```python
import functools

import jax
import jax.numpy as jnp
from jax import lax
from jax.experimental import pallas as pl
from jax.experimental.pallas import tpu as pltpu
from jax.sharding import PartitionSpec as P

EPSILON = 1e-05
AXES = ("img", "ha")
F32 = jnp.float32
BF16 = jnp.bfloat16
VMEM_MIB = 16


def nn(left, right):
    return lax.dot_general(left, right, (((1,), (0,)), ((), ())), preferred_element_type=F32)


def nt(left, right):
    return lax.dot_general(left, right, (((1,), (1,)), ((), ())), preferred_element_type=F32)


def tn(left, right):
    return lax.dot_general(left, right, (((0,), (0,)), ((), ())), preferred_element_type=F32)


def pair_rows(sizes, ref):
    return jnp.concatenate([ref[half].reshape(sizes.pairs * sizes.own, 256) for half in range(2)], axis=1)


def tn_pair(left, right):
    product = tn(left, right)
    return product[0:64, 0:256] + product[64:128, 256:512]


def pieces(values):
    high = values.astype(BF16)
    rest = values - high.astype(F32)
    middle = rest.astype(BF16)
    low = (rest - middle.astype(F32)).astype(BF16)
    return high, middle, low


def exact(product, values, weights):
    high, middle, _ = pieces(values)
    return product(high, weights) + product(middle, weights)


def exact_rows(product, rows, weights):
    parts = [part for row in rows for part in pieces(row)]
    parts = parts + [jnp.zeros_like(parts[0])] * (-len(parts) % 8)
    result = product(jnp.concatenate([part.astype(F32) for part in parts], axis=0).astype(BF16), weights)
    return [total_of(result[3 * index : 3 * index + 3, :]) for index in range(len(rows))]


def folded(values):
    return jnp.sum(values.reshape(values.shape[0] // 8, 8, values.shape[1]), axis=0)


def total_of(values):
    return jnp.sum(values, axis=0, keepdims=True)


def swap(values):
    return pltpu.roll(values, 64, axis=1)


def low_lanes(shape):
    return lax.broadcasted_iota(jnp.int32, shape, 1) < 64


def low_both(row):
    return jnp.where(low_lanes(row.shape), row, swap(row))


def high_both(row):
    return jnp.where(low_lanes(row.shape), swap(row), row)


def twice(row):
    place = lax.broadcasted_iota(jnp.int32, (64, 128), 0)
    lane = lax.rem(lax.broadcasted_iota(jnp.int32, (64, 128), 1), 64)
    return exact_rows(nn, [row], (place == lane).astype(BF16))[0]


def swish(values):
    half = 0.5 * values
    turn = jnp.tanh(half)
    plus = 1.0 + turn
    value = half * plus
    return value, 0.5 * (plus + value * (1.0 - turn))


def fill_real(sizes, out_ref, count):
    count = jnp.zeros((1, 256), F32) + count.astype(F32)
    low = lax.rem(lax.broadcasted_iota(jnp.int32, (1, 256), 1), 128) < 64
    images = [(float(image) < count).astype(F32) for image in range(sizes.images)]
    rows = [jnp.where(low, images[g], images[g + sizes.pairs]) for g in range(sizes.pairs)] + images
    rows = rows + [jnp.zeros((1, 256), F32)] * (15 - len(rows)) + [count * sizes.pixels]
    out_ref[...] = jnp.concatenate(rows, axis=0)


def pair_mask(real_ref, g):
    return real_ref[g : g + 1, 0:128]


def count_mask(count_ref, g, pairs):
    count = count_ref[0]
    low = (g < count).astype(F32)
    high = (g + pairs < count).astype(F32)
    return jnp.where(low_lanes((1, 128)), low, high)


def image_mask(sizes, real_ref, image):
    return real_ref[sizes.pairs + image : sizes.pairs + image + 1, :]


def real_pixels(real_ref):
    return real_ref[15:16, 0:128]


def columns(row):
    return jnp.transpose(jnp.broadcast_to(row, (128, 128)))


def put_row(out_ref, slot, slots, count, row):
    out_ref[pl.ds(slot, count, stride=slots), :] = jnp.broadcast_to(row, (count, 128))


def put_rows(out_ref, slot, slots, count, matrix):
    rows = min(count, matrix.shape[0])
    for part in range(matrix.shape[0] // rows):
        out_ref[pl.ds(slot + part, rows, stride=slots), :] = matrix[part * rows : (part + 1) * rows, :]


def get_sum(got_ref, slot, slots, count):
    return total_of(got_ref[pl.ds(slot, count, stride=slots), :])


def get_rows(got_ref, slot, slots, count, height):
    rows = min(count, height)
    parts = [got_ref[pl.ds(slot + part, rows, stride=slots), :] for part in range(height // rows)]
    return parts[0] if len(parts) == 1 else jnp.concatenate(parts, axis=0)


def clear(sizes, out_ref, slots, used):
    if sizes.count > 64:
        out_ref[...] = jnp.zeros(out_ref.shape, F32)
    else:
        for slot in range(used, slots):
            put_row(out_ref, slot, slots, sizes.count, jnp.zeros((1, 128), F32))


class Sizes:
    def __init__(self, images, height, across, count):
        self.images, self.height, self.across, self.count = images, height, across, count
        self.pairs = images // 2
        self.own = height * across
        self.pixels = float(height * across)
        self.step = 2 * across
        self.chunks = height // 2
        self.ext = self.own + self.step
        self.sample = 32
        self.wide1 = (height + 4) * across
        self.wide2 = (height + 2) * across
        self.share = max(1, 64 // count)
        self.rows1 = 4
        self.cross_early = min(3, 2 * self.share)
        self.cross_late = 2 * self.share - self.cross_early
        self.rows2 = 4
        self.rows3 = 4 + self.share + self.cross_late
        self.rows4 = 5 + self.share
        self.rows5 = -(-(4 + 8 * self.share) // 4) * 4
        self.rows6 = -(-(1 + 8 * self.share) // 2) * 2


def block(start, size):
    return pl.ds(pl.multiple_of(start, size), size)


def diagonal(out_ref, weight):
    out_ref[...] = jnp.zeros(out_ref.shape, out_ref.dtype)
    out_ref[0:64, 0:256] = weight
    out_ref[64:128, 256:512] = weight


def edge_masks(sizes, low_ref, high_ref):
    column = lax.rem(lax.broadcasted_iota(jnp.int32, (sizes.step, 128), 0), sizes.across)
    low_ref[...] = (column > 0).astype(F32)
    high_ref[...] = (column < sizes.across - 1).astype(F32)


def all_taps(out_ref, taps_ref, back):
    out_ref[...] = jnp.zeros(out_ref.shape, BF16)
    for vertical in range(3):
        for lateral in range(3):
            tap = taps_ref[(vertical * 3 + lateral) * 64 : (vertical * 3 + lateral + 1) * 64, :]
            if back:
                place_taps(out_ref, 2 - vertical, lateral, jnp.transpose(tap))
            else:
                place_taps(out_ref, vertical, lateral, tap)


def place_taps(out_ref, vertical, lateral, tap):
    for half in range(2):
        row = vertical * 64 if vertical < 2 else 128 + 64 * half
        column = 128 + 64 * half if lateral == 1 else 64 * ((lateral // 2 + half) % 2)
        out_ref[half, row : row + 64, column : column + 64] = tap


def taps_apart(windows, swapped, weight_ref):
    low = low_lanes(windows[0].shape)
    pair_low = jnp.where(low, windows[0], swapped[1]).astype(BF16)
    pair_high = jnp.where(low, swapped[0], windows[1]).astype(BF16)
    last = windows[2].astype(BF16)
    one = nn(jnp.concatenate([pair_low, last], axis=1), weight_ref[0])
    two = nn(jnp.concatenate([pair_high, last], axis=1), weight_ref[1])
    products = (
        jnp.where(low, one[:, 0:128], two[:, 0:128]),
        one[:, 128:256] + two[:, 128:256],
        swap(jnp.where(low, two[:, 0:128], one[:, 0:128])),
    )
    return products, jnp.concatenate([pair_low, pair_high, last], axis=1)


def from_left(values, low):
    return pltpu.roll(values, 1, axis=0) * low


def from_right(values, high):
    return pltpu.roll(values, values.shape[0] - 1, axis=0) * high


class Stats:
    def __init__(self, real_ref):
        self.real_ref = real_ref
        self.number = real_pixels(real_ref)
        self.near = None
        self.part = [jnp.zeros((8, 128), F32)] * 2
        self.whole = [jnp.zeros((8, 128), F32)] * 2

    def add(self, value):
        if self.near is None:
            self.near = low_both(total_of(value) / float(value.shape[0]))
        apart = value - self.near
        self.part = [self.part[0] + folded(apart), self.part[1] + folded(apart * apart)]

    def close(self, g):
        mask = pair_mask(self.real_ref, g)
        self.whole = [whole + part * mask for whole, part in zip(self.whole, self.part)]
        self.part = [jnp.zeros((8, 128), F32)] * 2

    def row(self):
        total, square = [total_of(value) for value in self.whole]
        total, square = total + swap(total), square + swap(square)
        square = square - total * total / self.number
        return jnp.where(low_lanes((1, 128)), total + self.number * self.near, square)


def prepare_kernel(
    sizes, feat_hbm, up_hbm, redt_hbm, count_ref, weight_ref, real_ref, near_ref, far_ref, redt_ref, sem_ref,
):
    step, own = sizes.step, sizes.own
    edges = []
    odd = lax.rem(lax.axis_index("ha"), 2)
    to_last = pl.multiple_of((1 - odd) * (own - step), step)
    to_head = pl.multiple_of(odd * (own - step), step)
    for out, start in ((near_ref, to_last), (far_ref, to_head)):
        for place, source in enumerate((feat_hbm, up_hbm)):
            copy = pltpu.make_async_copy(
                source.at[:, :, pl.ds(start, step), :], out.at[place], sem_ref.at[len(edges)]
            )
            copy.start()
            edges.append(copy)
    small = pltpu.make_async_copy(redt_hbm, redt_ref, sem_ref.at[4])
    small.start()
    fill_real(sizes, real_ref, count_ref[0])
    small.wait()
    diagonal(weight_ref, redt_ref[...])
    for copy in edges:
        copy.wait()


def reduce_kernel(sizes, feat_ref, weight_ref, real_ref, first_ref, sums_ref, out_ref):
    pairs, step = sizes.pairs, sizes.step
    stats = Stats(real_ref)
    feats = jnp.zeros((8, 256), F32)
    for g in range(pairs):
        low_sum = high_sum = jnp.zeros((8, 256), F32)
        for c in range(sizes.chunks):
            low = feat_ref[0, g, c * step : (c + 1) * step, :]
            high = feat_ref[1, g, c * step : (c + 1) * step, :]
            value = nt(jnp.concatenate([low, high], axis=1), weight_ref[...])
            first_ref[g, c * step : (c + 1) * step, :] = value
            stats.add(value)
            low_sum = low_sum + folded(low.astype(F32))
            high_sum = high_sum + folded(high.astype(F32))
        stats.close(g)
        feats = feats + low_sum * image_mask(sizes, real_ref, g)
        feats = feats + high_sum * image_mask(sizes, real_ref, g + pairs)
    feats = total_of(feats)
    sums_ref[...] = feats
    slots, count = sizes.rows1, sizes.count
    put_row(out_ref, 0, slots, count, stats.row())
    put_row(out_ref, 1, slots, count, stats.number)
    put_row(out_ref, 2, slots, count, feats[:, 0:128])
    put_row(out_ref, 3, slots, count, feats[:, 128:256])


def merged(sizes, got_ref, slots, numbers):
    rows = got_ref[pl.ds(0, sizes.count, stride=slots), :]
    whole = total_of(numbers)
    low = low_lanes(rows.shape)
    both = jnp.where(low, rows, swap(rows))
    average = total_of(both) / whole
    apart = both / numbers - average
    squares = jnp.where(low, swap(rows), rows)
    variance = total_of(squares + numbers * apart * apart) / whole
    return average, lax.rsqrt(variance + EPSILON), whole


def conv_kernel(
    sizes, got_ref, feat_ref, first_ref, near_ref, far_ref, weight_ref, taps_ref, gain_ref, bias_ref, real_ref,
    window_ref, slope_ref, second_ref, norm_ref, cross_ref, out_ref, conv_ref, hidden_ref, turned_ref, low_ref, high_ref, normed_ref,
):
    pairs, step, own, across = sizes.pairs, sizes.step, sizes.own, sizes.across
    numbers = got_ref[pl.ds(1, sizes.count, stride=sizes.rows1), :]
    average, inverse, whole = merged(sizes, got_ref, sizes.rows1, numbers)
    norm_ref[...] = jnp.concatenate([average, inverse, whole, jnp.zeros((5, 128), F32)], axis=0)
    gain, bias = twice(gain_ref[...]), twice(bias_ref[...])
    place = lax.axis_index("ha")
    odd = lax.rem(place, 2)
    has_far = jnp.logical_and(place > 0, place < lax.axis_size("ha") - 1).astype(F32)
    near_start = pl.multiple_of((1 - odd) * (own + step), step)
    far_start = pl.multiple_of(odd * (own + step), step)
    edge_masks(sizes, low_ref, high_ref)
    all_taps(conv_ref, taps_ref, False)
    for g in range(pairs):
        mask = pair_mask(real_ref, g)

        def activate(c, carry):
            normed = (first_ref[g, block(c * step, step), :] - average) * inverse
            value, slope = swish(normed * gain + bias)
            hidden_ref[g, block((c + 1) * step, step), :] = value
            turned_ref[g, block((c + 1) * step, step), :] = swap(value)
            slope_ref[g, block(c * step, step), :] = slope
            normed_ref[block(g * own + c * step, step), :] = (normed * mask).astype(BF16)
            return carry

        lax.fori_loop(0, sizes.chunks, activate, 0, unroll=True)
        for start, valid, rows_ref in ((near_start, 1.0, near_ref), (far_start, has_far, far_ref)):
            low, high = rows_ref[0, 0, g], rows_ref[0, 1, g]
            first = nt(jnp.concatenate([low, high], axis=1), weight_ref[...])
            value, _ = swish((first - average) * inverse * gain + bias)
            value = value * valid
            hidden_ref[g, pl.ds(start, step), :] = value
            turned_ref[g, pl.ds(start, step), :] = swap(value)
    cross = tn_pair(normed_ref[...], pair_rows(sizes, feat_ref))
    cross_ref[...] = cross

    def together(products):
        return from_left(products[0], low_ref[...]) + products[1] + from_right(products[2], high_ref[...])

    total = jnp.zeros((8, 128), F32)
    for g in range(pairs):
        part = jnp.zeros((8, 128), F32)
        starts = [slice((a + 1) * across, (a + 1) * across + own) for a in range(3)]
        products, window_ref[g] = taps_apart(
            *[[ref[g, start, :] for start in starts] for ref in (hidden_ref, turned_ref)], conv_ref
        )
        for c in range(sizes.chunks):
            rows = slice(c * step, (c + 1) * step)
            value = together([product[rows, :] for product in products])
            second_ref[g, rows, :] = value
            part = part + folded(value)
        total = total + part * pair_mask(real_ref, g)
        last = sizes.height + 1
        windows, swapped = [
            [
                jnp.concatenate(
                    [
                        ref[g, a * across : (a + 1) * across, :],
                        ref[g, (last + a) * across : (last + a + 1) * across, :],
                    ],
                    axis=0,
                )
                for a in range(3)
            ]
            for ref in (hidden_ref, turned_ref)
        ]
        products, _ = taps_apart(windows, swapped, conv_ref)
        second_ref[g, own : own + step, :] = together(products)
    total = total_of(total)
    total = total + swap(total)
    local = total / (real_pixels(real_ref))
    square = jnp.zeros((8, 128), F32)
    for g in range(pairs):
        part = jnp.zeros((8, 128), F32)
        for c in range(sizes.chunks):
            apart = second_ref[g, c * step : (c + 1) * step, :] - local
            part = part + folded(apart * apart)
        square = square + part * pair_mask(real_ref, g)
    square = total_of(square)
    square = square + swap(square)
    slots = sizes.rows2
    put_row(out_ref, 0, slots, sizes.count, jnp.where(low_lanes((1, 128)), total, square))
    put_cross(sizes, out_ref, 1, slots, cross, 0, sizes.cross_early)


def cross_rows(sizes):
    return [(half, part) for half in range(2) for part in range(sizes.share)]


def put_cross(sizes, out_ref, slot, slots, cross, start, stop):
    rows = min(sizes.count, 64)
    for index, (half, part) in enumerate(cross_rows(sizes)[start:stop]):
        matrix = cross[part * rows : (part + 1) * rows, half * 128 : (half + 1) * 128]
        out_ref[pl.ds(slot + index, rows, stride=slots), :] = matrix


def middle_kernel(
    sizes, got_ref, first_got_ref, second_ref, gain_ref, bias_ref, expander_ref, cross_ref, real_ref,
    hidden_ref, slope_ref, norm_ref, gram_ref, expand_ref, out_ref, left_ref, right_ref,
):
    pairs, step, own = sizes.pairs, sizes.step, sizes.own
    slots = sizes.rows3
    numbers = first_got_ref[pl.ds(1, sizes.count, stride=sizes.rows1), :]
    average, inverse, _ = merged(sizes, got_ref, sizes.rows2, numbers)
    gain, bias = twice(gain_ref[...]), twice(bias_ref[...])
    centre, tangent = swish(bias)
    centre = 0.125 * jnp.floor(8.0 * centre + 0.5)
    diagonal(expand_ref, expander_ref[...])
    sums = (jnp.zeros((8, 128), F32),) * 3
    for g in range(pairs):
        mask = pair_mask(real_ref, g)

        def activate(c, acc):
            rows = block(c * step, step)
            normed = (second_ref[g, rows, :] - average) * inverse
            value, slope = swish(normed * gain + bias)
            rounded = value.astype(BF16)
            hidden_ref[g, rows, :] = rounded
            slope_ref[g, rows, :] = slope
            apart = (rounded.astype(F32) - centre) * mask
            slope = slope * mask
            tilted = slope * normed
            rows = block(g * own + c * step, step)
            left_ref[rows, :] = apart.astype(BF16)
            right_ref[rows, 0:128] = apart.astype(BF16)
            right_ref[rows, 128:256] = (slope - tangent).astype(BF16)
            right_ref[rows, 256:384] = tilted.astype(BF16)
            return acc[0] + folded(apart), acc[1] + folded(slope), acc[2] + folded(tilted)

        sums = lax.fori_loop(0, sizes.chunks, activate, sums, unroll=True)
        value, slope = swish((second_ref[g, own : own + step, :] - average) * inverse * gain + bias)
        hidden_ref[g, own : own + step, :] = value.astype(BF16)
        slope_ref[g, own : own + step, :] = slope
    product = tn(left_ref[...], right_ref[...])
    apart, slope, tilted = [total_of(value) for value in sums]
    apart, slope, tilted = apart + swap(apart), slope + swap(slope), tilted + swap(tilted)
    low, high = product[0:64, :], product[64:128, :]
    gram = low[:, 0:128] + swap(high[:, 0:128])
    slopes = low[:, 128:256] + swap(high[:, 128:256])
    tilts = swap(low[:, 256:384]) + high[:, 256:384]
    wide = low_lanes((64, 128))
    slopes = slopes + columns(apart)[0:64, :] * tangent
    gram = jnp.where(wide, gram, 0.0)
    gram_ref[...] = gram
    weights = expander_ref[...]
    quad = total_of(exact(nn, gram[:, 0:64], weights) * weights.astype(F32))
    norm_ref[...] = jnp.concatenate(
        [average, inverse, centre, apart, jnp.where(low_lanes((1, 128)), slope, tilted), jnp.zeros((3, 128), F32)],
        axis=0,
    )
    put_row(out_ref, 0, slots, sizes.count, quad[:, 0:128])
    put_row(out_ref, 1, slots, sizes.count, quad[:, 128:256])
    put_row(out_ref, 2, slots, sizes.count, apart)
    put_row(out_ref, 3, slots, sizes.count, jnp.where(low_lanes((1, 128)), slope, tilted))
    put_rows(out_ref, 4, slots, sizes.count, jnp.where(wide, slopes, tilts))
    put_cross(sizes, out_ref, 4 + sizes.share, slots, cross_ref[...], sizes.cross_early, 2 * sizes.share)


def output_kernel(
    sizes, got_ref, norm_one_ref, norm_ref, hidden_ref, slope_ref, second_ref, feat_ref, up_ref,
    near_ref, far_ref, gain_ref, bias_ref, expand_ref, real_ref,
    active_ref, gsum_ref, back_ref, last_ref, raw_ref, out_ref, scaled_ref,
):
    pairs, step, own, across = sizes.pairs, sizes.step, sizes.own, sizes.across
    odd = lax.rem(lax.axis_index("ha"), 2) == 1
    slots, count = sizes.rows3, sizes.count
    whole = norm_one_ref[2:3, :]
    centre = norm_ref[2:3, :]
    apart = get_sum(got_ref, 2, slots, count) / whole
    mean_hidden = centre + apart
    column = expand_ref[:, 0:256]
    shift, average = exact_rows(nn, [apart, mean_hidden], column)
    quad = jnp.concatenate([get_sum(got_ref, 0, slots, count), get_sum(got_ref, 1, slots, count)], axis=1)
    wide = jnp.concatenate([whole, whole], axis=1)
    inverse = lax.rsqrt(quad / wide - shift * shift + EPSILON)
    gain, bias = gain_ref[...], bias_ref[...]
    scale = gain * inverse
    offset = bias - average * scale
    average_two, inverse_two = norm_ref[0:1, :], norm_ref[1:2, :]

    def outward(third, feat):
        half_sum = 0.5 * (third * scale + offset + feat)
        turn = jnp.tanh(half_sum)
        plus = 1.0 + turn
        value = half_sum * plus
        return value, plus + value * (1.0 - turn)

    sample = slice(0, sizes.sample)
    _, slope = outward(nn(hidden_ref[0, sample, :], column), feat_ref[0, 0, sample, :].astype(F32))
    middle = 0.5 * total_of(up_ref[0, 0, sample, :].astype(F32) * slope) / float(sizes.sample)
    flat = scale * middle
    (flat_back,) = exact_rows(nt, [flat], expand_ref[:, 0:256] + expand_ref[:, 256:512])
    last_ref[...] = jnp.concatenate(
        [average, inverse, scale, jnp.concatenate([mean_hidden, apart], axis=1), middle, flat, shift, jnp.zeros((1, 256), F32)],
        axis=0,
    )
    biases = jnp.zeros((8, 256), F32)
    for g in range(pairs):
        valids = [image_mask(sizes, real_ref, g + half * pairs) for half in range(2)]
        middles = [middle * valid for valid in valids]

        def body(c, biases):
            hidden = hidden_ref[g, block(c * step, step), :]
            for half in range(2):
                image = g + half * pairs
                third = nn(hidden, expand_ref[:, half * 256 : (half + 1) * 256])
                for start in range(0, step, 16):
                    here = pl.ds(pl.multiple_of(c * step + start, 16), 16)
                    place = pl.ds(pl.multiple_of(image * own + c * step + start, 16), 16)
                    value, slope = outward(third[start : start + 16, :], feat_ref[half, g, here, :].astype(F32))
                    active_ref[place, :] = value.astype(BF16)
                    grad = up_ref[half, g, here, :].astype(F32) * (0.5 * valids[half]) * slope
                    gsum_ref[place, :] = grad
                    grad = grad - middles[half]
                    biases = biases + folded(grad)
                    there = pl.ds(pl.multiple_of(g * own + c * step + start, 16), 16)
                    scaled_ref[there, half * 256 : (half + 1) * 256] = (grad * scale).astype(BF16)
            return biases

        biases = lax.fori_loop(0, sizes.chunks, body, biases, unroll=True)
        hidden = hidden_ref[g, own : own + step, :]
        edge = pairs * own + g * step
        for half in range(2):
            image = g + half * pairs
            both = []
            for which in range(2):
                near = near_ref[which, half, g].astype(F32)
                far = far_ref[which, half, g].astype(F32)
                upper = jnp.where(odd, near[across:, :], far[across:, :])
                lower = jnp.where(odd, far[0:across, :], near[0:across, :])
                both.append(jnp.concatenate([upper, lower], axis=0))
            _, slope = outward(nn(hidden, expand_ref[:, half * 256 : (half + 1) * 256]), both[0])
            grad = both[1] * (0.5 * valids[half]) * slope
            scaled = ((grad - middles[half]) * scale).astype(BF16)
            scaled_ref[edge : edge + step, half * 256 : (half + 1) * 256] = scaled
    tops = tilts = jnp.zeros((8, 128), F32)
    backs = nt(scaled_ref[...], expand_ref[...])
    for g in range(pairs):
        back = backs[g * own : (g + 1) * own, :]
        back_ref[g, 0:own, :] = back
        top = slope_ref[g, 0:own, :] * back
        normed_two = (second_ref[g, 0:own, :] - average_two) * inverse_two
        tops, tilts = tops + folded(top), tilts + folded(top * normed_two)
        edge = pairs * own + g * step
        back_ref[g, own : own + step, :] = backs[edge : edge + step, :]
    raw = tn_pair(hidden_ref[:, 0:own, :].reshape(pairs * own, 128), scaled_ref[0 : pairs * own, :])
    raw_ref[...] = raw
    biases, tops, tilts = [total_of(value) for value in (biases, tops, tilts)]
    gains = total_of(raw * expand_ref[0:64, 0:256].astype(F32)) / scale - average * biases
    number = real_pixels(real_ref)
    (third_sum,) = exact_rows(nn, [norm_ref[3:4, :] - number * apart], column)
    gains = inverse * (gains + middle * third_sum)
    biases = biases + number[:, 0:1] * middle
    tops, tilts = tops + swap(tops), tilts + swap(tilts)
    tops = jnp.where(low_lanes((1, 128)), tops, tilts) + norm_ref[4:5, :] * flat_back
    sent = sizes.rows4
    put_row(out_ref, 0, sent, count, biases[:, 0:128])
    put_row(out_ref, 1, sent, count, biases[:, 128:256])
    put_row(out_ref, 2, sent, count, gains[:, 0:128])
    put_row(out_ref, 3, sent, count, gains[:, 128:256])
    put_row(out_ref, 4, sent, count, tops)
    for part in range(sizes.share):
        put_row(out_ref, 5 + part, sent, count, get_sum(got_ref, 4 + part, slots, count))


def backward_kernel(
    sizes, got_ref, third_got_ref, norm_one_ref, norm_ref, last_ref, gram_ref, window_ref, slope_one_ref,
    first_ref, hidden_ref, slope_ref, second_ref, back_ref, raw_ref, feat_ref, sums_ref, gain_two_ref, expand_ref,
    taps_ref, active_ref, count_ref,
    gain3_out_ref, bias3_out_ref, gain2_out_ref, bias2_out_ref, grad_one_ref, active_hbm, out_ref,
    conv_back_ref, grad_ref, turned_ref, low_ref, high_ref, right_ref, send_ref, sem_ref,
):
    pairs, step, own, across = sizes.pairs, sizes.step, sizes.own, sizes.across
    leave = pltpu.make_async_copy(active_ref, active_hbm, sem_ref)
    leave.start()
    share, count = sizes.share, sizes.count
    third_slots, slots = sizes.rows3, sizes.rows4
    whole = norm_one_ref[2:3, :]
    whole_wide = jnp.concatenate([whole, whole], axis=1)
    bias3 = jnp.concatenate([get_sum(got_ref, 0, slots, count), get_sum(got_ref, 1, slots, count)], axis=1)
    gain3 = jnp.concatenate([get_sum(got_ref, 2, slots, count), get_sum(got_ref, 3, slots, count)], axis=1)
    bias3_out_ref[...] = bias3
    gain3_out_ref[...] = gain3
    inverse3, scale3 = last_ref[1:2, :], last_ref[2:3, :]
    mean_hidden, apart = last_ref[3:4, 0:128], last_ref[3:4, 128:256]
    flat = scale3 * bias3 / whole_wide
    tilt = scale3 * inverse3 * gain3 / whole_wide
    diag = expand_ref[...]
    stacked = diag[:, 0:256] + diag[:, 256:512]
    flat_here = flat - last_ref[5:6, :]
    flat_back, flat_here_back, mean_mix, apart_mix = exact_rows(
        nt, [flat, flat_here, last_ref[0:1, :] * tilt, last_ref[6:7, :] * tilt], stacked
    )
    tilt_wide = jnp.concatenate([tilt, tilt], axis=1)
    mixing = exact(nt, diag.astype(F32) * tilt_wide, diag)
    mix_high, mix_low, _ = pieces(mixing)
    mix_both = jnp.concatenate([mix_high, mix_low], axis=1)
    row_low = low_lanes((1, 128))
    slopes = get_sum(third_got_ref, 3, third_slots, count)
    cross = get_rows(got_ref, 5, slots, count, 64)
    mixed = total_of((mixing[0:64, :] + mixing[64:128, :]) * cross)
    sums = get_sum(got_ref, 4, slots, count) - (slopes * (flat_back - apart_mix) + mixed)
    bias2, gain2 = low_both(sums), high_both(sums)
    bias2_out_ref[...] = bias2[:, 0:64]
    gain2_out_ref[...] = gain2[:, 0:64]
    average_two, inverse_two, centre = norm_ref[0:1, :], norm_ref[1:2, :], norm_ref[2:3, :]
    scale2 = twice(gain_two_ref[...]) * inverse_two
    base = flat_here_back - mean_mix
    place = lax.axis_index("ha")
    has_above = (place > 0).astype(F32)
    has_below = (place < lax.axis_size("ha") - 1).astype(F32)
    edge_masks(sizes, low_ref, high_ref)
    all_taps(conv_back_ref, taps_ref, True)
    average_one, inverse_one = norm_one_ref[0:1, :], norm_one_ref[1:2, :]

    local = norm_ref[3:4, :]
    number = count_ref[0].astype(F32) * sizes.pixels
    col_hidden = columns(local + number * centre)[0:64, :]
    col_local = columns(local)[0:64, :]
    col_centre = columns(centre)[0:64, :]
    around = gram_ref[...] - col_local * apart + col_centre * (local - number * apart)
    around = exact(nn, around[:, 0:64], diag[0:64, 0:256])
    col_wide = jnp.concatenate([col_hidden, col_hidden], axis=1)
    expander = raw_ref[...] - col_wide * flat_here - around * tilt

    sums = (jnp.zeros((8, 128), F32), jnp.zeros((8, 128), F32))
    for g in range(pairs):
        mask = count_mask(count_ref, g, pairs)

        def inward(rows):
            hidden = hidden_ref[g, rows, :]
            mixed = nn(hidden, mix_both)
            mixed = mixed[:, 0:128] + mixed[:, 128:256]
            grad = slope_ref[g, rows, :] * (back_ref[g, rows, :] - mask * (base + mixed))
            normed = (second_ref[g, rows, :] - average_two) * inverse_two
            return scale2 * (grad - mask * ((bias2 + normed * gain2) / whole))

        def store(c, carry):
            rows = block(c * step, step)
            grad = inward(rows)
            here = pl.ds(pl.multiple_of(c * step + across, 8), step)
            grad_ref[here, :] = grad
            turned_ref[here, :] = swap(grad)
            rows = block(g * own + c * step, step)
            right_ref[rows, 0:128] = from_right(grad, high_ref[...]).astype(BF16)
            right_ref[rows, 128:256] = grad.astype(BF16)
            right_ref[rows, 256:384] = from_left(grad, low_ref[...]).astype(BF16)
            return carry

        lax.fori_loop(0, sizes.chunks, store, 0, unroll=True)
        edge = inward(pl.ds(own, step))
        for start, value in ((0, edge[0:across, :] * has_above), (own + across, edge[across:, :] * has_below)):
            grad_ref[start : start + across, :] = value
            turned_ref[start : start + across, :] = swap(value)

        starts = [slice(a * across, a * across + own) for a in range(3)]
        products, _ = taps_apart(
            [grad_ref[start, :] for start in starts], [turned_ref[start, :] for start in starts[0:2]], conv_back_ref
        )
        for c in range(sizes.chunks):
            rows = slice(c * step, (c + 1) * step)
            value = from_right(products[0][rows, :], high_ref[...]) + products[1][rows, :]
            value = value + from_left(products[2][rows, :], low_ref[...])
            grad = value * slope_one_ref[g, rows, :]
            grad_one_ref[g, rows, :] = grad
            normed = (first_ref[g, rows, :] - average_one) * inverse_one
            sums = sums[0] + folded(grad), sums[1] + folded(grad * normed)
    product = tn(window_ref[...].reshape(pairs * own, 384), right_ref[...])
    grad = grad_one_ref[...].reshape(pairs * own, 128).astype(BF16)
    reducer = tn_pair(grad, pair_rows(sizes, feat_ref))
    tops, tilts = total_of(sums[0]), total_of(sums[1])
    tops, tilts = tops + swap(tops), tilts + swap(tilts)
    sent = sizes.rows5
    clear(sizes, send_ref, sent, 4 + 8 * share)
    for slot, row in enumerate(pieces(jnp.where(row_low, tops, tilts))):
        put_row(send_ref, slot, sent, count, row.astype(F32))
    reducer = reducer - jnp.concatenate([columns(tops / number)[0:64, :]] * 2, axis=1) * sums_ref[...]
    slot = 3
    for matrix in (reducer, expander):
        for half in range(2):
            put_rows(send_ref, slot, sent, count, matrix[:, half * 128 : (half + 1) * 128])
            slot += share
    wide = low_lanes((64, 128))

    def tap(index):
        row, column = index // 3, (index % 3) * 128
        rows = (64 * row, 128 + 64 * row) if row < 2 else (256, 320)
        return [product[start : start + 64, column : column + 128] for start in rows]

    for pair in range(4):
        low, high = tap(2 * pair)
        even = low + swap(high)
        low, high = tap(2 * pair + 1)
        odd = swap(low) + high
        put_rows(send_ref, slot, sent, count, jnp.where(wide, even, odd))
        slot += share
    low, high = tap(8)
    even = low + swap(high)
    put_rows(send_ref, slot, sent, count, jnp.where(low_lanes((32, 128)), even[0:32, :], swap(even[32:64, :])))
    out_ref[...] = send_ref[...].astype(BF16)
    leave.wait()


def shares_kernel(
    sizes, got_ref, first_got_ref, second_got_ref, third_got_ref, norm_one_ref, gain_ref, grad_ref, first_ref,
    gsum_ref, weight_ref, real_ref,
    gain_out_ref, bias_out_ref, feature_ref, out_ref,
    send_ref, wide_ref,
):
    share, count, pairs, step, own = sizes.share, sizes.count, sizes.pairs, sizes.step, sizes.own
    slots = sizes.rows5
    wide_ref[...] = got_ref[...].astype(F32)
    total = jnp.sum(wide_ref[...].reshape(count // 2, 2 * slots, 128), axis=0)
    total = total[0:slots, :] + total[slots:, :]
    whole = norm_one_ref[2:3, :]
    average, inverse = norm_one_ref[0:1, :], norm_one_ref[1:2, :]
    sums = total[0:1, :] + (total[1:2, :] + total[2:3, :])
    bias, gain = low_both(sums), high_both(sums)
    bias_out_ref[...] = bias[:, 0:64]
    gain_out_ref[...] = gain[:, 0:64]
    scale = twice(gain_ref[...]) * inverse
    bias, gain = bias / whole, gain / whole
    for g in range(pairs):
        mask = pair_mask(real_ref, g)

        def body(c, carry):
            rows = block(c * step, step)
            normed = (first_ref[g, rows, :] - average) * inverse
            grad = (scale * (grad_ref[g, rows, :] - mask * (bias + normed * gain))).astype(BF16)
            for half in range(2):
                place = block((g + half * pairs) * own + c * step, step)
                value = nn(grad, weight_ref[:, half * 256 : (half + 1) * 256])
                feature_ref[half, g, rows, :] = (value + gsum_ref[place, :]).astype(BF16)
            return carry

        lax.fori_loop(0, sizes.chunks, body, 0, unroll=True)
    me = lax.axis_index("img") * lax.axis_size("ha") + lax.axis_index("ha")
    lane = lax.broadcasted_iota(jnp.int32, (1, 128), 1)
    sent = sizes.rows6
    local = wide_ref[pl.ds(0, count, stride=slots), :] + (
        wide_ref[pl.ds(1, count, stride=slots), :] + wide_ref[pl.ds(2, count, stride=slots), :]
    )
    local = jnp.where(low_lanes(local.shape), local, swap(local))
    local = local / first_got_ref[pl.ds(1, count, stride=sizes.rows1), :] - bias
    clear(sizes, send_ref, sent, 1 + 8 * share)
    rows = jnp.concatenate([local, scale, gain, jnp.zeros((6, 128), F32)], axis=0)
    picked = [
        jnp.sum(jnp.where(lane == me + part * count, rows, 0.0), axis=1, keepdims=True) for part in range(share)
    ]
    for index, (half, part) in enumerate(cross_rows(sizes)):
        place = 3 + half * share + part
        raw = total[place : place + 1, :]
        if index < sizes.cross_early:
            cross = get_sum(second_got_ref, 1 + index, sizes.rows2, count)
        else:
            cross = get_sum(third_got_ref, 4 + share + index - sizes.cross_early, sizes.rows3, count)
        features = first_got_ref[pl.ds(2 + half, count, stride=sizes.rows1), :]
        local, factor, tilt = [picked[part][a:b, :] for a, b in ((0, count), (count, count + 1), (count + 1, count + 2))]
        value = factor * (raw + total_of(local * features) - tilt * cross)
        put_row(send_ref, half * share + part, sent, count, value)
    for slot in range(2 * share, 8 * share + 1):
        place = 3 + slot
        put_row(send_ref, slot, sent, count, total[place : place + 1, :])
    out_ref[...] = send_ref[...].astype(BF16)


def weights_kernel(sizes, got_ref, redt_out_ref, expander_out_ref, spatial_out_ref, wide_ref):
    share, count = sizes.share, sizes.count
    slots = sizes.rows6
    wide_ref[...] = got_ref[...].astype(F32)
    for out_ref, slot in ((redt_out_ref, 0), (expander_out_ref, 2 * share)):
        for half in range(2):
            out_ref[:, half * 128 : (half + 1) * 128] = get_rows(wide_ref, slot + half * share, slots, count, 64)
    for index in range(8):
        value = get_rows(wide_ref, (4 + index // 2) * share, slots, count, 64)
        if index % 2:
            value = swap(value)
        spatial_out_ref[index * 64 : (index + 1) * 64, :] = value[:, 0:64]
    value = get_rows(wide_ref, 8 * share, slots, count, 32)
    spatial_out_ref[512:544, :] = value[:, 0:64]
    spatial_out_ref[544:576, :] = swap(value)[:, 0:64]


def exchange(rows, count):
    pack = 2 if rows.dtype == BF16 else 1
    parted = rows.reshape(count, rows.shape[0] // (count * pack), pack, 128)
    return lax.all_to_all(parted, AXES, 0, 0).reshape(rows.shape)


def on_device(
    features,
    reducer,
    spatial,
    expander,
    gain_reduce,
    bias_reduce,
    gain_spatial,
    bias_spatial,
    gain_expand,
    bias_expand,
    upstream,
    image_counts,
):
    images, height, across, wide = features.shape
    count = lax.axis_size("img") * lax.axis_size("ha")
    sizes = Sizes(images, height, across, count)
    pairs, own, step = sizes.pairs, sizes.own, sizes.step
    flat = (images * own, wide)
    deep = (2, pairs, own, wide)
    feat_hbm, up_hbm = features.reshape(deep), upstream.reshape(deep)
    taps = spatial.reshape(9 * 64, 64)
    gain1, bias1, gain2, bias2, gain3, bias3 = [
        value.reshape(1, value.shape[0])
        for value in (gain_reduce, bias_reduce, gain_spatial, bias_spatial, gain_expand, bias_expand)
    ]
    outside = pl.BlockSpec(memory_space=pltpu.HBM)
    inside = pl.BlockSpec(memory_space=pltpu.VMEM)

    def shape(*dims, dtype=F32):
        return jax.ShapeDtypeStruct(dims, dtype)

    def call(kernel, outs, args, scratch=(), away=(), far=()):
        specs = []
        for arg in args:
            if arg is image_counts:
                specs.append(pl.BlockSpec(memory_space=pltpu.SMEM))
            else:
                specs.append(outside if any(arg is other for other in far) else inside)
        return pl.pallas_call(
            functools.partial(kernel, sizes),
            out_shape=outs,
            in_specs=specs,
            out_specs=tuple(outside if index in away else inside for index in range(len(outs))),
            scratch_shapes=list(scratch),
            compiler_params=pltpu.CompilerParams(vmem_limit_bytes=VMEM_MIB << 20),
        )(*args)

    ha = lax.axis_size("ha")
    near = [(i, i ^ 1) for i in range(ha)]
    far = [(i, i + 1) for i in range(1, ha - 1, 2)]
    far = far + [(target, source) for source, target in far]
    masks = [pltpu.VMEM((step, 128), F32), pltpu.VMEM((step, 128), F32)]

    given = tuple(
        pltpu.with_memory_space_constraint(value, pltpu.HBM)
        for value in (feat_hbm, up_hbm, reducer.T)
    )
    weight, real, near_rows, far_rows = call(
        prepare_kernel,
        (
            shape(128, 512, dtype=BF16),
            shape(16, 256),
            shape(2, 2, pairs, step, wide, dtype=BF16),
            shape(2, 2, pairs, step, wide, dtype=BF16),
        ),
        (*given, image_counts),
        [pltpu.VMEM((64, 256), BF16), pltpu.SemaphoreType.DMA((5,))],
        far=given,
    )
    near_rows = lax.ppermute(near_rows, "ha", near)
    far_rows = lax.ppermute(far_rows, "ha", far)
    feat = feat_hbm
    first, sums, rows = call(
        reduce_kernel,
        (shape(pairs, own, 128), shape(1, 256), shape(count * sizes.rows1, 128)),
        (feat, weight, real),
    )
    got1 = exchange(rows, count)
    windows, slope_one, second, norm_one, cross, rows = call(
        conv_kernel,
        (
            shape(pairs, own, 384, dtype=BF16),
            shape(pairs, own, 128),
            shape(pairs, sizes.ext, 128),
            shape(8, 128),
            shape(64, 256),
            shape(count * sizes.rows2, 128),
        ),
        (got1, feat, first, near_rows, far_rows, weight, taps, gain1, bias1, real),
        [pltpu.VMEM((2, 256, 256), BF16)] + [pltpu.VMEM((pairs, sizes.wide1, 128), F32)] * 2 + [*masks, pltpu.VMEM((pairs * own, 128), BF16)],
    )
    got2 = exchange(rows, count)
    hidden_two, slope_two, norm_two, gram, expand, rows = call(
        middle_kernel,
        (
            shape(pairs, sizes.ext, 128, dtype=BF16),
            shape(pairs, sizes.ext, 128),
            shape(8, 128),
            shape(64, 128),
            shape(128, 512, dtype=BF16),
            shape(count * sizes.rows3, 128),
        ),
        (got2, got1, second, gain2, bias2, expander, cross, real),
        [pltpu.VMEM((pairs * own, 128), BF16), pltpu.VMEM((pairs * own, 384), BF16)],
    )
    got3 = exchange(rows, count)
    active, grad_sum, back, norm_three, raw, rows = call(
        output_kernel,
        (
            shape(*flat, dtype=BF16),
            shape(*flat),
            shape(pairs, sizes.ext, 128),
            shape(8, 256),
            shape(64, 256),
            shape(count * sizes.rows4, 128),
        ),
        (
            got3, norm_one, norm_two, hidden_two, slope_two, second, feat, up_hbm, near_rows, far_rows,
            gain3, bias3, expand, real,
        ),
        [pltpu.VMEM((pairs * sizes.ext, 2 * wide), BF16)],
    )
    got4 = exchange(rows, count)
    gradgain3, gradbias3, gradgain2, gradbias2, grad_one, activated, rows = call(
        backward_kernel,
        (
            shape(1, 256),
            shape(1, 256),
            shape(1, 64),
            shape(1, 64),
            shape(pairs, own, 128),
            shape(*flat, dtype=BF16),
            shape(count * sizes.rows5, 128, dtype=BF16),
        ),
        (
            got4, got3, norm_one, norm_two, norm_three, gram, windows, slope_one, first, hidden_two,
            slope_two, second, back, raw, feat, sums, gain2, expand, taps, active, image_counts,
        ),
        [pltpu.VMEM((2, 256, 256), BF16)]
        + [pltpu.VMEM((sizes.wide2, 128), F32)] * 2
        + masks
        + [
            pltpu.VMEM((pairs * own, 384), BF16),
            pltpu.VMEM((count * sizes.rows5, 128), F32),
            pltpu.SemaphoreType.DMA,
        ],
        away=(5,),
    )
    got5 = exchange(rows, count)
    gradgain1, gradbias1, feature_grad, rows = call(
        shares_kernel,
        (
            shape(1, 64),
            shape(1, 64),
            pltpu.VMEM(deep, BF16),
            shape(count * sizes.rows6, 128, dtype=BF16),
        ),
        (got5, got1, got2, got3, norm_one, gain1, grad_one, first, grad_sum, weight, real),
        [pltpu.VMEM((count * sizes.rows6, 128), F32), pltpu.VMEM((count * sizes.rows5, 128), F32)],
    )
    got6 = exchange(rows, count)
    redt_grad, expander_grad, spatial_grad = call(
        weights_kernel,
        (shape(64, 256), shape(64, 256), shape(9 * 64, 64)),
        (got6,),
        [pltpu.VMEM((count * sizes.rows6, 128), F32)],
    )
    return (
        activated.reshape(features.shape),
        feature_grad.reshape(features.shape),
        redt_grad.T,
        spatial_grad.reshape(spatial.shape),
        expander_grad,
        gradgain1.reshape(64),
        gradbias1.reshape(64),
        gradgain2.reshape(64),
        gradbias2.reshape(64),
        gradgain3.reshape(256),
        gradbias3.reshape(256),
    )


def solution(mesh):
    whole = P("img", "ha", None, None)
    in_specs = (whole,) + (P(),) * 9 + (whole, P("img"))
    out_specs = (whole, whole) + (P(),) * 9
    return jax.shard_map(
        on_device, mesh=mesh, in_specs=in_specs, out_specs=out_specs, check_vma=False
    )
```

```python
import functools

import jax
import jax.numpy as jnp
from jax import lax
from jax.experimental import pallas as pl
from jax.experimental.pallas import tpu as pltpu
from jax.sharding import PartitionSpec as P

EPSILON = 1e-05
AXES = ("img", "ha")
F32 = jnp.float32
BF16 = jnp.bfloat16
VMEM_MIB = 16


def nn(left, right):
    return lax.dot_general(left, right, (((1,), (0,)), ((), ())), preferred_element_type=F32)


def nt(left, right):
    return lax.dot_general(left, right, (((1,), (1,)), ((), ())), preferred_element_type=F32)


def tn(left, right):
    return lax.dot_general(left, right, (((0,), (0,)), ((), ())), preferred_element_type=F32)


def pair_rows(sizes, ref):
    return jnp.concatenate([ref[half].reshape(sizes.pairs * sizes.own, 256) for half in range(2)], axis=1)


def tn_pair(left, right):
    product = tn(left, right)
    return product[0:64, 0:256] + product[64:128, 256:512]


def pieces(values):
    high = values.astype(BF16)
    rest = values - high.astype(F32)
    middle = rest.astype(BF16)
    low = (rest - middle.astype(F32)).astype(BF16)
    return high, middle, low


def exact(product, values, weights):
    high, middle, _ = pieces(values)
    return product(high, weights) + product(middle, weights)


def exact_rows(product, rows, weights):
    parts = [part for row in rows for part in pieces(row)]
    parts = parts + [jnp.zeros_like(parts[0])] * (-len(parts) % 8)
    result = product(jnp.concatenate([part.astype(F32) for part in parts], axis=0).astype(BF16), weights)
    return [total_of(result[3 * index : 3 * index + 3, :]) for index in range(len(rows))]


def folded(values):
    return jnp.sum(values.reshape(values.shape[0] // 8, 8, values.shape[1]), axis=0)


def total_of(values):
    return jnp.sum(values, axis=0, keepdims=True)


def swap(values):
    return pltpu.roll(values, 64, axis=1)


def low_lanes(shape):
    return lax.broadcasted_iota(jnp.int32, shape, 1) < 64


def low_both(row):
    return jnp.where(low_lanes(row.shape), row, swap(row))


def high_both(row):
    return jnp.where(low_lanes(row.shape), swap(row), row)


def twice(row):
    place = lax.broadcasted_iota(jnp.int32, (64, 128), 0)
    lane = lax.rem(lax.broadcasted_iota(jnp.int32, (64, 128), 1), 64)
    return exact_rows(nn, [row], (place == lane).astype(BF16))[0]


def swish(values):
    half = 0.5 * values
    turn = jnp.tanh(half)
    plus = 1.0 + turn
    value = half * plus
    return value, 0.5 * (plus + value * (1.0 - turn))


def fill_real(sizes, out_ref, count):
    count = jnp.zeros((1, 256), F32) + count.astype(F32)
    low = lax.rem(lax.broadcasted_iota(jnp.int32, (1, 256), 1), 128) < 64
    images = [(float(image) < count).astype(F32) for image in range(sizes.images)]
    rows = [jnp.where(low, images[g], images[g + sizes.pairs]) for g in range(sizes.pairs)] + images
    rows = rows + [jnp.zeros((1, 256), F32)] * (15 - len(rows)) + [count * sizes.pixels]
    out_ref[...] = jnp.concatenate(rows, axis=0)


def pair_mask(real_ref, g):
    return real_ref[g : g + 1, 0:128]


def count_mask(count_ref, g, pairs):
    count = count_ref[0]
    low = (g < count).astype(F32)
    high = (g + pairs < count).astype(F32)
    return jnp.where(low_lanes((1, 128)), low, high)


def image_mask(sizes, real_ref, image):
    return real_ref[sizes.pairs + image : sizes.pairs + image + 1, :]


def real_pixels(real_ref):
    return real_ref[15:16, 0:128]


def columns(row):
    return jnp.transpose(jnp.broadcast_to(row, (128, 128)))


def put_row(out_ref, slot, slots, count, row):
    out_ref[pl.ds(slot, count, stride=slots), :] = jnp.broadcast_to(row, (count, 128))


def put_rows(out_ref, slot, slots, count, matrix):
    rows = min(count, matrix.shape[0])
    for part in range(matrix.shape[0] // rows):
        out_ref[pl.ds(slot + part, rows, stride=slots), :] = matrix[part * rows : (part + 1) * rows, :]


def get_sum(got_ref, slot, slots, count):
    return total_of(got_ref[pl.ds(slot, count, stride=slots), :])


def get_rows(got_ref, slot, slots, count, height):
    rows = min(count, height)
    parts = [got_ref[pl.ds(slot + part, rows, stride=slots), :] for part in range(height // rows)]
    return parts[0] if len(parts) == 1 else jnp.concatenate(parts, axis=0)


def clear(sizes, out_ref, slots, used):
    if sizes.count > 64:
        out_ref[...] = jnp.zeros(out_ref.shape, F32)
    else:
        for slot in range(used, slots):
            put_row(out_ref, slot, slots, sizes.count, jnp.zeros((1, 128), F32))


class Sizes:
    def __init__(self, images, height, across, count):
        self.images, self.height, self.across, self.count = images, height, across, count
        self.pairs = images // 2
        self.own = height * across
        self.pixels = float(height * across)
        self.step = 2 * across
        self.chunks = height // 2
        self.ext = self.own + self.step
        self.sample = 32
        self.edge = -(-across // 16) * 16
        self.wide1 = (height + 4) * across
        self.wide2 = (height + 2) * across
        self.share = max(1, 64 // count)
        self.rows1 = 4
        self.cross_early = min(3, 2 * self.share)
        self.cross_late = 2 * self.share - self.cross_early
        self.rows2 = 4
        self.rows3 = 4 + self.share + self.cross_late
        self.rows4 = 5 + self.share
        self.rows5 = -(-(4 + 8 * self.share) // 4) * 4
        self.rows6 = -(-(1 + 8 * self.share) // 2) * 2


def block(start, size):
    return pl.ds(pl.multiple_of(start, size), size)


def diagonal(out_ref, weight):
    out_ref[...] = jnp.zeros(out_ref.shape, out_ref.dtype)
    out_ref[0:64, 0:256] = weight
    out_ref[64:128, 256:512] = weight


def edge_masks(sizes, low_ref, high_ref):
    column = lax.rem(lax.broadcasted_iota(jnp.int32, (sizes.step, 128), 0), sizes.across)
    low_ref[...] = (column > 0).astype(F32)
    high_ref[...] = (column < sizes.across - 1).astype(F32)


def all_taps(out_ref, taps_ref, back):
    out_ref[...] = jnp.zeros(out_ref.shape, BF16)
    for vertical in range(3):
        for lateral in range(3):
            tap = taps_ref[(vertical * 3 + lateral) * 64 : (vertical * 3 + lateral + 1) * 64, :]
            if back:
                place_taps(out_ref, 2 - vertical, lateral, jnp.transpose(tap))
            else:
                place_taps(out_ref, vertical, lateral, tap)


def place_taps(out_ref, vertical, lateral, tap):
    for half in range(2):
        row = vertical * 64 if vertical < 2 else 128 + 64 * half
        column = 128 + 64 * half if lateral == 1 else 64 * ((lateral // 2 + half) % 2)
        out_ref[half, row : row + 64, column : column + 64] = tap


def taps_apart(windows, swapped, weight_ref):
    low = low_lanes(windows[0].shape)
    pair_low = jnp.where(low, windows[0], swapped[1]).astype(BF16)
    pair_high = jnp.where(low, swapped[0], windows[1]).astype(BF16)
    last = windows[2].astype(BF16)
    one = nn(jnp.concatenate([pair_low, last], axis=1), weight_ref[0])
    two = nn(jnp.concatenate([pair_high, last], axis=1), weight_ref[1])
    products = (
        jnp.where(low, one[:, 0:128], two[:, 0:128]),
        one[:, 128:256] + two[:, 128:256],
        swap(jnp.where(low, two[:, 0:128], one[:, 0:128])),
    )
    return products, jnp.concatenate([pair_low, pair_high, last], axis=1)


def from_left(values, low):
    return pltpu.roll(values, 1, axis=0) * low


def from_right(values, high):
    return pltpu.roll(values, values.shape[0] - 1, axis=0) * high


class Stats:
    def __init__(self, real_ref):
        self.real_ref = real_ref
        self.number = real_pixels(real_ref)
        self.near = None
        self.part = [jnp.zeros((8, 128), F32)] * 2
        self.whole = [jnp.zeros((8, 128), F32)] * 2

    def add(self, value):
        if self.near is None:
            self.near = low_both(total_of(value) / float(value.shape[0]))
        apart = value - self.near
        self.part = [self.part[0] + folded(apart), self.part[1] + folded(apart * apart)]

    def close(self, g):
        mask = pair_mask(self.real_ref, g)
        self.whole = [whole + part * mask for whole, part in zip(self.whole, self.part)]
        self.part = [jnp.zeros((8, 128), F32)] * 2

    def row(self):
        total, square = [total_of(value) for value in self.whole]
        total, square = total + swap(total), square + swap(square)
        square = square - total * total / self.number
        return jnp.where(low_lanes((1, 128)), total + self.number * self.near, square)


def prepare_kernel(
    sizes, feat_hbm, up_hbm, redt_hbm, count_ref, weight_ref, real_ref, near_ref, far_ref, redt_ref, sem_ref,
):
    step, own = sizes.step, sizes.own
    edges = []
    odd = lax.rem(lax.axis_index("ha"), 2)
    edge = sizes.edge
    for out, last in ((near_ref, 1 - odd), (far_ref, odd)):
        for source, size, place in ((feat_hbm, step, 0), (up_hbm, edge, step)):
            start = pl.multiple_of(last * (own - size), 16)
            copy = pltpu.make_async_copy(
                source.at[:, :, pl.ds(start, size), :], out.at[:, :, pl.ds(place, size), :], sem_ref.at[len(edges)]
            )
            copy.start()
            edges.append(copy)
    small = pltpu.make_async_copy(redt_hbm, redt_ref, sem_ref.at[4])
    small.start()
    fill_real(sizes, real_ref, count_ref[0])
    small.wait()
    diagonal(weight_ref, redt_ref[...])
    for copy in edges:
        copy.wait()


def reduce_kernel(sizes, feat_ref, weight_ref, real_ref, first_ref, sums_ref, out_ref):
    pairs, step = sizes.pairs, sizes.step
    stats = Stats(real_ref)
    feats = jnp.zeros((8, 256), F32)
    for g in range(pairs):
        low_sum = high_sum = jnp.zeros((8, 256), F32)
        for c in range(sizes.chunks):
            low = feat_ref[0, g, c * step : (c + 1) * step, :]
            high = feat_ref[1, g, c * step : (c + 1) * step, :]
            value = nt(jnp.concatenate([low, high], axis=1), weight_ref[...])
            first_ref[g, c * step : (c + 1) * step, :] = value
            stats.add(value)
            low_sum = low_sum + folded(low.astype(F32))
            high_sum = high_sum + folded(high.astype(F32))
        stats.close(g)
        feats = feats + low_sum * image_mask(sizes, real_ref, g)
        feats = feats + high_sum * image_mask(sizes, real_ref, g + pairs)
    feats = total_of(feats)
    sums_ref[...] = feats
    slots, count = sizes.rows1, sizes.count
    put_row(out_ref, 0, slots, count, stats.row())
    put_row(out_ref, 1, slots, count, stats.number)
    put_row(out_ref, 2, slots, count, feats[:, 0:128])
    put_row(out_ref, 3, slots, count, feats[:, 128:256])


def merged(sizes, got_ref, slots, numbers):
    rows = got_ref[pl.ds(0, sizes.count, stride=slots), :]
    whole = total_of(numbers)
    low = low_lanes(rows.shape)
    both = jnp.where(low, rows, swap(rows))
    average = total_of(both) / whole
    apart = both / numbers - average
    squares = jnp.where(low, swap(rows), rows)
    variance = total_of(squares + numbers * apart * apart) / whole
    return average, lax.rsqrt(variance + EPSILON), whole


def conv_kernel(
    sizes, got_ref, feat_ref, first_ref, near_ref, far_ref, weight_ref, taps_ref, gain_ref, bias_ref, real_ref,
    window_ref, slope_ref, second_ref, norm_ref, cross_ref, out_ref, conv_ref, hidden_ref, turned_ref, low_ref, high_ref, normed_ref,
):
    pairs, step, own, across = sizes.pairs, sizes.step, sizes.own, sizes.across
    numbers = got_ref[pl.ds(1, sizes.count, stride=sizes.rows1), :]
    average, inverse, whole = merged(sizes, got_ref, sizes.rows1, numbers)
    norm_ref[...] = jnp.concatenate([average, inverse, whole, jnp.zeros((5, 128), F32)], axis=0)
    gain, bias = twice(gain_ref[...]), twice(bias_ref[...])
    place = lax.axis_index("ha")
    odd = lax.rem(place, 2)
    has_far = jnp.logical_and(place > 0, place < lax.axis_size("ha") - 1).astype(F32)
    near_start = pl.multiple_of((1 - odd) * (own + step), step)
    far_start = pl.multiple_of(odd * (own + step), step)
    edge_masks(sizes, low_ref, high_ref)
    all_taps(conv_ref, taps_ref, False)
    for g in range(pairs):
        mask = pair_mask(real_ref, g)

        def activate(c, carry):
            normed = (first_ref[g, block(c * step, step), :] - average) * inverse
            value, slope = swish(normed * gain + bias)
            hidden_ref[g, block((c + 1) * step, step), :] = value
            turned_ref[g, block((c + 1) * step, step), :] = swap(value)
            slope_ref[g, block(c * step, step), :] = slope
            normed_ref[block(g * own + c * step, step), :] = (normed * mask).astype(BF16)
            return carry

        lax.fori_loop(0, sizes.chunks, activate, 0, unroll=True)
        for start, valid, rows_ref in ((near_start, 1.0, near_ref), (far_start, has_far, far_ref)):
            low, high = rows_ref[0, g, 0:step, :], rows_ref[1, g, 0:step, :]
            first = nt(jnp.concatenate([low, high], axis=1), weight_ref[...])
            value, _ = swish((first - average) * inverse * gain + bias)
            value = value * valid
            hidden_ref[g, pl.ds(start, step), :] = value
            turned_ref[g, pl.ds(start, step), :] = swap(value)
    cross = tn_pair(normed_ref[...], pair_rows(sizes, feat_ref))
    cross_ref[...] = cross

    def together(products):
        return from_left(products[0], low_ref[...]) + products[1] + from_right(products[2], high_ref[...])

    total = jnp.zeros((8, 128), F32)
    for g in range(pairs):
        part = jnp.zeros((8, 128), F32)
        starts = [slice((a + 1) * across, (a + 1) * across + own) for a in range(3)]
        products, window_ref[g] = taps_apart(
            *[[ref[g, start, :] for start in starts] for ref in (hidden_ref, turned_ref)], conv_ref
        )
        for c in range(sizes.chunks):
            rows = slice(c * step, (c + 1) * step)
            value = together([product[rows, :] for product in products])
            second_ref[g, rows, :] = value
            part = part + folded(value)
        total = total + part * pair_mask(real_ref, g)
        last = sizes.height + 1
        windows, swapped = [
            [
                jnp.concatenate(
                    [
                        ref[g, a * across : (a + 1) * across, :],
                        ref[g, (last + a) * across : (last + a + 1) * across, :],
                    ],
                    axis=0,
                )
                for a in range(3)
            ]
            for ref in (hidden_ref, turned_ref)
        ]
        products, _ = taps_apart(windows, swapped, conv_ref)
        second_ref[g, own : own + step, :] = together(products)
    total = total_of(total)
    total = total + swap(total)
    local = total / (real_pixels(real_ref))
    square = jnp.zeros((8, 128), F32)
    for g in range(pairs):
        part = jnp.zeros((8, 128), F32)
        for c in range(sizes.chunks):
            apart = second_ref[g, c * step : (c + 1) * step, :] - local
            part = part + folded(apart * apart)
        square = square + part * pair_mask(real_ref, g)
    square = total_of(square)
    square = square + swap(square)
    slots = sizes.rows2
    put_row(out_ref, 0, slots, sizes.count, jnp.where(low_lanes((1, 128)), total, square))
    put_cross(sizes, out_ref, 1, slots, cross, 0, sizes.cross_early)


def cross_rows(sizes):
    return [(half, part) for half in range(2) for part in range(sizes.share)]


def put_cross(sizes, out_ref, slot, slots, cross, start, stop):
    rows = min(sizes.count, 64)
    for index, (half, part) in enumerate(cross_rows(sizes)[start:stop]):
        matrix = cross[part * rows : (part + 1) * rows, half * 128 : (half + 1) * 128]
        out_ref[pl.ds(slot + index, rows, stride=slots), :] = matrix


def middle_kernel(
    sizes, got_ref, first_got_ref, second_ref, gain_ref, bias_ref, expander_ref, cross_ref, real_ref,
    hidden_ref, slope_ref, norm_ref, gram_ref, expand_ref, out_ref, left_ref, right_ref,
):
    pairs, step, own = sizes.pairs, sizes.step, sizes.own
    slots = sizes.rows3
    numbers = first_got_ref[pl.ds(1, sizes.count, stride=sizes.rows1), :]
    average, inverse, _ = merged(sizes, got_ref, sizes.rows2, numbers)
    gain, bias = twice(gain_ref[...]), twice(bias_ref[...])
    centre, tangent = swish(bias)
    centre = 0.125 * jnp.floor(8.0 * centre + 0.5)
    diagonal(expand_ref, expander_ref[...])
    sums = (jnp.zeros((8, 128), F32),) * 3
    for g in range(pairs):
        mask = pair_mask(real_ref, g)

        def activate(c, acc):
            rows = block(c * step, step)
            normed = (second_ref[g, rows, :] - average) * inverse
            value, slope = swish(normed * gain + bias)
            rounded = value.astype(BF16)
            hidden_ref[g, rows, :] = rounded
            slope_ref[g, rows, :] = slope
            apart = (rounded.astype(F32) - centre) * mask
            slope = slope * mask
            tilted = slope * normed
            rows = block(g * own + c * step, step)
            left_ref[rows, :] = apart.astype(BF16)
            right_ref[rows, 0:128] = apart.astype(BF16)
            right_ref[rows, 128:256] = (slope - tangent).astype(BF16)
            right_ref[rows, 256:384] = tilted.astype(BF16)
            return acc[0] + folded(apart), acc[1] + folded(slope), acc[2] + folded(tilted)

        sums = lax.fori_loop(0, sizes.chunks, activate, sums, unroll=True)
        value, slope = swish((second_ref[g, own : own + step, :] - average) * inverse * gain + bias)
        hidden_ref[g, own : own + step, :] = value.astype(BF16)
        slope_ref[g, own : own + step, :] = slope
    product = tn(left_ref[...], right_ref[...])
    apart, slope, tilted = [total_of(value) for value in sums]
    apart, slope, tilted = apart + swap(apart), slope + swap(slope), tilted + swap(tilted)
    low, high = product[0:64, :], product[64:128, :]
    gram = low[:, 0:128] + swap(high[:, 0:128])
    slopes = low[:, 128:256] + swap(high[:, 128:256])
    tilts = swap(low[:, 256:384]) + high[:, 256:384]
    wide = low_lanes((64, 128))
    slopes = slopes + columns(apart)[0:64, :] * tangent
    gram = jnp.where(wide, gram, 0.0)
    gram_ref[...] = gram
    weights = expander_ref[...]
    quad = total_of(exact(nn, gram[:, 0:64], weights) * weights.astype(F32))
    norm_ref[...] = jnp.concatenate(
        [average, inverse, centre, apart, jnp.where(low_lanes((1, 128)), slope, tilted), jnp.zeros((3, 128), F32)],
        axis=0,
    )
    put_row(out_ref, 0, slots, sizes.count, quad[:, 0:128])
    put_row(out_ref, 1, slots, sizes.count, quad[:, 128:256])
    put_row(out_ref, 2, slots, sizes.count, apart)
    put_row(out_ref, 3, slots, sizes.count, jnp.where(low_lanes((1, 128)), slope, tilted))
    put_rows(out_ref, 4, slots, sizes.count, jnp.where(wide, slopes, tilts))
    put_cross(sizes, out_ref, 4 + sizes.share, slots, cross_ref[...], sizes.cross_early, 2 * sizes.share)


def output_kernel(
    sizes, got_ref, norm_one_ref, norm_ref, hidden_ref, slope_ref, second_ref, feat_ref, up_ref,
    near_ref, far_ref, gain_ref, bias_ref, expand_ref, real_ref,
    active_ref, gsum_ref, back_ref, last_ref, raw_ref, out_ref, scaled_ref, third_ref,
):
    pairs, step, own, across = sizes.pairs, sizes.step, sizes.own, sizes.across
    odd = lax.rem(lax.axis_index("ha"), 2) == 1
    slots, count = sizes.rows3, sizes.count
    whole = norm_one_ref[2:3, :]
    centre = norm_ref[2:3, :]
    apart = get_sum(got_ref, 2, slots, count) / whole
    mean_hidden = centre + apart
    column = expand_ref[:, 0:256]
    shift, average = exact_rows(nn, [apart, mean_hidden], column)
    quad = jnp.concatenate([get_sum(got_ref, 0, slots, count), get_sum(got_ref, 1, slots, count)], axis=1)
    wide = jnp.concatenate([whole, whole], axis=1)
    inverse = lax.rsqrt(quad / wide - shift * shift + EPSILON)
    gain, bias = gain_ref[...], bias_ref[...]
    scale = gain * inverse
    offset = bias - average * scale
    average_two, inverse_two = norm_ref[0:1, :], norm_ref[1:2, :]

    def outward(third, feat):
        half_sum = 0.5 * (third * scale + offset + feat)
        turn = jnp.tanh(half_sum)
        plus = 1.0 + turn
        value = half_sum * plus
        return value, plus + value * (1.0 - turn)

    sample = slice(0, sizes.sample)
    _, slope = outward(nn(hidden_ref[0, sample, :], column), feat_ref[0, 0, sample, :].astype(F32))
    middle = 0.5 * total_of(up_ref[0, 0, sample, :].astype(F32) * slope) / float(sizes.sample)
    flat = scale * middle
    (flat_back,) = exact_rows(nt, [flat], expand_ref[:, 0:256] + expand_ref[:, 256:512])
    last_ref[...] = jnp.concatenate(
        [average, inverse, scale, jnp.concatenate([mean_hidden, apart], axis=1), middle, flat, shift, jnp.zeros((1, 256), F32)],
        axis=0,
    )
    biases = jnp.zeros((8, 256), F32)
    for g in range(pairs):
        valids = [image_mask(sizes, real_ref, g + half * pairs) for half in range(2)]
        middles = [middle * valid for valid in valids]

        third_ref[g * own : (g + 1) * own, :] = nn(hidden_ref[g, 0:own, :], expand_ref[...])

        def body(c, biases):
            for half in range(2):
                image = g + half * pairs
                third = third_ref[block(g * own + c * step, step), half * 256 : (half + 1) * 256]
                for start in range(0, step, 16):
                    here = pl.ds(pl.multiple_of(c * step + start, 16), 16)
                    place = pl.ds(pl.multiple_of(image * own + c * step + start, 16), 16)
                    value, slope = outward(third[start : start + 16, :], feat_ref[half, g, here, :].astype(F32))
                    active_ref[place, :] = value.astype(BF16)
                    grad = up_ref[half, g, here, :].astype(F32) * (0.5 * valids[half]) * slope
                    gsum_ref[place, :] = grad
                    grad = grad - middles[half]
                    biases = biases + folded(grad)
                    there = pl.ds(pl.multiple_of(g * own + c * step + start, 16), 16)
                    scaled_ref[there, half * 256 : (half + 1) * 256] = (grad * scale).astype(BF16)
            return biases

        biases = lax.fori_loop(0, sizes.chunks, body, biases, unroll=True)
        hidden = hidden_ref[g, own : own + step, :]
        edge = pairs * own + g * step
        for half in range(2):
            image = g + half * pairs
            both = []
            for start, size in ((0, step), (step, sizes.edge)):
                near = near_ref[half, g, start : start + size, :].astype(F32)
                far = far_ref[half, g, start : start + size, :].astype(F32)
                upper = jnp.where(odd, near[size - across :, :], far[size - across :, :])
                lower = jnp.where(odd, far[0:across, :], near[0:across, :])
                both.append(jnp.concatenate([upper, lower], axis=0))
            _, slope = outward(nn(hidden, expand_ref[:, half * 256 : (half + 1) * 256]), both[0])
            grad = both[1] * (0.5 * valids[half]) * slope
            scaled = ((grad - middles[half]) * scale).astype(BF16)
            scaled_ref[edge : edge + step, half * 256 : (half + 1) * 256] = scaled
    tops = tilts = jnp.zeros((8, 128), F32)
    backs = nt(scaled_ref[...], expand_ref[...])
    for g in range(pairs):
        back = backs[g * own : (g + 1) * own, :]
        back_ref[g, 0:own, :] = back
        top = slope_ref[g, 0:own, :] * back
        normed_two = (second_ref[g, 0:own, :] - average_two) * inverse_two
        tops, tilts = tops + folded(top), tilts + folded(top * normed_two)
        edge = pairs * own + g * step
        back_ref[g, own : own + step, :] = backs[edge : edge + step, :]
    raw = tn_pair(hidden_ref[:, 0:own, :].reshape(pairs * own, 128), scaled_ref[0 : pairs * own, :])
    raw_ref[...] = raw
    biases, tops, tilts = [total_of(value) for value in (biases, tops, tilts)]
    gains = total_of(raw * expand_ref[0:64, 0:256].astype(F32)) / scale - average * biases
    number = real_pixels(real_ref)
    (third_sum,) = exact_rows(nn, [norm_ref[3:4, :] - number * apart], column)
    gains = inverse * (gains + middle * third_sum)
    biases = biases + number[:, 0:1] * middle
    tops, tilts = tops + swap(tops), tilts + swap(tilts)
    tops = jnp.where(low_lanes((1, 128)), tops, tilts) + norm_ref[4:5, :] * flat_back
    sent = sizes.rows4
    put_row(out_ref, 0, sent, count, biases[:, 0:128])
    put_row(out_ref, 1, sent, count, biases[:, 128:256])
    put_row(out_ref, 2, sent, count, gains[:, 0:128])
    put_row(out_ref, 3, sent, count, gains[:, 128:256])
    put_row(out_ref, 4, sent, count, tops)
    for part in range(sizes.share):
        put_row(out_ref, 5 + part, sent, count, get_sum(got_ref, 4 + part, slots, count))


def backward_kernel(
    sizes, got_ref, third_got_ref, norm_one_ref, norm_ref, last_ref, gram_ref, window_ref, slope_one_ref,
    first_ref, hidden_ref, slope_ref, second_ref, back_ref, raw_ref, feat_ref, sums_ref, gain_two_ref, expand_ref,
    taps_ref, active_ref, count_ref,
    gain3_out_ref, bias3_out_ref, gain2_out_ref, bias2_out_ref, grad_one_ref, active_hbm, out_ref,
    conv_back_ref, grad_ref, turned_ref, low_ref, high_ref, right_ref, send_ref, sem_ref,
):
    pairs, step, own, across = sizes.pairs, sizes.step, sizes.own, sizes.across
    leave = pltpu.make_async_copy(active_ref, active_hbm, sem_ref)
    leave.start()
    share, count = sizes.share, sizes.count
    third_slots, slots = sizes.rows3, sizes.rows4
    whole = norm_one_ref[2:3, :]
    whole_wide = jnp.concatenate([whole, whole], axis=1)
    bias3 = jnp.concatenate([get_sum(got_ref, 0, slots, count), get_sum(got_ref, 1, slots, count)], axis=1)
    gain3 = jnp.concatenate([get_sum(got_ref, 2, slots, count), get_sum(got_ref, 3, slots, count)], axis=1)
    bias3_out_ref[...] = bias3
    gain3_out_ref[...] = gain3
    inverse3, scale3 = last_ref[1:2, :], last_ref[2:3, :]
    mean_hidden, apart = last_ref[3:4, 0:128], last_ref[3:4, 128:256]
    flat = scale3 * bias3 / whole_wide
    tilt = scale3 * inverse3 * gain3 / whole_wide
    diag = expand_ref[...]
    stacked = diag[:, 0:256] + diag[:, 256:512]
    flat_here = flat - last_ref[5:6, :]
    flat_back, flat_here_back, mean_mix, apart_mix = exact_rows(
        nt, [flat, flat_here, last_ref[0:1, :] * tilt, last_ref[6:7, :] * tilt], stacked
    )
    tilt_wide = jnp.concatenate([tilt, tilt], axis=1)
    mixing = exact(nt, diag.astype(F32) * tilt_wide, diag)
    mix_high, mix_low, _ = pieces(mixing)
    mix_both = jnp.concatenate([mix_high, mix_low], axis=1)
    row_low = low_lanes((1, 128))
    slopes = get_sum(third_got_ref, 3, third_slots, count)
    cross = get_rows(got_ref, 5, slots, count, 64)
    mixed = total_of((mixing[0:64, :] + mixing[64:128, :]) * cross)
    sums = get_sum(got_ref, 4, slots, count) - (slopes * (flat_back - apart_mix) + mixed)
    bias2, gain2 = low_both(sums), high_both(sums)
    bias2_out_ref[...] = bias2[:, 0:64]
    gain2_out_ref[...] = gain2[:, 0:64]
    average_two, inverse_two, centre = norm_ref[0:1, :], norm_ref[1:2, :], norm_ref[2:3, :]
    scale2 = twice(gain_two_ref[...]) * inverse_two
    base = flat_here_back - mean_mix
    place = lax.axis_index("ha")
    has_above = (place > 0).astype(F32)
    has_below = (place < lax.axis_size("ha") - 1).astype(F32)
    edge_masks(sizes, low_ref, high_ref)
    all_taps(conv_back_ref, taps_ref, True)
    average_one, inverse_one = norm_one_ref[0:1, :], norm_one_ref[1:2, :]

    local = norm_ref[3:4, :]
    number = count_ref[0].astype(F32) * sizes.pixels
    col_hidden = columns(local + number * centre)[0:64, :]
    col_local = columns(local)[0:64, :]
    col_centre = columns(centre)[0:64, :]
    around = gram_ref[...] - col_local * apart + col_centre * (local - number * apart)
    around = exact(nn, around[:, 0:64], diag[0:64, 0:256])
    col_wide = jnp.concatenate([col_hidden, col_hidden], axis=1)
    expander = raw_ref[...] - col_wide * flat_here - around * tilt

    sums = (jnp.zeros((8, 128), F32), jnp.zeros((8, 128), F32))
    for g in range(pairs):
        mask = count_mask(count_ref, g, pairs)

        def inward(rows):
            hidden = hidden_ref[g, rows, :]
            mixed = nn(hidden, mix_both)
            mixed = mixed[:, 0:128] + mixed[:, 128:256]
            grad = slope_ref[g, rows, :] * (back_ref[g, rows, :] - mask * (base + mixed))
            normed = (second_ref[g, rows, :] - average_two) * inverse_two
            return scale2 * (grad - mask * ((bias2 + normed * gain2) / whole))

        def store(c, carry):
            rows = block(c * step, step)
            grad = inward(rows)
            here = pl.ds(pl.multiple_of(c * step + across, 8), step)
            grad_ref[here, :] = grad
            turned_ref[here, :] = swap(grad)
            rows = block(g * own + c * step, step)
            right_ref[rows, 0:128] = from_right(grad, high_ref[...]).astype(BF16)
            right_ref[rows, 128:256] = grad.astype(BF16)
            right_ref[rows, 256:384] = from_left(grad, low_ref[...]).astype(BF16)
            return carry

        lax.fori_loop(0, sizes.chunks, store, 0, unroll=True)
        edge = inward(pl.ds(own, step))
        for start, value in ((0, edge[0:across, :] * has_above), (own + across, edge[across:, :] * has_below)):
            grad_ref[start : start + across, :] = value
            turned_ref[start : start + across, :] = swap(value)

        starts = [slice(a * across, a * across + own) for a in range(3)]
        products, _ = taps_apart(
            [grad_ref[start, :] for start in starts], [turned_ref[start, :] for start in starts[0:2]], conv_back_ref
        )
        for c in range(sizes.chunks):
            rows = slice(c * step, (c + 1) * step)
            value = from_right(products[0][rows, :], high_ref[...]) + products[1][rows, :]
            value = value + from_left(products[2][rows, :], low_ref[...])
            grad = value * slope_one_ref[g, rows, :]
            grad_one_ref[g, rows, :] = grad
            normed = (first_ref[g, rows, :] - average_one) * inverse_one
            sums = sums[0] + folded(grad), sums[1] + folded(grad * normed)
    product = tn(window_ref[...].reshape(pairs * own, 384), right_ref[...])
    grad = grad_one_ref[...].reshape(pairs * own, 128).astype(BF16)
    reducer = tn_pair(grad, pair_rows(sizes, feat_ref))
    tops, tilts = total_of(sums[0]), total_of(sums[1])
    tops, tilts = tops + swap(tops), tilts + swap(tilts)
    sent = sizes.rows5
    clear(sizes, send_ref, sent, 4 + 8 * share)
    for slot, row in enumerate(pieces(jnp.where(row_low, tops, tilts))):
        put_row(send_ref, slot, sent, count, row.astype(F32))
    reducer = reducer - jnp.concatenate([columns(tops / number)[0:64, :]] * 2, axis=1) * sums_ref[...]
    slot = 3
    for matrix in (reducer, expander):
        for half in range(2):
            put_rows(send_ref, slot, sent, count, matrix[:, half * 128 : (half + 1) * 128])
            slot += share
    wide = low_lanes((64, 128))

    def tap(index):
        row, column = index // 3, (index % 3) * 128
        rows = (64 * row, 128 + 64 * row) if row < 2 else (256, 320)
        return [product[start : start + 64, column : column + 128] for start in rows]

    for pair in range(4):
        low, high = tap(2 * pair)
        even = low + swap(high)
        low, high = tap(2 * pair + 1)
        odd = swap(low) + high
        put_rows(send_ref, slot, sent, count, jnp.where(wide, even, odd))
        slot += share
    low, high = tap(8)
    even = low + swap(high)
    put_rows(send_ref, slot, sent, count, jnp.where(low_lanes((32, 128)), even[0:32, :], swap(even[32:64, :])))
    out_ref[...] = send_ref[...].astype(BF16)
    leave.wait()


def shares_kernel(
    sizes, got_ref, first_got_ref, second_got_ref, third_got_ref, norm_one_ref, gain_ref, grad_ref, first_ref,
    gsum_ref, weight_ref, real_ref,
    gain_out_ref, bias_out_ref, feature_ref, out_ref,
    send_ref, wide_ref,
):
    share, count, pairs, step, own = sizes.share, sizes.count, sizes.pairs, sizes.step, sizes.own
    slots = sizes.rows5
    wide_ref[...] = got_ref[...].astype(F32)
    total = jnp.sum(wide_ref[...].reshape(count // 2, 2 * slots, 128), axis=0)
    total = total[0:slots, :] + total[slots:, :]
    whole = norm_one_ref[2:3, :]
    average, inverse = norm_one_ref[0:1, :], norm_one_ref[1:2, :]
    sums = total[0:1, :] + (total[1:2, :] + total[2:3, :])
    bias, gain = low_both(sums), high_both(sums)
    bias_out_ref[...] = bias[:, 0:64]
    gain_out_ref[...] = gain[:, 0:64]
    scale = twice(gain_ref[...]) * inverse
    bias, gain = bias / whole, gain / whole
    for g in range(pairs):
        mask = pair_mask(real_ref, g)

        def body(c, carry):
            rows = block(c * step, step)
            normed = (first_ref[g, rows, :] - average) * inverse
            grad = (scale * (grad_ref[g, rows, :] - mask * (bias + normed * gain))).astype(BF16)
            for half in range(2):
                place = block((g + half * pairs) * own + c * step, step)
                value = nn(grad, weight_ref[:, half * 256 : (half + 1) * 256])
                feature_ref[half, g, rows, :] = (value + gsum_ref[place, :]).astype(BF16)
            return carry

        lax.fori_loop(0, sizes.chunks, body, 0, unroll=True)
    me = lax.axis_index("img") * lax.axis_size("ha") + lax.axis_index("ha")
    lane = lax.broadcasted_iota(jnp.int32, (1, 128), 1)
    sent = sizes.rows6
    local = wide_ref[pl.ds(0, count, stride=slots), :] + (
        wide_ref[pl.ds(1, count, stride=slots), :] + wide_ref[pl.ds(2, count, stride=slots), :]
    )
    local = jnp.where(low_lanes(local.shape), local, swap(local))
    local = local / first_got_ref[pl.ds(1, count, stride=sizes.rows1), :] - bias
    clear(sizes, send_ref, sent, 1 + 8 * share)
    rows = jnp.concatenate([local, scale, gain, jnp.zeros((6, 128), F32)], axis=0)
    picked = [
        jnp.sum(jnp.where(lane == me + part * count, rows, 0.0), axis=1, keepdims=True) for part in range(share)
    ]
    for index, (half, part) in enumerate(cross_rows(sizes)):
        place = 3 + half * share + part
        raw = total[place : place + 1, :]
        if index < sizes.cross_early:
            cross = get_sum(second_got_ref, 1 + index, sizes.rows2, count)
        else:
            cross = get_sum(third_got_ref, 4 + share + index - sizes.cross_early, sizes.rows3, count)
        features = first_got_ref[pl.ds(2 + half, count, stride=sizes.rows1), :]
        local, factor, tilt = [picked[part][a:b, :] for a, b in ((0, count), (count, count + 1), (count + 1, count + 2))]
        value = factor * (raw + total_of(local * features) - tilt * cross)
        put_row(send_ref, half * share + part, sent, count, value)
    for slot in range(2 * share, 8 * share + 1):
        place = 3 + slot
        put_row(send_ref, slot, sent, count, total[place : place + 1, :])
    out_ref[...] = send_ref[...].astype(BF16)


def weights_kernel(sizes, got_ref, redt_out_ref, expander_out_ref, spatial_out_ref, wide_ref):
    share, count = sizes.share, sizes.count
    slots = sizes.rows6
    wide_ref[...] = got_ref[...].astype(F32)
    for out_ref, slot in ((redt_out_ref, 0), (expander_out_ref, 2 * share)):
        for half in range(2):
            out_ref[:, half * 128 : (half + 1) * 128] = get_rows(wide_ref, slot + half * share, slots, count, 64)
    for index in range(8):
        value = get_rows(wide_ref, (4 + index // 2) * share, slots, count, 64)
        if index % 2:
            value = swap(value)
        spatial_out_ref[index * 64 : (index + 1) * 64, :] = value[:, 0:64]
    value = get_rows(wide_ref, 8 * share, slots, count, 32)
    spatial_out_ref[512:544, :] = value[:, 0:64]
    spatial_out_ref[544:576, :] = swap(value)[:, 0:64]


def exchange(rows, count):
    pack = 2 if rows.dtype == BF16 else 1
    parted = rows.reshape(count, rows.shape[0] // (count * pack), pack, 128)
    return lax.all_to_all(parted, AXES, 0, 0).reshape(rows.shape)


def on_device(
    features,
    reducer,
    spatial,
    expander,
    gain_reduce,
    bias_reduce,
    gain_spatial,
    bias_spatial,
    gain_expand,
    bias_expand,
    upstream,
    image_counts,
):
    images, height, across, wide = features.shape
    count = lax.axis_size("img") * lax.axis_size("ha")
    sizes = Sizes(images, height, across, count)
    pairs, own, step = sizes.pairs, sizes.own, sizes.step
    flat = (images * own, wide)
    deep = (2, pairs, own, wide)
    feat_hbm, up_hbm = features.reshape(deep), upstream.reshape(deep)
    taps = spatial.reshape(9 * 64, 64)
    gain1, bias1, gain2, bias2, gain3, bias3 = [
        value.reshape(1, value.shape[0])
        for value in (gain_reduce, bias_reduce, gain_spatial, bias_spatial, gain_expand, bias_expand)
    ]
    outside = pl.BlockSpec(memory_space=pltpu.HBM)
    inside = pl.BlockSpec(memory_space=pltpu.VMEM)

    def shape(*dims, dtype=F32):
        return jax.ShapeDtypeStruct(dims, dtype)

    def call(kernel, outs, args, scratch=(), away=(), far=()):
        specs = []
        for arg in args:
            if arg is image_counts:
                specs.append(pl.BlockSpec(memory_space=pltpu.SMEM))
            else:
                specs.append(outside if any(arg is other for other in far) else inside)
        return pl.pallas_call(
            functools.partial(kernel, sizes),
            out_shape=outs,
            in_specs=specs,
            out_specs=tuple(outside if index in away else inside for index in range(len(outs))),
            scratch_shapes=list(scratch),
            compiler_params=pltpu.CompilerParams(vmem_limit_bytes=VMEM_MIB << 20),
        )(*args)

    ha = lax.axis_size("ha")
    near = [(i, i ^ 1) for i in range(ha)]
    far = [(i, i + 1) for i in range(1, ha - 1, 2)]
    far = far + [(target, source) for source, target in far]
    masks = [pltpu.VMEM((step, 128), F32), pltpu.VMEM((step, 128), F32)]

    given = tuple(
        pltpu.with_memory_space_constraint(value, pltpu.HBM)
        for value in (feat_hbm, up_hbm, reducer.T)
    )
    weight, real, near_rows, far_rows = call(
        prepare_kernel,
        (
            shape(128, 512, dtype=BF16),
            shape(16, 256),
            shape(2, pairs, step + sizes.edge, wide, dtype=BF16),
            shape(2, pairs, step + sizes.edge, wide, dtype=BF16),
        ),
        (*given, image_counts),
        [pltpu.VMEM((64, 256), BF16), pltpu.SemaphoreType.DMA((5,))],
        far=given,
    )
    near_rows = lax.ppermute(near_rows, "ha", near)
    far_rows = lax.ppermute(far_rows, "ha", far)
    feat = feat_hbm
    first, sums, rows = call(
        reduce_kernel,
        (shape(pairs, own, 128), shape(1, 256), shape(count * sizes.rows1, 128)),
        (feat, weight, real),
    )
    got1 = exchange(rows, count)
    windows, slope_one, second, norm_one, cross, rows = call(
        conv_kernel,
        (
            shape(pairs, own, 384, dtype=BF16),
            shape(pairs, own, 128),
            shape(pairs, sizes.ext, 128),
            shape(8, 128),
            shape(64, 256),
            shape(count * sizes.rows2, 128),
        ),
        (got1, feat, first, near_rows, far_rows, weight, taps, gain1, bias1, real),
        [pltpu.VMEM((2, 256, 256), BF16)] + [pltpu.VMEM((pairs, sizes.wide1, 128), F32)] * 2 + [*masks, pltpu.VMEM((pairs * own, 128), BF16)],
    )
    got2 = exchange(rows, count)
    hidden_two, slope_two, norm_two, gram, expand, rows = call(
        middle_kernel,
        (
            shape(pairs, sizes.ext, 128, dtype=BF16),
            shape(pairs, sizes.ext, 128),
            shape(8, 128),
            shape(64, 128),
            shape(128, 512, dtype=BF16),
            shape(count * sizes.rows3, 128),
        ),
        (got2, got1, second, gain2, bias2, expander, cross, real),
        [pltpu.VMEM((pairs * own, 128), BF16), pltpu.VMEM((pairs * own, 384), BF16)],
    )
    got3 = exchange(rows, count)
    active, grad_sum, back, norm_three, raw, rows = call(
        output_kernel,
        (
            shape(*flat, dtype=BF16),
            shape(*flat),
            shape(pairs, sizes.ext, 128),
            shape(8, 256),
            shape(64, 256),
            shape(count * sizes.rows4, 128),
        ),
        (
            got3, norm_one, norm_two, hidden_two, slope_two, second, feat, up_hbm, near_rows, far_rows,
            gain3, bias3, expand, real,
        ),
        [pltpu.VMEM((pairs * sizes.ext, 2 * wide), BF16), pltpu.VMEM((pairs * own, 2 * wide), F32)],
    )
    got4 = exchange(rows, count)
    gradgain3, gradbias3, gradgain2, gradbias2, grad_one, activated, rows = call(
        backward_kernel,
        (
            shape(1, 256),
            shape(1, 256),
            shape(1, 64),
            shape(1, 64),
            shape(pairs, own, 128),
            shape(*flat, dtype=BF16),
            shape(count * sizes.rows5, 128, dtype=BF16),
        ),
        (
            got4, got3, norm_one, norm_two, norm_three, gram, windows, slope_one, first, hidden_two,
            slope_two, second, back, raw, feat, sums, gain2, expand, taps, active, image_counts,
        ),
        [pltpu.VMEM((2, 256, 256), BF16)]
        + [pltpu.VMEM((sizes.wide2, 128), F32)] * 2
        + masks
        + [
            pltpu.VMEM((pairs * own, 384), BF16),
            pltpu.VMEM((count * sizes.rows5, 128), F32),
            pltpu.SemaphoreType.DMA,
        ],
        away=(5,),
    )
    got5 = exchange(rows, count)
    gradgain1, gradbias1, feature_grad, rows = call(
        shares_kernel,
        (
            shape(1, 64),
            shape(1, 64),
            pltpu.VMEM(deep, BF16),
            shape(count * sizes.rows6, 128, dtype=BF16),
        ),
        (got5, got1, got2, got3, norm_one, gain1, grad_one, first, grad_sum, weight, real),
        [pltpu.VMEM((count * sizes.rows6, 128), F32), pltpu.VMEM((count * sizes.rows5, 128), F32)],
    )
    got6 = exchange(rows, count)
    redt_grad, expander_grad, spatial_grad = call(
        weights_kernel,
        (shape(64, 256), shape(64, 256), shape(9 * 64, 64)),
        (got6,),
        [pltpu.VMEM((count * sizes.rows6, 128), F32)],
    )
    return (
        activated.reshape(features.shape),
        feature_grad.reshape(features.shape),
        redt_grad.T,
        spatial_grad.reshape(spatial.shape),
        expander_grad,
        gradgain1.reshape(64),
        gradbias1.reshape(64),
        gradgain2.reshape(64),
        gradbias2.reshape(64),
        gradgain3.reshape(256),
        gradbias3.reshape(256),
    )


def solution(mesh):
    whole = P("img", "ha", None, None)
    in_specs = (whole,) + (P(),) * 9 + (whole, P("img"))
    out_specs = (whole, whole) + (P(),) * 9
    return jax.shard_map(
        on_device, mesh=mesh, in_specs=in_specs, out_specs=out_specs, check_vma=False
    )
```

```python
import functools

import jax
import jax.numpy as jnp
from jax import lax
from jax.experimental import pallas as pl
from jax.experimental.pallas import tpu as pltpu
from jax.sharding import PartitionSpec as P

EPSILON = 1e-05
AXES = ("img", "ha")
F32 = jnp.float32
BF16 = jnp.bfloat16
VMEM_MIB = 16


def nn(left, right):
    return lax.dot_general(left, right, (((1,), (0,)), ((), ())), preferred_element_type=F32)


def nt(left, right):
    return lax.dot_general(left, right, (((1,), (1,)), ((), ())), preferred_element_type=F32)


def tn(left, right):
    return lax.dot_general(left, right, (((0,), (0,)), ((), ())), preferred_element_type=F32)


def pair_rows(sizes, ref):
    return jnp.concatenate([ref[half].reshape(sizes.pairs * sizes.own, 256) for half in range(2)], axis=1)


def tn_pair(left, right):
    product = tn(left, right)
    return product[0:64, 0:256] + product[64:128, 256:512]


def pieces(values):
    high = values.astype(BF16)
    rest = values - high.astype(F32)
    middle = rest.astype(BF16)
    low = (rest - middle.astype(F32)).astype(BF16)
    return high, middle, low


def exact(product, values, weights):
    high, middle, _ = pieces(values)
    return product(high, weights) + product(middle, weights)


def exact_rows(product, rows, weights):
    parts = [part for row in rows for part in pieces(row)]
    parts = parts + [jnp.zeros_like(parts[0])] * (-len(parts) % 8)
    result = product(jnp.concatenate([part.astype(F32) for part in parts], axis=0).astype(BF16), weights)
    return [total_of(result[3 * index : 3 * index + 3, :]) for index in range(len(rows))]


def folded(values):
    return jnp.sum(values.reshape(values.shape[0] // 8, 8, values.shape[1]), axis=0)


def total_of(values):
    return jnp.sum(values, axis=0, keepdims=True)


def swap(values):
    return pltpu.roll(values, 64, axis=1)


def low_lanes(shape):
    return lax.broadcasted_iota(jnp.int32, shape, 1) < 64


def low_both(row):
    return jnp.where(low_lanes(row.shape), row, swap(row))


def high_both(row):
    return jnp.where(low_lanes(row.shape), swap(row), row)


def twice(row):
    place = lax.broadcasted_iota(jnp.int32, (64, 128), 0)
    lane = lax.rem(lax.broadcasted_iota(jnp.int32, (64, 128), 1), 64)
    return exact_rows(nn, [row], (place == lane).astype(BF16))[0]


def swish(values):
    half = 0.5 * values
    turn = jnp.tanh(half)
    plus = 1.0 + turn
    value = half * plus
    return value, 0.5 * (plus + value * (1.0 - turn))


def fill_real(sizes, out_ref, count):
    count = jnp.zeros((1, 256), F32) + count.astype(F32)
    low = lax.rem(lax.broadcasted_iota(jnp.int32, (1, 256), 1), 128) < 64
    images = [(float(image) < count).astype(F32) for image in range(sizes.images)]
    rows = [jnp.where(low, images[g], images[g + sizes.pairs]) for g in range(sizes.pairs)] + images
    rows = rows + [jnp.zeros((1, 256), F32)] * (15 - len(rows)) + [count * sizes.pixels]
    out_ref[...] = jnp.concatenate(rows, axis=0)


def pair_mask(real_ref, g):
    return real_ref[g : g + 1, 0:128]


def count_mask(count_ref, g, pairs):
    count = count_ref[0]
    low = (g < count).astype(F32)
    high = (g + pairs < count).astype(F32)
    return jnp.where(low_lanes((1, 128)), low, high)


def image_mask(sizes, real_ref, image):
    return real_ref[sizes.pairs + image : sizes.pairs + image + 1, :]


def real_pixels(real_ref):
    return real_ref[15:16, 0:128]


def columns(row):
    return jnp.transpose(jnp.broadcast_to(row, (128, 128)))


def put_row(out_ref, slot, slots, count, row):
    out_ref[pl.ds(slot, count, stride=slots), :] = jnp.broadcast_to(row, (count, 128))


def put_rows(out_ref, slot, slots, count, matrix):
    rows = min(count, matrix.shape[0])
    for part in range(matrix.shape[0] // rows):
        out_ref[pl.ds(slot + part, rows, stride=slots), :] = matrix[part * rows : (part + 1) * rows, :]


def get_sum(got_ref, slot, slots, count):
    return total_of(got_ref[pl.ds(slot, count, stride=slots), :])


def get_rows(got_ref, slot, slots, count, height):
    rows = min(count, height)
    parts = [got_ref[pl.ds(slot + part, rows, stride=slots), :] for part in range(height // rows)]
    return parts[0] if len(parts) == 1 else jnp.concatenate(parts, axis=0)


def clear(sizes, out_ref, slots, used):
    if sizes.count > 64:
        out_ref[...] = jnp.zeros(out_ref.shape, F32)
    else:
        for slot in range(used, slots):
            put_row(out_ref, slot, slots, sizes.count, jnp.zeros((1, 128), F32))


class Sizes:
    def __init__(self, images, height, across, count):
        self.images, self.height, self.across, self.count = images, height, across, count
        self.pairs = images // 2
        self.own = height * across
        self.pixels = float(height * across)
        self.step = 2 * across
        self.chunks = height // 2
        self.ext = self.own + self.step
        self.sample = 32
        self.wide1 = (height + 4) * across
        self.wide2 = (height + 2) * across
        self.share = max(1, 64 // count)
        self.rows1 = 4
        self.cross_early = min(3, 2 * self.share)
        self.cross_late = 2 * self.share - self.cross_early
        self.rows2 = 4
        self.rows3 = 4 + self.share + self.cross_late
        self.rows4 = 5 + self.share
        self.rows5 = -(-(4 + 8 * self.share) // 4) * 4
        self.rows6 = -(-(1 + 8 * self.share) // 2) * 2


def block(start, size):
    return pl.ds(pl.multiple_of(start, size), size)


def diagonal(out_ref, weight):
    out_ref[...] = jnp.zeros(out_ref.shape, out_ref.dtype)
    out_ref[0:64, 0:256] = weight
    out_ref[64:128, 256:512] = weight


def edge_masks(sizes, low_ref, high_ref):
    column = lax.rem(lax.broadcasted_iota(jnp.int32, (sizes.step, 128), 0), sizes.across)
    low_ref[...] = (column > 0).astype(F32)
    high_ref[...] = (column < sizes.across - 1).astype(F32)


def all_taps(out_ref, taps_ref, back):
    out_ref[...] = jnp.zeros(out_ref.shape, BF16)
    for vertical in range(3):
        for lateral in range(3):
            tap = taps_ref[(vertical * 3 + lateral) * 64 : (vertical * 3 + lateral + 1) * 64, :]
            if back:
                place_taps(out_ref, 2 - vertical, lateral, jnp.transpose(tap))
            else:
                place_taps(out_ref, vertical, lateral, tap)


def place_taps(out_ref, vertical, lateral, tap):
    for half in range(2):
        row = vertical * 64 if vertical < 2 else 128 + 64 * half
        column = 128 + 64 * half if lateral == 1 else 64 * ((lateral // 2 + half) % 2)
        out_ref[half, row : row + 64, column : column + 64] = tap


def taps_apart(windows, swapped, weight_ref):
    low = low_lanes(windows[0].shape)
    pair_low = jnp.where(low, windows[0], swapped[1]).astype(BF16)
    pair_high = jnp.where(low, swapped[0], windows[1]).astype(BF16)
    last = windows[2].astype(BF16)
    one = nn(jnp.concatenate([pair_low, last], axis=1), weight_ref[0])
    two = nn(jnp.concatenate([pair_high, last], axis=1), weight_ref[1])
    products = (
        jnp.where(low, one[:, 0:128], two[:, 0:128]),
        one[:, 128:256] + two[:, 128:256],
        swap(jnp.where(low, two[:, 0:128], one[:, 0:128])),
    )
    return products, jnp.concatenate([pair_low, pair_high, last], axis=1)


def from_left(values, low):
    return pltpu.roll(values, 1, axis=0) * low


def from_right(values, high):
    return pltpu.roll(values, values.shape[0] - 1, axis=0) * high


class Stats:
    def __init__(self, real_ref):
        self.real_ref = real_ref
        self.number = real_pixels(real_ref)
        self.near = None
        self.part = [jnp.zeros((8, 128), F32)] * 2
        self.whole = [jnp.zeros((8, 128), F32)] * 2

    def add(self, value):
        if self.near is None:
            self.near = low_both(total_of(value) / float(value.shape[0]))
        apart = value - self.near
        self.part = [self.part[0] + folded(apart), self.part[1] + folded(apart * apart)]

    def close(self, g):
        mask = pair_mask(self.real_ref, g)
        self.whole = [whole + part * mask for whole, part in zip(self.whole, self.part)]
        self.part = [jnp.zeros((8, 128), F32)] * 2

    def row(self):
        total, square = [total_of(value) for value in self.whole]
        total, square = total + swap(total), square + swap(square)
        square = square - total * total / self.number
        return jnp.where(low_lanes((1, 128)), total + self.number * self.near, square)


def prepare_kernel(
    sizes, feat_hbm, up_hbm, redt_hbm, count_ref, weight_ref, real_ref, near_ref, far_ref, redt_ref, sem_ref,
):
    step, own = sizes.step, sizes.own
    edges = []
    odd = lax.rem(lax.axis_index("ha"), 2)
    to_last = pl.multiple_of((1 - odd) * (own - step), step)
    to_head = pl.multiple_of(odd * (own - step), step)
    for out, start in ((near_ref, to_last), (far_ref, to_head)):
        for place, source in enumerate((feat_hbm, up_hbm)):
            copy = pltpu.make_async_copy(
                source.at[:, :, pl.ds(start, step), :], out.at[place], sem_ref.at[len(edges)]
            )
            copy.start()
            edges.append(copy)
    small = pltpu.make_async_copy(redt_hbm, redt_ref, sem_ref.at[4])
    small.start()
    fill_real(sizes, real_ref, count_ref[0])
    small.wait()
    diagonal(weight_ref, redt_ref[...])
    for copy in edges:
        copy.wait()


def reduce_kernel(sizes, feat_ref, weight_ref, real_ref, first_ref, sums_ref, out_ref):
    pairs, step = sizes.pairs, sizes.step
    stats = Stats(real_ref)
    feats = jnp.zeros((8, 256), F32)
    for g in range(pairs):
        low_sum = high_sum = jnp.zeros((8, 256), F32)
        for c in range(sizes.chunks):
            low = feat_ref[0, g, c * step : (c + 1) * step, :]
            high = feat_ref[1, g, c * step : (c + 1) * step, :]
            value = nt(jnp.concatenate([low, high], axis=1), weight_ref[...])
            first_ref[g, c * step : (c + 1) * step, :] = value
            stats.add(value)
            low_sum = low_sum + folded(low.astype(F32))
            high_sum = high_sum + folded(high.astype(F32))
        stats.close(g)
        feats = feats + low_sum * image_mask(sizes, real_ref, g)
        feats = feats + high_sum * image_mask(sizes, real_ref, g + pairs)
    feats = total_of(feats)
    sums_ref[...] = feats
    slots, count = sizes.rows1, sizes.count
    put_row(out_ref, 0, slots, count, stats.row())
    put_row(out_ref, 1, slots, count, stats.number)
    put_row(out_ref, 2, slots, count, feats[:, 0:128])
    put_row(out_ref, 3, slots, count, feats[:, 128:256])


def merged(sizes, got_ref, slots, numbers):
    rows = got_ref[pl.ds(0, sizes.count, stride=slots), :]
    whole = total_of(numbers)
    low = low_lanes(rows.shape)
    both = jnp.where(low, rows, swap(rows))
    average = total_of(both) / whole
    apart = both / numbers - average
    squares = jnp.where(low, swap(rows), rows)
    variance = total_of(squares + numbers * apart * apart) / whole
    return average, lax.rsqrt(variance + EPSILON), whole


def conv_kernel(
    sizes, got_ref, feat_ref, first_ref, near_ref, far_ref, weight_ref, taps_ref, gain_ref, bias_ref, real_ref,
    window_ref, slope_ref, second_ref, norm_ref, cross_ref, out_ref, conv_ref, hidden_ref, turned_ref, low_ref, high_ref, normed_ref,
):
    pairs, step, own, across = sizes.pairs, sizes.step, sizes.own, sizes.across
    numbers = got_ref[pl.ds(1, sizes.count, stride=sizes.rows1), :]
    average, inverse, whole = merged(sizes, got_ref, sizes.rows1, numbers)
    norm_ref[...] = jnp.concatenate([average, inverse, whole, jnp.zeros((5, 128), F32)], axis=0)
    gain, bias = twice(gain_ref[...]), twice(bias_ref[...])
    place = lax.axis_index("ha")
    odd = lax.rem(place, 2)
    has_far = jnp.logical_and(place > 0, place < lax.axis_size("ha") - 1).astype(F32)
    near_start = pl.multiple_of((1 - odd) * (own + step), step)
    far_start = pl.multiple_of(odd * (own + step), step)
    edge_masks(sizes, low_ref, high_ref)
    all_taps(conv_ref, taps_ref, False)
    for g in range(pairs):
        mask = pair_mask(real_ref, g)

        def activate(c, carry):
            normed = (first_ref[g, block(c * step, step), :] - average) * inverse
            value, slope = swish(normed * gain + bias)
            hidden_ref[g, block((c + 1) * step, step), :] = value
            turned_ref[g, block((c + 1) * step, step), :] = swap(value)
            slope_ref[g, block(c * step, step), :] = slope
            normed_ref[block(g * own + c * step, step), :] = (normed * mask).astype(BF16)
            return carry

        lax.fori_loop(0, sizes.chunks, activate, 0, unroll=True)
        for start, valid, rows_ref in ((near_start, 1.0, near_ref), (far_start, has_far, far_ref)):
            low, high = rows_ref[0, 0, g], rows_ref[0, 1, g]
            first = nt(jnp.concatenate([low, high], axis=1), weight_ref[...])
            value, _ = swish((first - average) * inverse * gain + bias)
            value = value * valid
            hidden_ref[g, pl.ds(start, step), :] = value
            turned_ref[g, pl.ds(start, step), :] = swap(value)
    cross = tn_pair(normed_ref[...], pair_rows(sizes, feat_ref))
    cross_ref[...] = cross

    def together(products):
        return from_left(products[0], low_ref[...]) + products[1] + from_right(products[2], high_ref[...])

    total = jnp.zeros((8, 128), F32)
    for g in range(pairs):
        part = jnp.zeros((8, 128), F32)
        starts = [slice((a + 1) * across, (a + 1) * across + own) for a in range(3)]
        products, window_ref[g] = taps_apart(
            *[[ref[g, start, :] for start in starts] for ref in (hidden_ref, turned_ref)], conv_ref
        )
        for c in range(sizes.chunks):
            rows = slice(c * step, (c + 1) * step)
            value = together([product[rows, :] for product in products])
            second_ref[g, rows, :] = value
            part = part + folded(value)
        total = total + part * pair_mask(real_ref, g)
        last = sizes.height + 1
        windows, swapped = [
            [
                jnp.concatenate(
                    [
                        ref[g, a * across : (a + 1) * across, :],
                        ref[g, (last + a) * across : (last + a + 1) * across, :],
                    ],
                    axis=0,
                )
                for a in range(3)
            ]
            for ref in (hidden_ref, turned_ref)
        ]
        products, _ = taps_apart(windows, swapped, conv_ref)
        second_ref[g, own : own + step, :] = together(products)
    total = total_of(total)
    total = total + swap(total)
    local = total / (real_pixels(real_ref))
    square = jnp.zeros((8, 128), F32)
    for g in range(pairs):
        part = jnp.zeros((8, 128), F32)
        for c in range(sizes.chunks):
            apart = second_ref[g, c * step : (c + 1) * step, :] - local
            part = part + folded(apart * apart)
        square = square + part * pair_mask(real_ref, g)
    square = total_of(square)
    square = square + swap(square)
    slots = sizes.rows2
    put_row(out_ref, 0, slots, sizes.count, jnp.where(low_lanes((1, 128)), total, square))
    put_cross(sizes, out_ref, 1, slots, cross, 0, sizes.cross_early)


def cross_rows(sizes):
    return [(half, part) for half in range(2) for part in range(sizes.share)]


def put_cross(sizes, out_ref, slot, slots, cross, start, stop):
    rows = min(sizes.count, 64)
    for index, (half, part) in enumerate(cross_rows(sizes)[start:stop]):
        matrix = cross[part * rows : (part + 1) * rows, half * 128 : (half + 1) * 128]
        out_ref[pl.ds(slot + index, rows, stride=slots), :] = matrix


def middle_kernel(
    sizes, got_ref, first_got_ref, second_ref, gain_ref, bias_ref, expander_ref, cross_ref, real_ref,
    hidden_ref, slope_ref, norm_ref, gram_ref, expand_ref, out_ref, left_ref, right_ref,
):
    pairs, step, own = sizes.pairs, sizes.step, sizes.own
    slots = sizes.rows3
    numbers = first_got_ref[pl.ds(1, sizes.count, stride=sizes.rows1), :]
    average, inverse, _ = merged(sizes, got_ref, sizes.rows2, numbers)
    gain, bias = twice(gain_ref[...]), twice(bias_ref[...])
    centre, tangent = swish(bias)
    centre = 0.125 * jnp.floor(8.0 * centre + 0.5)
    diagonal(expand_ref, expander_ref[...])
    sums = (jnp.zeros((8, 128), F32),) * 3
    for g in range(pairs):
        mask = pair_mask(real_ref, g)

        def activate(c, acc):
            rows = block(c * step, step)
            normed = (second_ref[g, rows, :] - average) * inverse
            value, slope = swish(normed * gain + bias)
            rounded = value.astype(BF16)
            hidden_ref[g, rows, :] = rounded
            slope_ref[g, rows, :] = slope
            apart = (rounded.astype(F32) - centre) * mask
            slope = slope * mask
            tilted = slope * normed
            rows = block(g * own + c * step, step)
            left_ref[rows, :] = apart.astype(BF16)
            right_ref[rows, 0:128] = apart.astype(BF16)
            right_ref[rows, 128:256] = (slope - tangent).astype(BF16)
            right_ref[rows, 256:384] = tilted.astype(BF16)
            return acc[0] + folded(apart), acc[1] + folded(slope), acc[2] + folded(tilted)

        sums = lax.fori_loop(0, sizes.chunks, activate, sums, unroll=True)
        value, slope = swish((second_ref[g, own : own + step, :] - average) * inverse * gain + bias)
        hidden_ref[g, own : own + step, :] = value.astype(BF16)
        slope_ref[g, own : own + step, :] = slope
    product = tn(left_ref[...], right_ref[...])
    apart, slope, tilted = [total_of(value) for value in sums]
    apart, slope, tilted = apart + swap(apart), slope + swap(slope), tilted + swap(tilted)
    low, high = product[0:64, :], product[64:128, :]
    gram = low[:, 0:128] + swap(high[:, 0:128])
    slopes = low[:, 128:256] + swap(high[:, 128:256])
    tilts = swap(low[:, 256:384]) + high[:, 256:384]
    wide = low_lanes((64, 128))
    slopes = slopes + columns(apart)[0:64, :] * tangent
    gram = jnp.where(wide, gram, 0.0)
    gram_ref[...] = gram
    weights = expander_ref[...]
    quad = total_of(exact(nn, gram[:, 0:64], weights) * weights.astype(F32))
    norm_ref[...] = jnp.concatenate(
        [average, inverse, centre, apart, jnp.where(low_lanes((1, 128)), slope, tilted), jnp.zeros((3, 128), F32)],
        axis=0,
    )
    put_row(out_ref, 0, slots, sizes.count, quad[:, 0:128])
    put_row(out_ref, 1, slots, sizes.count, quad[:, 128:256])
    put_row(out_ref, 2, slots, sizes.count, apart)
    put_row(out_ref, 3, slots, sizes.count, jnp.where(low_lanes((1, 128)), slope, tilted))
    put_rows(out_ref, 4, slots, sizes.count, jnp.where(wide, slopes, tilts))
    put_cross(sizes, out_ref, 4 + sizes.share, slots, cross_ref[...], sizes.cross_early, 2 * sizes.share)


def output_kernel(
    sizes, got_ref, norm_one_ref, norm_ref, hidden_ref, slope_ref, second_ref, feat_ref, up_ref,
    near_ref, far_ref, gain_ref, bias_ref, expand_ref, real_ref,
    active_ref, gsum_ref, back_ref, last_ref, raw_ref, out_ref, scaled_ref, third_ref,
):
    pairs, step, own, across = sizes.pairs, sizes.step, sizes.own, sizes.across
    odd = lax.rem(lax.axis_index("ha"), 2) == 1
    slots, count = sizes.rows3, sizes.count
    whole = norm_one_ref[2:3, :]
    centre = norm_ref[2:3, :]
    apart = get_sum(got_ref, 2, slots, count) / whole
    mean_hidden = centre + apart
    column = expand_ref[:, 0:256]
    shift, average = exact_rows(nn, [apart, mean_hidden], column)
    quad = jnp.concatenate([get_sum(got_ref, 0, slots, count), get_sum(got_ref, 1, slots, count)], axis=1)
    wide = jnp.concatenate([whole, whole], axis=1)
    inverse = lax.rsqrt(quad / wide - shift * shift + EPSILON)
    gain, bias = gain_ref[...], bias_ref[...]
    scale = gain * inverse
    offset = bias - average * scale
    average_two, inverse_two = norm_ref[0:1, :], norm_ref[1:2, :]

    def outward(third, feat):
        half_sum = 0.5 * (third * scale + offset + feat)
        turn = jnp.tanh(half_sum)
        plus = 1.0 + turn
        value = half_sum * plus
        return value, plus + value * (1.0 - turn)

    sample = slice(0, sizes.sample)
    _, slope = outward(nn(hidden_ref[0, sample, :], column), feat_ref[0, 0, sample, :].astype(F32))
    middle = 0.5 * total_of(up_ref[0, 0, sample, :].astype(F32) * slope) / float(sizes.sample)
    flat = scale * middle
    (flat_back,) = exact_rows(nt, [flat], expand_ref[:, 0:256] + expand_ref[:, 256:512])
    last_ref[...] = jnp.concatenate(
        [average, inverse, scale, jnp.concatenate([mean_hidden, apart], axis=1), middle, flat, shift, jnp.zeros((1, 256), F32)],
        axis=0,
    )
    biases = jnp.zeros((8, 256), F32)
    for g in range(pairs):
        valids = [image_mask(sizes, real_ref, g + half * pairs) for half in range(2)]
        middles = [middle * valid for valid in valids]

        third_ref[g * own : (g + 1) * own, :] = nn(hidden_ref[g, 0:own, :], expand_ref[...])

        def body(c, biases):
            for half in range(2):
                image = g + half * pairs
                third = third_ref[block(g * own + c * step, step), half * 256 : (half + 1) * 256]
                for start in range(0, step, 16):
                    here = pl.ds(pl.multiple_of(c * step + start, 16), 16)
                    place = pl.ds(pl.multiple_of(image * own + c * step + start, 16), 16)
                    value, slope = outward(third[start : start + 16, :], feat_ref[half, g, here, :].astype(F32))
                    active_ref[place, :] = value.astype(BF16)
                    grad = up_ref[half, g, here, :].astype(F32) * (0.5 * valids[half]) * slope
                    gsum_ref[place, :] = grad
                    grad = grad - middles[half]
                    biases = biases + folded(grad)
                    there = pl.ds(pl.multiple_of(g * own + c * step + start, 16), 16)
                    scaled_ref[there, half * 256 : (half + 1) * 256] = (grad * scale).astype(BF16)
            return biases

        biases = lax.fori_loop(0, sizes.chunks, body, biases, unroll=True)
        hidden = hidden_ref[g, own : own + step, :]
        edge = pairs * own + g * step
        for half in range(2):
            image = g + half * pairs
            both = []
            for which in range(2):
                near = near_ref[which, half, g].astype(F32)
                far = far_ref[which, half, g].astype(F32)
                upper = jnp.where(odd, near[across:, :], far[across:, :])
                lower = jnp.where(odd, far[0:across, :], near[0:across, :])
                both.append(jnp.concatenate([upper, lower], axis=0))
            _, slope = outward(nn(hidden, expand_ref[:, half * 256 : (half + 1) * 256]), both[0])
            grad = both[1] * (0.5 * valids[half]) * slope
            scaled = ((grad - middles[half]) * scale).astype(BF16)
            scaled_ref[edge : edge + step, half * 256 : (half + 1) * 256] = scaled
    tops = tilts = jnp.zeros((8, 128), F32)
    backs = nt(scaled_ref[...], expand_ref[...])
    for g in range(pairs):
        back = backs[g * own : (g + 1) * own, :]
        back_ref[g, 0:own, :] = back
        top = slope_ref[g, 0:own, :] * back
        normed_two = (second_ref[g, 0:own, :] - average_two) * inverse_two
        tops, tilts = tops + folded(top), tilts + folded(top * normed_two)
        edge = pairs * own + g * step
        back_ref[g, own : own + step, :] = backs[edge : edge + step, :]
    raw = tn_pair(hidden_ref[:, 0:own, :].reshape(pairs * own, 128), scaled_ref[0 : pairs * own, :])
    raw_ref[...] = raw
    biases, tops, tilts = [total_of(value) for value in (biases, tops, tilts)]
    gains = total_of(raw * expand_ref[0:64, 0:256].astype(F32)) / scale - average * biases
    number = real_pixels(real_ref)
    (third_sum,) = exact_rows(nn, [norm_ref[3:4, :] - number * apart], column)
    gains = inverse * (gains + middle * third_sum)
    biases = biases + number[:, 0:1] * middle
    tops, tilts = tops + swap(tops), tilts + swap(tilts)
    tops = jnp.where(low_lanes((1, 128)), tops, tilts) + norm_ref[4:5, :] * flat_back
    sent = sizes.rows4
    put_row(out_ref, 0, sent, count, biases[:, 0:128])
    put_row(out_ref, 1, sent, count, biases[:, 128:256])
    put_row(out_ref, 2, sent, count, gains[:, 0:128])
    put_row(out_ref, 3, sent, count, gains[:, 128:256])
    put_row(out_ref, 4, sent, count, tops)
    for part in range(sizes.share):
        put_row(out_ref, 5 + part, sent, count, get_sum(got_ref, 4 + part, slots, count))


def backward_kernel(
    sizes, got_ref, third_got_ref, norm_one_ref, norm_ref, last_ref, gram_ref, window_ref, slope_one_ref,
    first_ref, hidden_ref, slope_ref, second_ref, back_ref, raw_ref, feat_ref, sums_ref, gain_two_ref, expand_ref,
    taps_ref, active_ref, count_ref,
    gain3_out_ref, bias3_out_ref, gain2_out_ref, bias2_out_ref, grad_one_ref, active_hbm, out_ref,
    conv_back_ref, grad_ref, turned_ref, low_ref, high_ref, right_ref, send_ref, sem_ref,
):
    pairs, step, own, across = sizes.pairs, sizes.step, sizes.own, sizes.across
    leave = pltpu.make_async_copy(active_ref, active_hbm, sem_ref)
    leave.start()
    share, count = sizes.share, sizes.count
    third_slots, slots = sizes.rows3, sizes.rows4
    whole = norm_one_ref[2:3, :]
    whole_wide = jnp.concatenate([whole, whole], axis=1)
    bias3 = jnp.concatenate([get_sum(got_ref, 0, slots, count), get_sum(got_ref, 1, slots, count)], axis=1)
    gain3 = jnp.concatenate([get_sum(got_ref, 2, slots, count), get_sum(got_ref, 3, slots, count)], axis=1)
    bias3_out_ref[...] = bias3
    gain3_out_ref[...] = gain3
    inverse3, scale3 = last_ref[1:2, :], last_ref[2:3, :]
    mean_hidden, apart = last_ref[3:4, 0:128], last_ref[3:4, 128:256]
    flat = scale3 * bias3 / whole_wide
    tilt = scale3 * inverse3 * gain3 / whole_wide
    diag = expand_ref[...]
    stacked = diag[:, 0:256] + diag[:, 256:512]
    flat_here = flat - last_ref[5:6, :]
    flat_back, flat_here_back, mean_mix, apart_mix = exact_rows(
        nt, [flat, flat_here, last_ref[0:1, :] * tilt, last_ref[6:7, :] * tilt], stacked
    )
    tilt_wide = jnp.concatenate([tilt, tilt], axis=1)
    mixing = exact(nt, diag.astype(F32) * tilt_wide, diag)
    mix_high, mix_low, _ = pieces(mixing)
    mix_both = jnp.concatenate([mix_high, mix_low], axis=1)
    row_low = low_lanes((1, 128))
    slopes = get_sum(third_got_ref, 3, third_slots, count)
    cross = get_rows(got_ref, 5, slots, count, 64)
    mixed = total_of((mixing[0:64, :] + mixing[64:128, :]) * cross)
    sums = get_sum(got_ref, 4, slots, count) - (slopes * (flat_back - apart_mix) + mixed)
    bias2, gain2 = low_both(sums), high_both(sums)
    bias2_out_ref[...] = bias2[:, 0:64]
    gain2_out_ref[...] = gain2[:, 0:64]
    average_two, inverse_two, centre = norm_ref[0:1, :], norm_ref[1:2, :], norm_ref[2:3, :]
    scale2 = twice(gain_two_ref[...]) * inverse_two
    base = flat_here_back - mean_mix
    place = lax.axis_index("ha")
    has_above = (place > 0).astype(F32)
    has_below = (place < lax.axis_size("ha") - 1).astype(F32)
    edge_masks(sizes, low_ref, high_ref)
    all_taps(conv_back_ref, taps_ref, True)
    average_one, inverse_one = norm_one_ref[0:1, :], norm_one_ref[1:2, :]

    local = norm_ref[3:4, :]
    number = count_ref[0].astype(F32) * sizes.pixels
    col_hidden = columns(local + number * centre)[0:64, :]
    col_local = columns(local)[0:64, :]
    col_centre = columns(centre)[0:64, :]
    around = gram_ref[...] - col_local * apart + col_centre * (local - number * apart)
    around = exact(nn, around[:, 0:64], diag[0:64, 0:256])
    col_wide = jnp.concatenate([col_hidden, col_hidden], axis=1)
    expander = raw_ref[...] - col_wide * flat_here - around * tilt

    sums = (jnp.zeros((8, 128), F32), jnp.zeros((8, 128), F32))
    for g in range(pairs):
        mask = count_mask(count_ref, g, pairs)

        def inward(rows):
            hidden = hidden_ref[g, rows, :]
            mixed = nn(hidden, mix_both)
            mixed = mixed[:, 0:128] + mixed[:, 128:256]
            grad = slope_ref[g, rows, :] * (back_ref[g, rows, :] - mask * (base + mixed))
            normed = (second_ref[g, rows, :] - average_two) * inverse_two
            return scale2 * (grad - mask * ((bias2 + normed * gain2) / whole))

        def store(c, carry):
            rows = block(c * step, step)
            grad = inward(rows)
            here = pl.ds(pl.multiple_of(c * step + across, 8), step)
            grad_ref[here, :] = grad
            turned_ref[here, :] = swap(grad)
            rows = block(g * own + c * step, step)
            right_ref[rows, 0:128] = from_right(grad, high_ref[...]).astype(BF16)
            right_ref[rows, 128:256] = grad.astype(BF16)
            right_ref[rows, 256:384] = from_left(grad, low_ref[...]).astype(BF16)
            return carry

        lax.fori_loop(0, sizes.chunks, store, 0, unroll=True)
        edge = inward(pl.ds(own, step))
        for start, value in ((0, edge[0:across, :] * has_above), (own + across, edge[across:, :] * has_below)):
            grad_ref[start : start + across, :] = value
            turned_ref[start : start + across, :] = swap(value)

        starts = [slice(a * across, a * across + own) for a in range(3)]
        products, _ = taps_apart(
            [grad_ref[start, :] for start in starts], [turned_ref[start, :] for start in starts[0:2]], conv_back_ref
        )
        for c in range(sizes.chunks):
            rows = slice(c * step, (c + 1) * step)
            value = from_right(products[0][rows, :], high_ref[...]) + products[1][rows, :]
            value = value + from_left(products[2][rows, :], low_ref[...])
            grad = value * slope_one_ref[g, rows, :]
            grad_one_ref[g, rows, :] = grad
            normed = (first_ref[g, rows, :] - average_one) * inverse_one
            sums = sums[0] + folded(grad), sums[1] + folded(grad * normed)
    product = tn(window_ref[...].reshape(pairs * own, 384), right_ref[...])
    grad = grad_one_ref[...].reshape(pairs * own, 128).astype(BF16)
    reducer = tn_pair(grad, pair_rows(sizes, feat_ref))
    tops, tilts = total_of(sums[0]), total_of(sums[1])
    tops, tilts = tops + swap(tops), tilts + swap(tilts)
    sent = sizes.rows5
    clear(sizes, send_ref, sent, 4 + 8 * share)
    for slot, row in enumerate(pieces(jnp.where(row_low, tops, tilts))):
        put_row(send_ref, slot, sent, count, row.astype(F32))
    reducer = reducer - jnp.concatenate([columns(tops / number)[0:64, :]] * 2, axis=1) * sums_ref[...]
    slot = 3
    for matrix in (reducer, expander):
        for half in range(2):
            put_rows(send_ref, slot, sent, count, matrix[:, half * 128 : (half + 1) * 128])
            slot += share
    wide = low_lanes((64, 128))

    def tap(index):
        row, column = index // 3, (index % 3) * 128
        rows = (64 * row, 128 + 64 * row) if row < 2 else (256, 320)
        return [product[start : start + 64, column : column + 128] for start in rows]

    for pair in range(4):
        low, high = tap(2 * pair)
        even = low + swap(high)
        low, high = tap(2 * pair + 1)
        odd = swap(low) + high
        put_rows(send_ref, slot, sent, count, jnp.where(wide, even, odd))
        slot += share
    low, high = tap(8)
    even = low + swap(high)
    put_rows(send_ref, slot, sent, count, jnp.where(low_lanes((32, 128)), even[0:32, :], swap(even[32:64, :])))
    out_ref[...] = send_ref[...].astype(BF16)
    leave.wait()


def shares_kernel(
    sizes, got_ref, first_got_ref, second_got_ref, third_got_ref, norm_one_ref, gain_ref, grad_ref, first_ref,
    gsum_ref, weight_ref, real_ref,
    gain_out_ref, bias_out_ref, feature_ref, out_ref,
    send_ref, wide_ref,
):
    share, count, pairs, step, own = sizes.share, sizes.count, sizes.pairs, sizes.step, sizes.own
    slots = sizes.rows5
    wide_ref[...] = got_ref[...].astype(F32)
    total = jnp.sum(wide_ref[...].reshape(count // 2, 2 * slots, 128), axis=0)
    total = total[0:slots, :] + total[slots:, :]
    whole = norm_one_ref[2:3, :]
    average, inverse = norm_one_ref[0:1, :], norm_one_ref[1:2, :]
    sums = total[0:1, :] + (total[1:2, :] + total[2:3, :])
    bias, gain = low_both(sums), high_both(sums)
    bias_out_ref[...] = bias[:, 0:64]
    gain_out_ref[...] = gain[:, 0:64]
    scale = twice(gain_ref[...]) * inverse
    bias, gain = bias / whole, gain / whole
    for g in range(pairs):
        mask = pair_mask(real_ref, g)

        def body(c, carry):
            rows = block(c * step, step)
            normed = (first_ref[g, rows, :] - average) * inverse
            grad = (scale * (grad_ref[g, rows, :] - mask * (bias + normed * gain))).astype(BF16)
            for half in range(2):
                place = block((g + half * pairs) * own + c * step, step)
                value = nn(grad, weight_ref[:, half * 256 : (half + 1) * 256])
                feature_ref[half, g, rows, :] = (value + gsum_ref[place, :]).astype(BF16)
            return carry

        lax.fori_loop(0, sizes.chunks, body, 0, unroll=True)
    me = lax.axis_index("img") * lax.axis_size("ha") + lax.axis_index("ha")
    lane = lax.broadcasted_iota(jnp.int32, (1, 128), 1)
    sent = sizes.rows6
    local = wide_ref[pl.ds(0, count, stride=slots), :] + (
        wide_ref[pl.ds(1, count, stride=slots), :] + wide_ref[pl.ds(2, count, stride=slots), :]
    )
    local = jnp.where(low_lanes(local.shape), local, swap(local))
    local = local / first_got_ref[pl.ds(1, count, stride=sizes.rows1), :] - bias
    clear(sizes, send_ref, sent, 1 + 8 * share)
    rows = jnp.concatenate([local, scale, gain, jnp.zeros((6, 128), F32)], axis=0)
    picked = [
        jnp.sum(jnp.where(lane == me + part * count, rows, 0.0), axis=1, keepdims=True) for part in range(share)
    ]
    for index, (half, part) in enumerate(cross_rows(sizes)):
        place = 3 + half * share + part
        raw = total[place : place + 1, :]
        if index < sizes.cross_early:
            cross = get_sum(second_got_ref, 1 + index, sizes.rows2, count)
        else:
            cross = get_sum(third_got_ref, 4 + share + index - sizes.cross_early, sizes.rows3, count)
        features = first_got_ref[pl.ds(2 + half, count, stride=sizes.rows1), :]
        local, factor, tilt = [picked[part][a:b, :] for a, b in ((0, count), (count, count + 1), (count + 1, count + 2))]
        value = factor * (raw + total_of(local * features) - tilt * cross)
        put_row(send_ref, half * share + part, sent, count, value)
    for slot in range(2 * share, 8 * share + 1):
        place = 3 + slot
        put_row(send_ref, slot, sent, count, total[place : place + 1, :])
    out_ref[...] = send_ref[...].astype(BF16)


def weights_kernel(sizes, got_ref, redt_out_ref, expander_out_ref, spatial_out_ref, wide_ref):
    share, count = sizes.share, sizes.count
    slots = sizes.rows6
    wide_ref[...] = got_ref[...].astype(F32)
    for out_ref, slot in ((redt_out_ref, 0), (expander_out_ref, 2 * share)):
        for half in range(2):
            out_ref[:, half * 128 : (half + 1) * 128] = get_rows(wide_ref, slot + half * share, slots, count, 64)
    for index in range(8):
        value = get_rows(wide_ref, (4 + index // 2) * share, slots, count, 64)
        if index % 2:
            value = swap(value)
        spatial_out_ref[index * 64 : (index + 1) * 64, :] = value[:, 0:64]
    value = get_rows(wide_ref, 8 * share, slots, count, 32)
    spatial_out_ref[512:544, :] = value[:, 0:64]
    spatial_out_ref[544:576, :] = swap(value)[:, 0:64]


def exchange(rows, count):
    pack = 2 if rows.dtype == BF16 else 1
    parted = rows.reshape(count, rows.shape[0] // (count * pack), pack, 128)
    return lax.all_to_all(parted, AXES, 0, 0).reshape(rows.shape)


def on_device(
    features,
    reducer,
    spatial,
    expander,
    gain_reduce,
    bias_reduce,
    gain_spatial,
    bias_spatial,
    gain_expand,
    bias_expand,
    upstream,
    image_counts,
):
    images, height, across, wide = features.shape
    count = lax.axis_size("img") * lax.axis_size("ha")
    sizes = Sizes(images, height, across, count)
    pairs, own, step = sizes.pairs, sizes.own, sizes.step
    flat = (images * own, wide)
    deep = (2, pairs, own, wide)
    feat_hbm, up_hbm = features.reshape(deep), upstream.reshape(deep)
    taps = spatial.reshape(9 * 64, 64)
    gain1, bias1, gain2, bias2, gain3, bias3 = [
        value.reshape(1, value.shape[0])
        for value in (gain_reduce, bias_reduce, gain_spatial, bias_spatial, gain_expand, bias_expand)
    ]
    outside = pl.BlockSpec(memory_space=pltpu.HBM)
    inside = pl.BlockSpec(memory_space=pltpu.VMEM)

    def shape(*dims, dtype=F32):
        return jax.ShapeDtypeStruct(dims, dtype)

    def call(kernel, outs, args, scratch=(), away=(), far=()):
        specs = []
        for arg in args:
            if arg is image_counts:
                specs.append(pl.BlockSpec(memory_space=pltpu.SMEM))
            else:
                specs.append(outside if any(arg is other for other in far) else inside)
        return pl.pallas_call(
            functools.partial(kernel, sizes),
            out_shape=outs,
            in_specs=specs,
            out_specs=tuple(outside if index in away else inside for index in range(len(outs))),
            scratch_shapes=list(scratch),
            compiler_params=pltpu.CompilerParams(vmem_limit_bytes=VMEM_MIB << 20),
        )(*args)

    ha = lax.axis_size("ha")
    near = [(i, i ^ 1) for i in range(ha)]
    far = [(i, i + 1) for i in range(1, ha - 1, 2)]
    far = far + [(target, source) for source, target in far]
    masks = [pltpu.VMEM((step, 128), F32), pltpu.VMEM((step, 128), F32)]

    given = tuple(
        pltpu.with_memory_space_constraint(value, pltpu.HBM)
        for value in (feat_hbm, up_hbm, reducer.T)
    )
    weight, real, near_rows, far_rows = call(
        prepare_kernel,
        (
            shape(128, 512, dtype=BF16),
            shape(16, 256),
            shape(2, 2, pairs, step, wide, dtype=BF16),
            shape(2, 2, pairs, step, wide, dtype=BF16),
        ),
        (*given, image_counts),
        [pltpu.VMEM((64, 256), BF16), pltpu.SemaphoreType.DMA((5,))],
        far=given,
    )
    near_rows = lax.ppermute(near_rows, "ha", near)
    far_rows = lax.ppermute(far_rows, "ha", far)
    feat = feat_hbm
    first, sums, rows = call(
        reduce_kernel,
        (shape(pairs, own, 128), shape(1, 256), shape(count * sizes.rows1, 128)),
        (feat, weight, real),
    )
    got1 = exchange(rows, count)
    windows, slope_one, second, norm_one, cross, rows = call(
        conv_kernel,
        (
            shape(pairs, own, 384, dtype=BF16),
            shape(pairs, own, 128),
            shape(pairs, sizes.ext, 128),
            shape(8, 128),
            shape(64, 256),
            shape(count * sizes.rows2, 128),
        ),
        (got1, feat, first, near_rows, far_rows, weight, taps, gain1, bias1, real),
        [pltpu.VMEM((2, 256, 256), BF16)] + [pltpu.VMEM((pairs, sizes.wide1, 128), F32)] * 2 + [*masks, pltpu.VMEM((pairs * own, 128), BF16)],
    )
    got2 = exchange(rows, count)
    hidden_two, slope_two, norm_two, gram, expand, rows = call(
        middle_kernel,
        (
            shape(pairs, sizes.ext, 128, dtype=BF16),
            shape(pairs, sizes.ext, 128),
            shape(8, 128),
            shape(64, 128),
            shape(128, 512, dtype=BF16),
            shape(count * sizes.rows3, 128),
        ),
        (got2, got1, second, gain2, bias2, expander, cross, real),
        [pltpu.VMEM((pairs * own, 128), BF16), pltpu.VMEM((pairs * own, 384), BF16)],
    )
    got3 = exchange(rows, count)
    active, grad_sum, back, norm_three, raw, rows = call(
        output_kernel,
        (
            shape(*flat, dtype=BF16),
            shape(*flat),
            shape(pairs, sizes.ext, 128),
            shape(8, 256),
            shape(64, 256),
            shape(count * sizes.rows4, 128),
        ),
        (
            got3, norm_one, norm_two, hidden_two, slope_two, second, feat, up_hbm, near_rows, far_rows,
            gain3, bias3, expand, real,
        ),
        [pltpu.VMEM((pairs * sizes.ext, 2 * wide), BF16), pltpu.VMEM((pairs * own, 2 * wide), F32)],
    )
    got4 = exchange(rows, count)
    gradgain3, gradbias3, gradgain2, gradbias2, grad_one, activated, rows = call(
        backward_kernel,
        (
            shape(1, 256),
            shape(1, 256),
            shape(1, 64),
            shape(1, 64),
            shape(pairs, own, 128),
            shape(*flat, dtype=BF16),
            shape(count * sizes.rows5, 128, dtype=BF16),
        ),
        (
            got4, got3, norm_one, norm_two, norm_three, gram, windows, slope_one, first, hidden_two,
            slope_two, second, back, raw, feat, sums, gain2, expand, taps, active, image_counts,
        ),
        [pltpu.VMEM((2, 256, 256), BF16)]
        + [pltpu.VMEM((sizes.wide2, 128), F32)] * 2
        + masks
        + [
            pltpu.VMEM((pairs * own, 384), BF16),
            pltpu.VMEM((count * sizes.rows5, 128), F32),
            pltpu.SemaphoreType.DMA,
        ],
        away=(5,),
    )
    got5 = exchange(rows, count)
    gradgain1, gradbias1, feature_grad, rows = call(
        shares_kernel,
        (
            shape(1, 64),
            shape(1, 64),
            pltpu.VMEM(deep, BF16),
            shape(count * sizes.rows6, 128, dtype=BF16),
        ),
        (got5, got1, got2, got3, norm_one, gain1, grad_one, first, grad_sum, weight, real),
        [pltpu.VMEM((count * sizes.rows6, 128), F32), pltpu.VMEM((count * sizes.rows5, 128), F32)],
    )
    got6 = exchange(rows, count)
    redt_grad, expander_grad, spatial_grad = call(
        weights_kernel,
        (shape(64, 256), shape(64, 256), shape(9 * 64, 64)),
        (got6,),
        [pltpu.VMEM((count * sizes.rows6, 128), F32)],
    )
    return (
        activated.reshape(features.shape),
        feature_grad.reshape(features.shape),
        redt_grad.T,
        spatial_grad.reshape(spatial.shape),
        expander_grad,
        gradgain1.reshape(64),
        gradbias1.reshape(64),
        gradgain2.reshape(64),
        gradbias2.reshape(64),
        gradgain3.reshape(256),
        gradbias3.reshape(256),
    )


def solution(mesh):
    whole = P("img", "ha", None, None)
    in_specs = (whole,) + (P(),) * 9 + (whole, P("img"))
    out_specs = (whole, whole) + (P(),) * 9
    return jax.shard_map(
        on_device, mesh=mesh, in_specs=in_specs, out_specs=out_specs, check_vma=False
    )
```
